32 devices in a mesh: seq: 8 (over y, x, core), head: 4 (over z).
Axes of the slice: x: 2, y: 2, z: 4, core: 2. Of those that a mesh axis runs over, the one named last changes fastest.
Arguments:
- queries: bfloat16 [1024, 4096], P('seq', 'head'), may hold values from -64 to 64
- keys: bfloat16 [1024, 4096], P('seq', 'head'), may hold values from -8 to 8
- values: bfloat16 [1024, 4096], P('seq', 'head'), may hold values from -8 to 8
- gate: float32 [32], P('head'), may hold values from -6 to 6
- out_weight: bfloat16 [4096, 4096], P('head'), may hold values from -0.09375 to 0.09375
- out_grad: bfloat16 [1024, 4096], P('seq', 'head'), may hold values from -6 to 6
- valid: int32 [8], P('seq'), may hold values from 32 to 128, as said below
- starts: int32 [8], P('seq'), may hold values from 0 to 1, as said below
Outputs:
- output: bfloat16 [1024, 4096], P('seq', 'head')
- query_grad: bfloat16 [1024, 4096], P('seq', 'head')
- key_grad: bfloat16 [1024, 4096], P('seq', 'head')
- value_grad: bfloat16 [1024, 4096], P('seq', 'head')
The draws below stay inside these ranges and needn't reach their ends.
Inputs may be any that keep to these rules, and one draw needn't show every extreme that they name: `valid`: A segment with fewer than 128 live tokens is followed by a segment that starts a document, or is the last one. The first segment starts a document and the second does not.
All inputs are finite; a program needn't handle non-finite values.
Results may differ from the reference program's by a relative error of at most 0.029.
Values may be sent and summed in bfloat16 or wider, within the bound.
No kernel may reach another device: no remote copies, remote signals or barrier semaphores. Data moves between devices by JAX's collectives and lax.ppermute only.
A program may use at most 64 MiB of HBM per device.

```python
import jax
import jax.numpy as jnp
from jax import lax

H = 32
DH = 128
D = 4096
TOK_DEV = 128
NSEG = 8
TOKENS = 1024


def streams(key):
    base_key = jax.random.fold_in(key, 101)
    keys_list = jax.random.split(base_key, 5)
    segs = TOKENS // TOK_DEV
    width = H * DH

    def noise(sub_key, shape):
        return jax.random.truncated_normal(sub_key, -4.0, 4.0, shape, jnp.float32)
    key_offset = jnp.repeat(noise(keys_list[1], (segs, width)), TOK_DEV, axis=0)
    value_offset = jnp.repeat(noise(keys_list[3], (segs, width)), TOK_DEV, axis=0)
    key_drawn = 0.8 * noise(keys_list[0], (TOKENS, width)) + 0.6 * key_offset
    value_vals = 0.8 * noise(keys_list[2], (TOKENS, width)) + 0.8 * value_offset
    query_vals = noise(keys_list[4], (TOKENS, width))
    key_vals = key_drawn
    return (query_vals, key_vals, value_vals)


def draw_queries(key, part):
    return streams(key)[0].astype(jnp.bfloat16)


def draw_keys(key, part):
    return streams(key)[1].astype(jnp.bfloat16)


def draw_values(key, part):
    return streams(key)[2].astype(jnp.bfloat16)


def documents(key):
    split_keys = jax.random.split(jax.random.fold_in(key, 202), 3)
    index = jnp.arange(NSEG)
    coin = (jax.random.randint(split_keys[0], (NSEG,), 0, 6) == 0).astype(jnp.int32)
    forced = jax.random.randint(split_keys[2], (), 2, NSEG)
    coin = jnp.where(index == forced, 1, coin)
    starts = jnp.where(index == 0, 1, jnp.where(index == 1, 0, coin)).astype(jnp.int32)
    following = jnp.concatenate([starts[1:], jnp.ones((1,), jnp.int32)])
    short = jax.random.randint(split_keys[1], (NSEG,), TOK_DEV // 4, TOK_DEV)
    short = jnp.where(index == NSEG - 1, TOK_DEV // 4, short)
    valid = jnp.where(following == 1, short, TOK_DEV).astype(jnp.int32)
    return (valid, starts)


def draw_valid(key, part):
    return documents(key)[0]


def draw_starts(key, part):
    return documents(key)[1]


def block_scale(own_key, dims, pieces, least, top_value):
    def one(dim, blocks):
        steps = jax.random.uniform(jax.random.fold_in(jax.random.fold_in(own_key, 6), dim), (blocks,), jnp.float32, least / len(pieces), top_value / len(pieces))
        return jnp.repeat(jnp.exp(steps), dims[dim] // blocks).reshape((-1,) + (1,) * (len(dims) - dim - 1))

    factor_of = one(*pieces[0])
    for cut in pieces[1:]:
        factor_of = factor_of * one(*cut)
    return factor_of


def gaussian(rng, dims, scale, limit, cuts=(), held_as=jnp.bfloat16):
    gain = block_scale(rng, dims, cuts, -0.22, 0.18) if cuts else 1.0
    values = jax.random.normal(rng, dims, jnp.float32) * scale * gain
    return jnp.minimum(jnp.maximum(values, -limit), limit).astype(held_as)


def setup_inputs(seed: int = 0) -> dict:
    splits = jax.random.split(jax.random.key(seed), 9)
    queries = draw_queries(jax.random.fold_in(splits[8], 71), 0)
    keys = draw_keys(jax.random.fold_in(splits[8], 71), 0)
    values = draw_values(jax.random.fold_in(splits[8], 71), 0)
    gate = gaussian(splits[3], (H,), 2.0, 6.0, ((0, 4),), jnp.float32)
    out_weight = gaussian(splits[4], (H * DH, D), D ** -0.5, 0.09375, ((0, 4),))
    out_grad = gaussian(splits[5], (TOKENS, D), 1.0, 6.0, ((0, 8), (1, 4)))
    valid = draw_valid(jax.random.fold_in(splits[8], 71), 0)
    starts = draw_starts(jax.random.fold_in(splits[8], 71), 0)
    return {"queries": queries, "keys": keys, "values": values, "gate": gate, "out_weight": out_weight, "out_grad": out_grad, "valid": valid, "starts": starts}


precise = lax.Precision.HIGHEST

def feature_map(inputs):
    return jnp.where(inputs > 0, inputs + 1.0, jnp.exp(jnp.minimum(inputs, 0.0)))

def segment_state(key_vals, value_vals, live_mask):
    length = key_vals.shape[0]
    sig_keys = feature_map(key_vals.reshape(length, -1, DH)) * live_mask[:, None, None]
    val_heads = value_vals.reshape(length, -1, DH) * live_mask[:, None, None]
    memory = jnp.einsum('thd,the->hde', sig_keys, val_heads, precision=precise)
    return (memory, lax.optimization_barrier(jnp.sum(sig_keys, axis=0)))

def segment_read(query_vals, key_vals, value_vals, live_mask, memory, norm_sum, gate_weight):
    length = query_vals.shape[0]
    query_heads = query_vals.reshape(length, -1, DH)
    query_low = query_heads.astype(jnp.bfloat16)
    key_low = key_vals.reshape(length, -1, DH).astype(jnp.bfloat16)
    value_low = value_vals.reshape(length, -1, DH).astype(jnp.bfloat16)
    sig_query = feature_map(query_heads)
    numer = jnp.einsum('thd,hde->the', sig_query, memory, precision=precise)
    denom = jnp.einsum('thd,hd->th', sig_query, norm_sum, precision=precise) + 1.0
    memory_read = numer / denom[:, :, None]
    scores = jnp.einsum('thd,shd->hts', query_low, key_low, preferred_element_type=jnp.float32) * DH ** (-0.5)
    where_pos = jnp.arange(length)
    allowed = (where_pos[None, :] <= where_pos[:, None]) & (live_mask[None, :] > 0)
    scores = jnp.where(allowed[None], scores, -1e+30)
    row_top = lax.stop_gradient(lax.optimization_barrier(jnp.max(scores, axis=-1, keepdims=True)))
    expo = jnp.exp(scores - row_top)
    probs = expo / lax.optimization_barrier(jnp.sum(expo, axis=-1, keepdims=True))
    probs_low = probs.astype(jnp.bfloat16)
    local_read = jnp.einsum('hts,she->the', probs_low, value_low, preferred_element_type=jnp.float32)
    mixed = gate_weight[None, :, None] * memory_read + (1.0 - gate_weight)[None, :, None] * local_read
    return (mixed * live_mask[:, None, None]).reshape(length, -1)

def reference(queries, keys, values, gate, out_weight, out_grad, valid, starts):
    segs = valid.shape[0]
    length = queries.shape[0] // segs

    def split_rows(array):
        return array.reshape(segs, length, array.shape[1])
    query_all = split_rows(queries.astype(jnp.float32))
    key_all = split_rows(keys.astype(jnp.float32))
    value_all = split_rows(values.astype(jnp.float32))
    live = (jnp.arange(length)[None, :] < valid[:, None]).astype(jnp.float32)
    opened = (1 - starts).astype(jnp.float32)
    gate_weight = jax.nn.sigmoid(gate)

    def state_one(item):
        return segment_state(item[0], item[1], item[2])
    memory_local, norm_local = lax.map(state_one, (key_all, value_all, live))
    zero_state = (jnp.zeros(memory_local.shape[1:], jnp.float32), jnp.zeros(norm_local.shape[1:], jnp.float32))

    def forward_step(carry, item):
        memory_used = item[2] * carry[0]
        norm_used = item[2] * carry[1]
        return ((memory_used + item[0], norm_used + item[1]), (memory_used, norm_used))
    _, (memory_in, norm_in) = lax.scan(forward_step, zero_state, (memory_local, norm_local, opened))

    def read_one(item):
        return segment_read(item[0], item[1], item[2], item[3], item[4], item[5], gate_weight).astype(jnp.bfloat16)
    mixed = lax.map(read_one, (query_all, key_all, value_all, live, memory_in, norm_in)).reshape(-1, out_weight.shape[0])
    output = jnp.dot(mixed, out_weight, preferred_element_type=jnp.float32).astype(jnp.bfloat16)
    mixed_grad = jnp.dot(out_grad, out_weight.T, preferred_element_type=jnp.float32).astype(jnp.bfloat16)
    mixed_grad = lax.optimization_barrier(mixed_grad).astype(jnp.float32)
    mixed_grad = split_rows(mixed_grad)

    def backward_one(item):
        live_mask = item[3]

        def read_local(query_arg, key_arg, value_arg, memory_arg, norm_arg):
            return segment_read(query_arg, key_arg, value_arg, live_mask, memory_arg, norm_arg, gate_weight)
        _, pullback = jax.vjp(read_local, item[0], item[1], item[2], item[4], item[5])
        return pullback(item[6])
    query_part, key_part, value_part, memory_grad, norm_grad = lax.map(backward_one, (query_all, key_all, value_all, live, memory_in, norm_in, mixed_grad))

    def reverse_step(carry, item):
        passed = (item[2] * (item[0] + carry[0]), item[2] * (item[1] + carry[1]))
        return (passed, carry)
    _, (memory_back, norm_back) = lax.scan(reverse_step, zero_state, (memory_grad, norm_grad, opened), reverse=True)

    def state_back(item):
        live_mask = item[2]

        def state_local(key_arg, value_arg):
            return segment_state(key_arg, value_arg, live_mask)
        _, pullback = jax.vjp(state_local, item[0], item[1])
        return pullback((item[3], item[4]))
    key_more, value_more = lax.map(state_back, (key_all, value_all, live, memory_back, norm_back))
    width = queries.shape[1]
    query_grad = query_part.reshape(-1, width).astype(jnp.bfloat16)
    key_grad = (key_part + key_more).reshape(-1, width).astype(jnp.bfloat16)
    value_grad = (value_part + value_more).reshape(-1, width).astype(jnp.bfloat16)
    return (output, query_grad, key_grad, value_grad)
```

```python
import functools

import jax
import jax.numpy as jnp
from jax import lax
from jax.experimental import pallas as pl
from jax.experimental.pallas import tpu as pltpu
from jax.sharding import PartitionSpec as P

DH = 128
ROWS = 136
SENT = 144
BF16 = jnp.bfloat16
F32 = jnp.float32
VMEM = pl.BlockSpec(memory_space=pltpu.VMEM)
SMEM = pl.BlockSpec(memory_space=pltpu.SMEM)


def call(kernel, outs, in_specs, args, flops=0, name=None):
    moved = sum(a.size * a.dtype.itemsize for a in args)
    moved += sum(o.size * o.dtype.itemsize for o in outs)
    return pl.pallas_call(
        kernel,
        out_shape=outs,
        in_specs=in_specs,
        out_specs=[VMEM] * len(outs),
        compiler_params=pltpu.CompilerParams(vmem_limit_bytes=48 * 1024 * 1024),
        cost_estimate=pl.CostEstimate(flops=flops, bytes_accessed=moved, transcendentals=0),
        name=name,
    )(*args)


def feature(x):
    return jnp.where(x > 0, x + 1.0, jnp.exp(jnp.minimum(x, 0.0)))


def slope(x):
    return jnp.where(x > 0, 1.0, jnp.where(x == 0, 0.5, jnp.exp(jnp.minimum(x, 0.0))))


def sigmoid(x):
    return 1.0 / (1.0 + jnp.exp(-x))


def dot(a, b, dims):
    return lax.dot_general(a, b, (dims, ((), ())), preferred_element_type=F32)


NN = ((1,), (0,))
NT = ((1,), (1,))
TN = ((0,), (0,))


def live_rows(valid_ref, length):
    where = lax.broadcasted_iota(jnp.int32, (length, 1), 0)
    return (where < valid_ref[0]).astype(F32)


def head(ref, h):
    return ref[:, h * DH : (h + 1) * DH]


def tail(rows, *values):
    where = lax.broadcasted_iota(jnp.int32, (rows, DH), 0)
    out = jnp.zeros((rows, DH), F32)
    for at, value in enumerate(values):
        out = jnp.where(where == at, value, out)
    return out


def split(x):
    top = x.astype(BF16)
    rest = x - top.astype(F32)
    return top, rest.astype(BF16)


def state_kernel(heads, valid_ref, starts_ref, k_ref, v_ref, state_ref):
    live = live_rows(valid_ref, k_ref.shape[0])
    opened = 1.0 - starts_ref[0].astype(F32)
    for h in range(heads):
        sig = (feature(head(k_ref, h).astype(F32)) * live).astype(BF16)
        state_ref[h, 0:DH, :] = dot(sig, head(v_ref, h), TN)
        norm = jnp.sum(sig.astype(F32), axis=0, keepdims=True)
        state_ref[h, DH:ROWS, :] = tail(ROWS - DH, norm, opened)


def pair_kernel(heads, forward, pos_ref, mine_ref, other_ref, sent_ref):
    half = lax.rem(pos_ref[0], 2)
    lower = half == 0
    for i in range(heads // 2):
        h = half * (heads // 2) + i
        mine, other = mine_ref[h], other_ref[h]
        first = jnp.where(lower, mine, other)
        second = jnp.where(lower, other, mine)
        open_first, open_second = first[DH + 1 : DH + 2], second[DH + 1 : DH + 2]
        if forward:
            total = open_second * first + second
        else:
            total = open_first * (first + open_second * second)
        memory, norm = total[0:DH], total[DH : DH + 1]
        norm_1, rest = split(norm)
        norm_1 = norm_1.astype(F32)
        norm_2 = rest.astype(F32)
        norm_3 = norm - norm_1 - norm_2
        if forward:
            weight = jnp.maximum(jnp.sum(norm, axis=1, keepdims=True), 1e-30)
            centre = jnp.sum(memory, axis=0, keepdims=True) / weight
            centre = centre.astype(BF16).astype(F32)
            norms = tail(16, norm_1, norm_2, norm_3).astype(BF16)
            centres = tail(16, centre, centre, centre).astype(BF16)
            memory = memory - dot(norms, centres, TN)
        else:
            centre = jnp.zeros_like(norm)
        sent_ref[i, 0:DH, :] = memory.astype(BF16)
        rows = tail(SENT - DH, norm_1, norm_2, norm_3, centre, open_first * open_second)
        sent_ref[i, DH:SENT, :] = rows.astype(BF16)


def join_kernel(heads, forward, pos_ref, x_ref, y_ref, d_ref, carry_ref):
    chip = pos_ref[0] // 2
    place = chip if forward else 3 - chip
    for i in range(heads // 2):
        totals = []
        for ref in (x_ref, y_ref, d_ref):
            memory = ref[i, 0:DH, :].astype(F32)
            rows = ref[i, DH:SENT, :].astype(F32)
            norm = rows[0:1] + rows[1:2] + rows[2:3]
            if forward:
                norms = tail(16, rows[0:1], rows[1:2], rows[2:3]).astype(BF16)
                centres = tail(16, rows[3:4], rows[3:4], rows[3:4]).astype(BF16)
                memory = memory + dot(norms, centres, TN)
            totals.append((memory, norm, rows[4:5]))
        (x_mem, x_norm, x_open), (y_mem, y_norm, y_open), (d_mem, d_norm, d_open) = totals
        on_y = jnp.where(place == 2, d_open, x_open)
        on_d = jnp.where(place == 2, 1.0, x_open * y_open)
        carry_ref[i, 0:DH, :] = x_mem + on_y * y_mem + on_d * d_mem
        carry_ref[i, DH:ROWS, :] = tail(ROWS - DH, x_norm + on_y * y_norm + on_d * d_norm)


def local_kernel(heads, valid_ref, q_ref, k_ref, v_ref, probs_ref, local_ref):
    length = q_ref.shape[0]
    row = lax.broadcasted_iota(jnp.int32, (length, length), 0)
    col = lax.broadcasted_iota(jnp.int32, (length, length), 1)
    allowed = (col <= row) & (col < valid_ref[0])
    for h in range(heads):
        scores = dot(head(q_ref, h), head(k_ref, h), NT) * DH ** (-0.5)
        scores = jnp.where(allowed, scores, -1e30)
        expo = jnp.exp(scores - jnp.max(scores, axis=1, keepdims=True))
        probs = (expo / jnp.sum(expo, axis=1, keepdims=True)).astype(BF16)
        probs_ref[h] = probs
        local_ref[:, h * DH : (h + 1) * DH] = dot(probs, head(v_ref, h), NN)


def read_kernel(
    heads, pos_ref, valid_ref, gate_ref, q_ref, mine_ref, other_ref, own_ref, far_ref, local_ref,
    mixed_ref, read_ref, memory_ref, norm_ref,
):
    length = q_ref.shape[0]
    live = live_rows(valid_ref, length)
    upper = lax.rem(pos_ref[0], 2) == 1
    for h in range(heads):
        i, part = h % (heads // 2), h // (heads // 2)
        own_here = upper if part else jnp.logical_not(upper)
        carry = jnp.where(own_here, own_ref[i], far_ref[i])
        other = other_ref[h]
        before = jnp.where(upper, other[DH + 1 : DH + 2] * carry + other, carry)
        state = mine_ref[h, DH + 1 : DH + 2, :] * before
        memory, norm = state[0:DH], state[DH : DH + 1]
        parts = jnp.concatenate(split(memory), axis=1)
        memory_ref[h] = parts
        norm_ref[h] = jnp.broadcast_to(norm, (8, DH))
        sig = feature(head(q_ref, h).astype(F32)).astype(BF16)
        numer = dot(sig, parts, NN)
        numer = numer[:, 0:DH] + numer[:, DH:]
        denom = jnp.sum(sig.astype(F32) * norm, axis=1, keepdims=True) + 1.0
        read = numer / denom
        gate = sigmoid(jnp.full((1, DH), gate_ref[h], F32))
        mixed = live * (gate * read + (1.0 - gate) * head(local_ref, h))
        read_ref[:, h * DH : (h + 1) * DH] = read
        mixed_ref[:, h * DH : (h + 1) * DH] = mixed.astype(BF16)


def spread_kernel(heads, valid_ref, starts_ref, gate_ref, q_ref, norm_ref, read_ref, grad_ref,
                  passed_ref, numer_ref, denom_ref):
    length = q_ref.shape[0]
    live = live_rows(valid_ref, length)
    opened = 1.0 - starts_ref[0].astype(F32)
    for h in range(heads):
        sig = feature(head(q_ref, h).astype(F32)).astype(BF16)
        sig_full = sig.astype(F32)
        denom = jnp.sum(sig_full * norm_ref[h, 0:1, :], axis=1, keepdims=True) + 1.0
        gate = sigmoid(jnp.full((1, DH), gate_ref[h], F32))
        numer_grad = (head(grad_ref, h).astype(F32) * gate * (live / denom)).astype(BF16)
        denom_grad = -jnp.sum(
            numer_grad.astype(F32) * head(read_ref, h), axis=1, keepdims=True
        )
        passed_ref[h, 0:DH, :] = dot(sig, numer_grad, TN)
        norm_grad = jnp.sum(sig_full * denom_grad, axis=0, keepdims=True)
        passed_ref[h, DH:ROWS, :] = tail(ROWS - DH, norm_grad, opened)
        numer_ref[:, h * DH : (h + 1) * DH] = numer_grad
        denom_ref[h] = denom_grad


def grads_kernel(heads, valid_ref, gate_ref, q_ref, k_ref, v_ref, probs_ref, grad_ref, numer_ref,
                 denom_ref, memory_ref, norm_ref, query_ref, key_ref, value_ref):
    length = q_ref.shape[0]
    live = live_rows(valid_ref, length)
    for h in range(heads):
        cut = slice(h * DH, (h + 1) * DH)
        q, k, v = head(q_ref, h), head(k_ref, h), head(v_ref, h)
        gate = sigmoid(jnp.full((1, DH), gate_ref[h], F32))
        grad = (head(grad_ref, h).astype(F32) * (1.0 - gate) * live).astype(BF16)
        probs = probs_ref[h]
        probs_grad = dot(grad, v, NT)
        full = probs.astype(F32)
        mean = jnp.sum(full * probs_grad, axis=1, keepdims=True)
        scores_grad = (full * (probs_grad - mean) * DH ** (-0.5)).astype(BF16)
        key_ref[:, cut] = dot(scores_grad, q, TN)
        value_ref[:, cut] = dot(probs, grad, TN)
        parts = memory_ref[h]
        numer = head(numer_ref, h)
        sig_grad = dot(numer, parts[:, 0:DH], NT) + dot(numer, parts[:, DH:], NT)
        sig_grad = sig_grad + denom_ref[h] * norm_ref[h, 0:1, :]
        total = dot(scores_grad, k, NN) + sig_grad * slope(q.astype(F32))
        query_ref[:, cut] = total.astype(BF16)


def last_kernel(heads, pos_ref, valid_ref, k_ref, v_ref, other_ref, own_ref, far_ref, key_ref,
                value_ref, key_out, value_out):
    length = k_ref.shape[0]
    live = live_rows(valid_ref, length)
    upper = lax.rem(pos_ref[0], 2) == 1
    for h in range(heads):
        cut = slice(h * DH, (h + 1) * DH)
        i, part = h % (heads // 2), h // (heads // 2)
        own_here = upper if part else jnp.logical_not(upper)
        carry = jnp.where(own_here, own_ref[i], far_ref[i])
        other = other_ref[h]
        back = jnp.where(upper, carry, other[DH + 1 : DH + 2] * (other + carry))
        memory, norm = back[0:DH], back[DH : DH + 1]
        top, low = split(memory)
        k, v = head(k_ref, h).astype(F32), head(v_ref, h)
        sig = (feature(k) * live).astype(BF16)
        sig_grad = (dot(v, top, NT) + dot(v, low, NT) + norm) * live
        key_out[:, cut] = (key_ref[:, cut] + sig_grad * slope(k)).astype(BF16)
        more = dot(sig, jnp.concatenate([top, low], axis=1), NN)
        value_out[:, cut] = (value_ref[:, cut] + more[:, 0:DH] + more[:, DH:]).astype(BF16)


def project_kernel(ids_ref, mixed_ref, weight_ref, out_ref):
    out_ref[0] = dot(mixed_ref[...], weight_ref[...], NN).astype(BF16)


def project(ids, mixed, weight, cols, name):
    count, (length, width) = ids.shape[0], mixed.shape
    return pl.pallas_call(
        project_kernel,
        grid_spec=pltpu.PrefetchScalarGridSpec(
            num_scalar_prefetch=1,
            grid=(count,),
            in_specs=[
                pl.BlockSpec((length, width), lambda s, ids: (0, 0)),
                pl.BlockSpec((width, cols), lambda s, ids: (0, ids[s])),
            ],
            out_specs=pl.BlockSpec((1, length, cols), lambda s, ids: (s, 0, 0)),
        ),
        out_shape=jax.ShapeDtypeStruct((count, length, cols), BF16),
        compiler_params=pltpu.CompilerParams(vmem_limit_bytes=48 * 1024 * 1024),
        cost_estimate=pl.CostEstimate(
            flops=2 * length * width * cols * count,
            bytes_accessed=2 * count * width * cols,
            transcendentals=0,
        ),
        name=name,
    )(ids, mixed, weight)


def unproject_kernel(blocks, grad_first, ids_ref, *refs):
    parts, (weight_ref, total_ref) = refs[:-2], refs[-2:]
    step = pl.program_id(0)
    for s, members in enumerate(blocks):

        @pl.when(step == s)
        def _():
            block = parts[members[0]][...]
            for more in members[1:]:
                block = block + parts[more][...]
            term = dot(block, weight_ref[...], NT)
            if s == 0 and grad_first:
                total_ref[...] = term
            elif s == 0:
                total_ref[...] = parts[-1][...] + term
            else:
                total_ref[...] += term


def unproject(ids, groups, weight, before, name):
    flat, blocks = [], []
    for group in groups:
        blocks.append(tuple(range(len(flat), len(flat) + len(group))))
        flat += group
    length, cols = flat[0].shape
    width = weight.shape[0]
    extra = [] if before is None else [before]
    return pl.pallas_call(
        functools.partial(unproject_kernel, blocks, before is None),
        grid_spec=pltpu.PrefetchScalarGridSpec(
            num_scalar_prefetch=1,
            grid=(len(groups),),
            in_specs=[pl.BlockSpec((length, cols), lambda s, ids: (0, 0)) for _ in flat]
            + [pl.BlockSpec((length, width), lambda s, ids: (0, 0)) for _ in extra]
            + [pl.BlockSpec((width, cols), lambda s, ids: (0, ids[s]))],
            out_specs=pl.BlockSpec((length, width), lambda s, ids: (0, 0)),
        ),
        out_shape=jax.ShapeDtypeStruct((length, width), F32),
        compiler_params=pltpu.CompilerParams(vmem_limit_bytes=48 * 1024 * 1024),
        cost_estimate=pl.CostEstimate(
            flops=2 * length * width * cols * len(groups),
            bytes_accessed=2 * len(groups) * width * cols,
            transcendentals=0,
        ),
        name=name,
    )(ids, *flat, *extra, weight)


def weighted(state, forward):
    count, mine = lax.axis_size("seq"), lax.axis_index("seq")
    states = lax.all_gather(state, "seq")
    total = jnp.zeros_like(state)
    weight = jnp.ones((), F32)

    def turn(step, carried):
        total, weight = carried
        at = mine - 1 - step if forward else mine + 1 + step
        inside = (at >= 0) & (at < count)
        one = lax.dynamic_index_in_dim(states, jnp.clip(at, 0, count - 1), keepdims=False)
        opened = one[0, DH + 1, 0]
        here = weight if forward else weight * opened
        total = jnp.where(inside, total + here * one, total)
        return total, weight * opened

    return lax.fori_loop(0, count - 1, turn, (total, weight))[0]


def scan_states(state, pos, heads, forward):
    count = lax.axis_size("seq")
    if count != 8:
        carry = weighted(state, forward)
        place = jnp.full_like(pos, 0 if forward else 1)
        own, far = carry[: heads // 2], carry[heads // 2 :]
        return (own, far, state, place) if forward else (far, own, state, place)
    pairs = [(s, s ^ 1) for s in range(count)]
    other = lax.ppermute(state, "seq", pairs)
    flops = heads * DH * DH * 40
    sent = call(
        functools.partial(pair_kernel, heads, forward),
        [jax.ShapeDtypeStruct((heads // 2, SENT, DH), BF16)],
        [SMEM, VMEM, VMEM],
        [pos, state, other],
        flops,
        name="pair",
    )[0]
    x = [(0, 2), (1, 3), (4, 6), (5, 7)]
    y = [(0, 4), (1, 5), (2, 6), (3, 7)]
    d = [(0, 6), (1, 7), (2, 4), (3, 5)]
    if not forward:
        x, y, d = ([(b, a) for a, b in ways] for ways in (x, y, d))
    arrived = [lax.ppermute(sent, "seq", ways) for ways in (d, x, y)]
    own = call(
        functools.partial(join_kernel, heads, forward),
        [jax.ShapeDtypeStruct((heads // 2, ROWS, DH), F32)],
        [SMEM, VMEM, VMEM, VMEM],
        [pos, arrived[1], arrived[2], arrived[0]],
        flops,
        name="join",
    )[0]
    far = lax.ppermute(own, "seq", pairs)
    return own, far, other, pos


def shards(queries, keys, values, gate, out_weight, out_grad, valid, starts):
    length, width = queries.shape
    heads = width // DH
    cols = out_grad.shape[1]
    groups = lax.axis_size("head")
    pos = lax.axis_index("seq").astype(jnp.int32).reshape(1)
    z = lax.axis_index("head").astype(jnp.int32)
    flat = jax.ShapeDtypeStruct((length, width), F32)
    low = jax.ShapeDtypeStruct((length, width), BF16)
    states = jax.ShapeDtypeStruct((heads, ROWS, DH), F32)
    square = 2 * heads * length * DH * DH

    state = call(
        functools.partial(state_kernel, heads), [states], [SMEM, SMEM, VMEM, VMEM],
        [valid, starts, keys, values], square, name="state",
    )[0]

    if groups == 4:
        swap = [(0, 1), (1, 0), (2, 3), (3, 2)]
        ends = [(0, 3), (3, 0)]
        skip_in, skip_out = [(0, 2), (3, 1)], [(1, 3), (2, 0)]
        middle = [(1, 2), (2, 1)]
        outward, inward = [(1, 0), (2, 3)], [(0, 1), (3, 2)]
        near = z + 1 - 2 * (z % 2)
        far_id = jnp.where(z < 2, 3, 0)
        mid_id = jnp.where(z < 2, 2, 1)
        from_mid = lax.ppermute(out_grad, "head", middle)
        from_near = lax.ppermute(out_grad, "head", swap)
        from_end = lax.ppermute(out_grad, "head", ends)
        from_skip = lax.ppermute(out_grad, "head", skip_in)
        from_out = lax.ppermute(from_mid, "head", outward)

    probs, local = call(
        functools.partial(local_kernel, heads),
        [jax.ShapeDtypeStruct((heads, length, length), BF16), flat],
        [SMEM, VMEM, VMEM, VMEM],
        [valid, queries, keys, values], 2 * square, name="local",
    )

    own, far, other, place = scan_states(state, pos, heads, True)
    mixed, read, memory, norm = call(
        functools.partial(read_kernel, heads),
        [low, flat, jax.ShapeDtypeStruct((heads, DH, 2 * DH), BF16),
         jax.ShapeDtypeStruct((heads, 8, DH), F32)],
        [SMEM, SMEM, SMEM] + [VMEM] * 6,
        [place, valid, gate, queries, state, other, own, far, local], 2 * square, name="read",
    )

    if groups == 4:
        first = project(jnp.stack([mid_id, far_id]), mixed, out_weight, cols, "project_far")
        to_in = lax.ppermute(first[0], "head", inward)
        end = lax.ppermute(first[1], "head", ends)
        skip = lax.ppermute(first[1], "head", skip_out)
        second = project(jnp.stack([near, z]), mixed, out_weight, cols, "project_near")
        next_to = lax.ppermute(second[0], "head", swap)
        mid = lax.ppermute(first[0] + to_in, "head", middle)
        output = second[1].astype(F32) + next_to.astype(F32) + end.astype(F32)
        output = (output + skip.astype(F32) + mid.astype(F32)).astype(BF16)
        total = unproject(
            jnp.stack([z, near, far_id]), [[out_grad], [from_near], [from_end, from_skip]],
            out_weight, None, "unproject_first",
        )
        total = unproject(
            mid_id.reshape(1), [[from_mid, from_out]], out_weight, total, "unproject_last"
        )
    else:
        part = dot(mixed, out_weight, NN)
        output = lax.psum_scatter(part, "head", scatter_dimension=1, tiled=True).astype(BF16)
        whole = lax.all_gather(out_grad, "head", axis=1, tiled=True)
        total = dot(whole, out_weight, NT)
    mixed_grad = total.astype(BF16)

    passed, numer_grad, denom_grad = call(
        functools.partial(spread_kernel, heads),
        [states, low, jax.ShapeDtypeStruct((heads, length, 1), F32)],
        [SMEM] * 3 + [VMEM] * 4,
        [valid, starts, gate, queries, norm, read, mixed_grad], square, name="spread",
    )
    query_grad, key_part, value_part = call(
        functools.partial(grads_kernel, heads),
        [low, flat, flat],
        [SMEM] * 2 + [VMEM] * 9,
        [valid, gate, queries, keys, values, probs, mixed_grad, numer_grad, denom_grad, memory, norm],
        6 * square, name="grads",
    )
    own, far, other, place = scan_states(passed, pos, heads, False)
    key_grad, value_grad = call(
        functools.partial(last_kernel, heads),
        [low, low],
        [SMEM] * 2 + [VMEM] * 7,
        [place, valid, keys, values, other, own, far, key_part, value_part], 4 * square, name="last",
    )
    return (output, query_grad, key_grad, value_grad)


def solution(mesh):
    placed = (
        P("seq", "head"),
        P("seq", "head"),
        P("seq", "head"),
        P("head"),
        P("head", None),
        P("seq", "head"),
        P("seq"),
        P("seq"),
    )
    return jax.shard_map(
        shards,
        mesh=mesh,
        in_specs=placed,
        out_specs=(P("seq", "head"), P("seq", "head"), P("seq", "head"), P("seq", "head")),
        check_vma=False,
    )
```

```python
import functools

import jax
import jax.numpy as jnp
from jax import lax
from jax.experimental import pallas as pl
from jax.experimental.pallas import tpu as pltpu
from jax.sharding import PartitionSpec as P

DH = 128
ROWS = 136
SENT = 144
BF16 = jnp.bfloat16
F32 = jnp.float32
VMEM = pl.BlockSpec(memory_space=pltpu.VMEM)
SMEM = pl.BlockSpec(memory_space=pltpu.SMEM)


ANY = pl.BlockSpec(memory_space=pl.ANY)
DMA = pltpu.SemaphoreType.DMA


def call(kernel, outs, in_specs, args, flops=0, scratch=(), name=None):
    moved = sum(a.size * a.dtype.itemsize for a in args)
    moved += sum(o.size * o.dtype.itemsize for o in outs)
    return pl.pallas_call(
        kernel,
        out_shape=outs,
        in_specs=in_specs,
        out_specs=[VMEM] * len(outs),
        scratch_shapes=scratch,
        compiler_params=pltpu.CompilerParams(vmem_limit_bytes=24 * 1024 * 1024),
        cost_estimate=pl.CostEstimate(
            flops=flops, bytes_accessed=min(moved, 1 << 20), transcendentals=0
        ),
        name=name,
    )(*args)


def feature(x):
    return jnp.where(x > 0, x + 1.0, jnp.exp(jnp.minimum(x, 0.0)))


def slope(x):
    return jnp.where(x > 0, 1.0, jnp.where(x == 0, 0.5, jnp.exp(jnp.minimum(x, 0.0))))


def sigmoid(x):
    return 1.0 / (1.0 + jnp.exp(-x))


def dot(a, b, dims):
    return lax.dot_general(a, b, (dims, ((), ())), preferred_element_type=F32)


NN = ((1,), (0,))
NT = ((1,), (1,))
TN = ((0,), (0,))


def live_rows(info_ref, heads, length):
    where = lax.broadcasted_iota(jnp.int32, (length, 1), 0).astype(F32)
    return (where < info_ref[heads + 1 : heads + 2, 0:1]).astype(F32)


def head(ref, h):
    return ref[:, h * DH : (h + 1) * DH]


def tail(rows, *values):
    where = lax.broadcasted_iota(jnp.int32, (rows, DH), 0)
    out = jnp.zeros((rows, DH), F32)
    for at, value in enumerate(values):
        out = jnp.where(where == at, value, out)
    return out


def split(x):
    top = x.astype(BF16)
    rest = x - top.astype(F32)
    return top, rest.astype(BF16)


def load_kernel(
    heads, q_in, k_in, v_in, grad_in, valid_in, starts_in, gate_in,
    q_ref, k_ref, v_ref, grad_ref, info_ref, state_ref, valid_ref, starts_ref, gate_ref, sems,
):
    pairs = [(valid_in, valid_ref), (starts_in, starts_ref), (gate_in, gate_ref), (k_in, k_ref),
             (v_in, v_ref), (q_in, q_ref), (grad_in, grad_ref)]
    copies = [pltpu.make_async_copy(a, b, sems.at[i]) for i, (a, b) in enumerate(pairs)]
    for copy in copies:
        copy.start()
    for copy in copies[:3]:
        copy.wait()
    opened = 1.0 - starts_ref[0].astype(F32)
    valid = valid_ref[0].astype(F32)
    rows = [sigmoid(jnp.full((1, DH), gate_ref[h], F32)) for h in range(heads)]
    info_ref[...] = tail(heads + 8, *rows, opened, valid)
    live = live_rows(info_ref, heads, k_ref.shape[0])
    for copy in copies[3:5]:
        copy.wait()
    for h in range(heads):
        sig = (feature(head(k_ref, h).astype(F32)) * live).astype(BF16)
        state_ref[h, 0:DH, :] = dot(sig, head(v_ref, h), TN)
        norm = jnp.sum(sig.astype(F32), axis=0, keepdims=True)
        state_ref[h, DH:ROWS, :] = tail(ROWS - DH, norm, opened)
    for copy in copies[5:]:
        copy.wait()


def pair_kernel(heads, forward, pos_ref, mine_ref, other_ref, *refs):
    sent_ref = refs[-1]
    half = lax.rem(pos_ref[0], 2)
    lower = half == 0
    for i in range(heads // 2):
        h = half * (heads // 2) + i
        mine, other = mine_ref[h], other_ref[h]
        first = jnp.where(lower, mine, other)
        second = jnp.where(lower, other, mine)
        open_first, open_second = first[DH + 1 : DH + 2], second[DH + 1 : DH + 2]
        if forward:
            total = open_second * first + second
        else:
            total = open_first * (first + open_second * second)
        memory, norm = total[0:DH], total[DH : DH + 1]
        norm_1, rest = split(norm)
        norm_1 = norm_1.astype(F32)
        norm_2 = rest.astype(F32)
        norm_3 = norm - norm_1 - norm_2
        if forward:
            weight = jnp.maximum(jnp.sum(norm, axis=1, keepdims=True), 1e-30)
            centre = jnp.sum(memory, axis=0, keepdims=True) / weight
            centre = centre.astype(BF16).astype(F32)
            norms = tail(16, norm_1, norm_2, norm_3).astype(BF16)
            centres = tail(16, centre, centre, centre).astype(BF16)
            memory = memory - dot(norms, centres, TN)
        else:
            centre = jnp.zeros_like(norm)
        sent_ref[i, 0:DH, :] = memory.astype(BF16)
        rows = tail(SENT - DH, norm_1, norm_2, norm_3, centre, open_first * open_second)
        sent_ref[i, DH:SENT, :] = rows.astype(BF16)


def join_kernel(heads, forward, pos_ref, x_ref, y_ref, d_ref, *refs):
    carry_ref = refs[-1]
    chip = pos_ref[0] // 2
    place = chip if forward else 3 - chip
    for i in range(heads // 2):
        totals = []
        for ref in (x_ref, y_ref, d_ref):
            memory = ref[i, 0:DH, :].astype(F32)
            rows = ref[i, DH:SENT, :].astype(F32)
            norm = rows[0:1] + rows[1:2] + rows[2:3]
            if forward:
                norms = tail(16, rows[0:1], rows[1:2], rows[2:3]).astype(BF16)
                centres = tail(16, rows[3:4], rows[3:4], rows[3:4]).astype(BF16)
                memory = memory + dot(norms, centres, TN)
            totals.append((memory, norm, rows[4:5]))
        (x_mem, x_norm, x_open), (y_mem, y_norm, y_open), (d_mem, d_norm, d_open) = totals
        odd, high = lax.rem(place, 2) == 1, place >= 2
        on_x = jnp.where(odd, jnp.ones_like(x_open), 0.0)
        on_y = jnp.where(high, jnp.where(odd, x_open, d_open), 0.0)
        on_d = jnp.where(high, jnp.where(odd, x_open * y_open, 1.0), 0.0)
        norm = on_x * x_norm + on_y * y_norm + on_d * d_norm
        carry_ref[i, 0:DH, :] = on_x * x_mem + on_y * y_mem + on_d * d_mem
        carry_ref[i, DH:ROWS, :] = tail(ROWS - DH, norm)


def local_kernel(heads, info_ref, q_ref, k_ref, v_ref, after_ref, probs_ref, local_ref):
    length = q_ref.shape[0]
    row = lax.broadcasted_iota(jnp.int32, (length, length), 0)
    col = lax.broadcasted_iota(jnp.int32, (length, length), 1)
    allowed = (col <= row) & (col.astype(F32) < info_ref[heads + 1 : heads + 2, 0:1])
    for h in range(heads):
        scores = dot(head(q_ref, h), head(k_ref, h), NT) * DH ** (-0.5)
        scores = jnp.where(allowed, scores, -1e30)
        expo = jnp.exp(scores - jnp.max(scores, axis=1, keepdims=True))
        probs = (expo / jnp.sum(expo, axis=1, keepdims=True)).astype(BF16)
        probs_ref[h] = probs
        local_ref[:, h * DH : (h + 1) * DH] = dot(probs, head(v_ref, h), NN)


def fetch(weight_ref, ids_ref, slots, sems, rows, row_at=0):
    cols = slots.shape[-1]
    copies = []
    for s in range(slots.shape[0]):
        first = pl.multiple_of(ids_ref[s] * cols, DH)
        source = weight_ref.at[pl.ds(row_at, rows), pl.ds(first, cols)]
        copies.append(pltpu.make_async_copy(source, slots.at[s, pl.ds(row_at, rows)], sems.at[s]))
    for copy in copies:
        copy.start()
    return copies


def read_kernel(
    heads, project, pos_ref, ids_ref, info_ref, q_ref, mine_ref, other_ref, own_ref, far_ref,
    local_ref, *refs,
):
    if project:
        weight_ref, mixed_ref, read_ref, memory_ref, norm_ref, first_ref, slots, sems = refs
        (copy,) = fetch(weight_ref, ids_ref, slots, sems, weight_ref.shape[0])
    else:
        mixed_ref, read_ref, memory_ref, norm_ref = refs
    live = live_rows(info_ref, heads, q_ref.shape[0])
    upper = lax.rem(pos_ref[0], 2) == 1
    for h in range(heads):
        i, part = h % (heads // 2), h // (heads // 2)
        own_here = upper if part else jnp.logical_not(upper)
        carry = jnp.where(own_here, own_ref[i], far_ref[i])
        other = other_ref[h]
        before = jnp.where(upper, other[DH + 1 : DH + 2] * carry + other, carry)
        state = mine_ref[h, DH + 1 : DH + 2, :] * before
        memory, norm = state[0:DH], state[DH : DH + 1]
        parts = jnp.concatenate(split(memory), axis=1)
        memory_ref[h] = parts
        norm_ref[h] = jnp.broadcast_to(norm, (8, DH))
        sig = feature(head(q_ref, h).astype(F32)).astype(BF16)
        numer = dot(sig, parts, NN)
        numer = numer[:, 0:DH] + numer[:, DH:]
        denom = jnp.sum(sig.astype(F32) * norm, axis=1, keepdims=True) + 1.0
        read = numer / denom
        gate = info_ref[h : h + 1, :]
        mixed = live * (gate * read + (1.0 - gate) * head(local_ref, h))
        read_ref[:, h * DH : (h + 1) * DH] = read
        mixed_ref[:, h * DH : (h + 1) * DH] = mixed.astype(BF16)
    if project:
        copy.wait()
        first_ref[...] = dot(mixed_ref[...], slots[0], NN).astype(BF16)


def own_kernel(ids_ref, grad_ref, weight_ref, after_ref, total_ref, slots, sems):
    (copy,) = fetch(weight_ref, ids_ref, slots, sems, weight_ref.shape[0])
    copy.wait()
    total_ref[...] = dot(grad_ref[...], slots[0], NT)


def add_kernel(ids_ref, mixed_ref, weight_ref, more_ref, after_ref, out_ref, slots, sems):
    (copy,) = fetch(weight_ref, ids_ref, slots, sems, weight_ref.shape[0])
    copy.wait()
    part = dot(mixed_ref[...], slots[0], NN)
    out_ref[...] = (part + more_ref[...].astype(F32)).astype(BF16)


def rest_kernel(ids_ref, mixed_ref, weight_ref, after_ref, near_ref, own_ref, slots, sems):
    copies = fetch(weight_ref, ids_ref, slots, sems, weight_ref.shape[0])
    copies[0].wait()
    near_ref[...] = dot(mixed_ref[...], slots[0], NN).astype(BF16)
    copies[1].wait()
    own_ref[...] = dot(mixed_ref[...], slots[1], NN)


def spread_kernel(heads, blocks, ids_ref, info_ref, q_ref, norm_ref, read_ref, *refs):
    if blocks:
        parts, (total_ref, weight_ref) = refs[:blocks], refs[blocks : blocks + 2]
        refs = refs[blocks + 2 :]
        passed_ref, numer_ref, denom_ref, grad_ref, slots, sems = refs
        rows = 2 * DH
        copies = [
            fetch(weight_ref, ids_ref, slots, sems.at[at], rows, at * rows)
            for at in range(heads // 2)
        ]
    else:
        grad_ref, passed_ref, numer_ref, denom_ref = refs
    live = live_rows(info_ref, heads, q_ref.shape[0])
    opened = info_ref[heads : heads + 1, :]
    for h in range(heads):
        cut = slice(h * DH, (h + 1) * DH)
        if blocks and h % 2 == 0:
            wide = slice(h * DH, (h + 2) * DH)
            total = total_ref[:, wide]
            for s in range(blocks):
                copies[h // 2][s].wait()
                total = total + dot(parts[s][...], slots[s, h * DH : (h + 2) * DH, :], NT)
            grad_ref[:, wide] = total.astype(BF16)
        sig = feature(head(q_ref, h).astype(F32)).astype(BF16)
        sig_full = sig.astype(F32)
        denom = jnp.sum(sig_full * norm_ref[h, 0:1, :], axis=1, keepdims=True) + 1.0
        gate = info_ref[h : h + 1, :]
        numer_grad = (head(grad_ref, h).astype(F32) * gate * (live / denom)).astype(BF16)
        denom_grad = -jnp.sum(
            numer_grad.astype(F32) * head(read_ref, h), axis=1, keepdims=True
        )
        passed_ref[h, 0:DH, :] = dot(sig, numer_grad, TN)
        norm_grad = jnp.sum(sig_full * denom_grad, axis=0, keepdims=True)
        passed_ref[h, DH:ROWS, :] = tail(ROWS - DH, norm_grad, opened)
        numer_ref[:, cut] = numer_grad
        denom_ref[h] = denom_grad


def grads_kernel(heads, info_ref, q_ref, k_ref, v_ref, probs_ref, grad_ref, numer_ref,
                 denom_ref, memory_ref, norm_ref, after_ref, query_ref, key_ref, value_ref):
    length = q_ref.shape[0]
    live = live_rows(info_ref, heads, length)
    for h in range(heads):
        cut = slice(h * DH, (h + 1) * DH)
        q, k, v = head(q_ref, h), head(k_ref, h), head(v_ref, h)
        gate = info_ref[h : h + 1, :]
        grad = (head(grad_ref, h).astype(F32) * (1.0 - gate) * live).astype(BF16)
        probs = probs_ref[h]
        probs_grad = dot(grad, v, NT)
        full = probs.astype(F32)
        mean = jnp.sum(full * probs_grad, axis=1, keepdims=True)
        scores_grad = (full * (probs_grad - mean) * DH ** (-0.5)).astype(BF16)
        key_ref[:, cut] = dot(scores_grad, q, TN)
        value_ref[:, cut] = dot(probs, grad, TN)
        parts = memory_ref[h]
        numer = head(numer_ref, h)
        sig_grad = dot(numer, parts[:, 0:DH], NT) + dot(numer, parts[:, DH:], NT)
        sig_grad = sig_grad + denom_ref[h] * norm_ref[h, 0:1, :]
        total = dot(scores_grad, k, NN) + sig_grad * slope(q.astype(F32))
        query_ref[:, cut] = total.astype(BF16)


def last_kernel(heads, pos_ref, info_ref, k_ref, v_ref, other_ref, own_ref, far_ref, key_ref,
                value_ref, key_out, value_out):
    live = live_rows(info_ref, heads, k_ref.shape[0])
    upper = lax.rem(pos_ref[0], 2) == 1
    for h in range(heads):
        cut = slice(h * DH, (h + 1) * DH)
        i, part = h % (heads // 2), h // (heads // 2)
        own_here = upper if part else jnp.logical_not(upper)
        carry = jnp.where(own_here, own_ref[i], far_ref[i])
        other = other_ref[h]
        back = jnp.where(upper, carry, other[DH + 1 : DH + 2] * (other + carry))
        memory, norm = back[0:DH], back[DH : DH + 1]
        top, low = split(memory)
        k, v = head(k_ref, h).astype(F32), head(v_ref, h)
        sig = (feature(k) * live).astype(BF16)
        sig_grad = (dot(v, top, NT) + dot(v, low, NT) + norm) * live
        key_out[:, cut] = (key_ref[:, cut] + sig_grad * slope(k)).astype(BF16)
        more = dot(sig, jnp.concatenate([top, low], axis=1), NN)
        value_out[:, cut] = (value_ref[:, cut] + more[:, 0:DH] + more[:, DH:]).astype(BF16)


def weighted(state, forward):
    count, mine = lax.axis_size("seq"), lax.axis_index("seq")
    states = lax.all_gather(state, "seq")
    total = jnp.zeros_like(state)
    weight = jnp.ones((), F32)

    def turn(step, carried):
        total, weight = carried
        at = mine - 1 - step if forward else mine + 1 + step
        inside = (at >= 0) & (at < count)
        one = lax.dynamic_index_in_dim(states, jnp.clip(at, 0, count - 1), keepdims=False)
        opened = one[0, DH + 1, 0]
        here = weight if forward else weight * opened
        total = jnp.where(inside, total + here * one, total)
        return total, weight * opened

    return lax.fori_loop(0, count - 1, turn, (total, weight))[0]


def scan_states(state, pos, heads, forward, before_pair, before_join):
    count = lax.axis_size("seq")
    if count != 8:
        before_pair()
        before_join(state)
        carry = weighted(state, forward)
        place = jnp.full_like(pos, 0 if forward else 1)
        own, far = carry[: heads // 2], carry[heads // 2 :]
        return (own, far, state, place) if forward else (far, own, state, place)
    pairs = [(s, s ^ 1) for s in range(count)]
    other = lax.ppermute(state, "seq", pairs)
    flops = heads * DH * DH * 40
    after = before_pair()
    sent = call(
        functools.partial(pair_kernel, heads, forward),
        [jax.ShapeDtypeStruct((heads // 2, SENT, DH), BF16)],
        [SMEM, VMEM, VMEM] + [ANY] * len(after),
        [pos, state, other, *after],
        flops,
        name="pair",
    )[0]
    arrived = [
        lax.ppermute(sent, "seq", [(s, s ^ way) for s in range(count)]) for way in (6, 2, 4)
    ]
    after = before_join(sent)
    own = call(
        functools.partial(join_kernel, heads, forward),
        [jax.ShapeDtypeStruct((heads // 2, ROWS, DH), F32)],
        [SMEM, VMEM, VMEM, VMEM] + [ANY] * len(after),
        [pos, arrived[1], arrived[2], arrived[0], *after],
        flops,
        name="join",
    )[0]
    far = lax.ppermute(own, "seq", pairs)
    return own, far, other, pos


def shards(queries, keys, values, gate, out_weight, out_grad, valid, starts):
    length, width = queries.shape
    heads = width // DH
    cols = out_grad.shape[1]
    groups = lax.axis_size("head")
    direct = groups == 4
    pos = lax.axis_index("seq").astype(jnp.int32).reshape(1)
    z = lax.axis_index("head").astype(jnp.int32)
    flat = jax.ShapeDtypeStruct((length, width), F32)
    low = jax.ShapeDtypeStruct((length, width), BF16)
    part_low = jax.ShapeDtypeStruct((length, cols), BF16)
    part_full = jax.ShapeDtypeStruct((length, cols), F32)
    states = jax.ShapeDtypeStruct((heads, ROWS, DH), F32)
    square = 2 * heads * length * DH * DH
    block = 2 * length * width * cols

    def ids(*ways):
        return jnp.stack([z ^ way for way in ways])

    def slots(count):
        return pltpu.VMEM((count, width, cols), BF16)

    queries, keys, values, grad_here, info, state = call(
        functools.partial(load_kernel, heads),
        [low, low, low, part_low, jax.ShapeDtypeStruct((heads + 8, DH), F32), states],
        [ANY] * 7,
        [queries, keys, values, out_grad, valid, starts, gate], square,
        [pltpu.SMEM((1,), jnp.int32), pltpu.SMEM((1,), jnp.int32), pltpu.SMEM((heads,), F32),
         DMA((7,))],
        name="load",
    )

    def swap(array, way):
        return lax.ppermute(array, "head", [(s, s ^ way) for s in range(groups)])

    if direct:
        grad_3 = swap(grad_here, 3)
        grad_1 = swap(grad_here, 1)
        grad_2 = swap(grad_3, 1)

    kept = {}

    def beside_forward(sent):
        kept["local"] = call(
            functools.partial(local_kernel, heads),
            [jax.ShapeDtypeStruct((heads, length, length), BF16), flat],
            [VMEM] * 4 + [ANY],
            [info, queries, keys, values, sent], 2 * square, name="local",
        )
        if not direct:
            return []
        kept["total"] = call(
            own_kernel, [flat], [SMEM, VMEM, ANY, ANY],
            [ids(0), grad_here, out_weight, kept["local"][0]], block, [slots(1), DMA((1,))],
            name="unproject_own",
        )[0]
        return [kept["total"]]

    own, far, other, place = scan_states(state, pos, heads, True, lambda: [], beside_forward)
    probs, local = kept["local"]
    read_outs = [low, flat, jax.ShapeDtypeStruct((heads, DH, 2 * DH), BF16),
                 jax.ShapeDtypeStruct((heads, 8, DH), F32)]
    outs = call(
        functools.partial(read_kernel, heads, direct),
        read_outs + [part_low] * direct,
        [SMEM, SMEM] + [VMEM] * 7 + [ANY] * direct,
        [place, ids(2), info, queries, state, other, own, far, local] + [out_weight] * direct,
        2 * square + block * direct,
        [slots(1), DMA((1,))] if direct else [],
        name="read",
    )
    mixed, read, memory, norm = outs[:4]
    if direct:
        sum_2 = swap(outs[4], 1)
        grads_in = [grad_1, grad_3, grad_2, kept["total"], out_weight]
    else:
        part = dot(mixed, out_weight, NN)
        output = lax.psum_scatter(part, "head", scatter_dimension=1, tiled=True).astype(BF16)
        whole = lax.all_gather(out_grad, "head", axis=1, tiled=True)
        grads_in = [dot(whole, out_weight, NT).astype(BF16)]
    outs = call(
        functools.partial(spread_kernel, heads, 3 * direct),
        [states, low, jax.ShapeDtypeStruct((heads, length, 1), F32)] + [low] * direct,
        [SMEM] + [VMEM] * 4 + ([VMEM] * 4 + [ANY] if direct else [VMEM]),
        [ids(1, 3, 2), info, queries, norm, read, *grads_in],
        square + 3 * block * direct,
        [slots(3), DMA((heads // 2, 3))] if direct else [],
        name="spread",
    )
    passed, numer_grad, denom_grad = outs[:3]
    mixed_grad = outs[3] if direct else grads_in[0]

    def add_here():
        if not direct:
            return []
        kept["sum_3"] = call(
            add_kernel, [part_low], [SMEM, VMEM, ANY, VMEM, ANY],
            [ids(3), mixed, out_weight, sum_2, passed], block, [slots(1), DMA((1,))],
            name="project_add",
        )[0]
        kept["from_3"] = swap(kept["sum_3"], 3)
        return [kept["sum_3"]]

    def beside_back(sent):
        after = sent
        if direct:
            near, kept["own"] = call(
                rest_kernel, [part_low, part_full], [SMEM, VMEM, ANY, ANY],
                [ids(1, 0), mixed, out_weight, sent], 2 * block, [slots(2), DMA((2,))],
                name="project_rest",
            )
            kept["from_1"] = swap(near, 1)
            after = near
        kept["grads"] = call(
            functools.partial(grads_kernel, heads),
            [low, flat, flat],
            [VMEM] * 10 + [ANY],
            [info, queries, keys, values, probs, mixed_grad, numer_grad, denom_grad, memory, norm,
             after],
            6 * square, name="grads",
        )
        return [kept["grads"][1]]

    own, far, other, place = scan_states(passed, pos, heads, False, add_here, beside_back)
    query_grad, key_part, value_part = kept["grads"]
    if direct:
        output = kept["own"] + kept["from_1"].astype(F32) + kept["from_3"].astype(F32)
        output = output.astype(BF16)
    key_grad, value_grad = call(
        functools.partial(last_kernel, heads),
        [low, low],
        [SMEM] + [VMEM] * 8,
        [place, info, keys, values, other, own, far, key_part, value_part], 4 * square, name="last",
    )
    return (output, query_grad, key_grad, value_grad)


def solution(mesh):
    placed = (
        P("seq", "head"),
        P("seq", "head"),
        P("seq", "head"),
        P("head"),
        P("head", None),
        P("seq", "head"),
        P("seq"),
        P("seq"),
    )
    return jax.shard_map(
        shards,
        mesh=mesh,
        in_specs=placed,
        out_specs=(P("seq", "head"), P("seq", "head"), P("seq", "head"), P("seq", "head")),
        check_vma=False,
    )
```

```python
import functools

import jax
import jax.numpy as jnp
from jax import lax
from jax.experimental import pallas as pl
from jax.experimental.pallas import tpu as pltpu
from jax.sharding import PartitionSpec as P

DH = 128
ROWS = 136
SENT = 144
BF16 = jnp.bfloat16
F32 = jnp.float32
VMEM = pl.BlockSpec(memory_space=pltpu.VMEM)
SMEM = pl.BlockSpec(memory_space=pltpu.SMEM)


ANY = pl.BlockSpec(memory_space=pl.ANY)


def call(kernel, outs, in_specs, args, micros, name):
    return pl.pallas_call(
        kernel,
        out_shape=outs,
        in_specs=in_specs,
        out_specs=[VMEM] * len(outs),
        compiler_params=pltpu.CompilerParams(vmem_limit_bytes=24 * 1024 * 1024),
        cost_estimate=pl.CostEstimate(flops=int(micros * 1.15e9), bytes_accessed=1024, transcendentals=0),
        name=name,
    )(*args)


def feature(x):
    return jnp.where(x > 0, x + 1.0, jnp.exp(jnp.minimum(x, 0.0)))


def slope(x):
    return jnp.where(x > 0, 1.0, jnp.where(x == 0, 0.5, jnp.exp(jnp.minimum(x, 0.0))))


def sigmoid(x):
    return 1.0 / (1.0 + jnp.exp(-x))


def dot(a, b, dims):
    return lax.dot_general(a, b, (dims, ((), ())), preferred_element_type=F32)


NN = ((1,), (0,))
NT = ((1,), (1,))
TN = ((0,), (0,))


def live_rows(valid_ref, length):
    where = lax.broadcasted_iota(jnp.int32, (length, 1), 0)
    return (where < valid_ref[...]).astype(F32)


def opened(starts_ref):
    return 1.0 - starts_ref[...].astype(F32)


def gate_row(gate_ref, h):
    return sigmoid(jnp.full((1, DH), gate_ref[h], F32))


def head(ref, h):
    return ref[:, h * DH : (h + 1) * DH]


def tail(rows, *values):
    where = lax.broadcasted_iota(jnp.int32, (rows, DH), 0)
    out = jnp.zeros((rows, DH), F32)
    for at, value in enumerate(values):
        out = jnp.where(where == at, value, out)
    return out


def split(x):
    top = x.astype(BF16)
    rest = x - top.astype(F32)
    return top, rest.astype(BF16)


def state_kernel(heads, pos_ref, z_ref, valid_ref, starts_ref, k_ref, v_ref, state_ref):
    live = live_rows(valid_ref, k_ref.shape[0])
    for h in range(heads):
        sig = (feature(head(k_ref, h).astype(F32)) * live).astype(BF16)
        state_ref[h, 0:DH, :] = dot(sig, head(v_ref, h), TN)
        norm = jnp.sum(sig.astype(F32), axis=0, keepdims=True)
        state_ref[h, DH:ROWS, :] = tail(ROWS - DH, norm, opened(starts_ref))


def pair_kernel(heads, forward, pos_ref, mine_ref, other_ref, *refs):
    sent_ref = refs[-1]
    half = lax.rem(pos_ref[0], 2)
    lower = half == 0
    for i in range(heads // 2):
        h = half * (heads // 2) + i
        mine, other = mine_ref[h], other_ref[h]
        first = jnp.where(lower, mine, other)
        second = jnp.where(lower, other, mine)
        open_first, open_second = first[DH + 1 : DH + 2], second[DH + 1 : DH + 2]
        if forward:
            total = open_second * first + second
        else:
            total = open_first * (first + open_second * second)
        memory, norm = total[0:DH], total[DH : DH + 1]
        norm_1, rest = split(norm)
        norm_1 = norm_1.astype(F32)
        norm_2 = rest.astype(F32)
        norm_3 = norm - norm_1 - norm_2
        if forward:
            weight = jnp.maximum(jnp.sum(norm, axis=1, keepdims=True), 1e-30)
            centre = jnp.sum(memory, axis=0, keepdims=True) / weight
            centre = centre.astype(BF16).astype(F32)
            norms = tail(16, norm_1, norm_2, norm_3).astype(BF16)
            centres = tail(16, centre, centre, centre).astype(BF16)
            memory = memory - dot(norms, centres, TN)
        else:
            centre = jnp.zeros_like(norm)
        sent_ref[i, 0:DH, :] = memory.astype(BF16)
        rows = tail(SENT - DH, norm_1, norm_2, norm_3, centre, open_first * open_second)
        sent_ref[i, DH:SENT, :] = rows.astype(BF16)


def join_kernel(heads, forward, pos_ref, x_ref, y_ref, d_ref, *refs):
    carry_ref = refs[-1]
    chip = pos_ref[0] // 2
    place = chip if forward else 3 - chip
    for i in range(heads // 2):
        totals = []
        for ref in (x_ref, y_ref, d_ref):
            memory = ref[i, 0:DH, :].astype(F32)
            rows = ref[i, DH:SENT, :].astype(F32)
            norm = rows[0:1] + rows[1:2] + rows[2:3]
            if forward:
                norms = tail(16, rows[0:1], rows[1:2], rows[2:3]).astype(BF16)
                centres = tail(16, rows[3:4], rows[3:4], rows[3:4]).astype(BF16)
                memory = memory + dot(norms, centres, TN)
            totals.append((memory, norm, rows[4:5]))
        (x_mem, x_norm, x_open), (y_mem, y_norm, y_open), (d_mem, d_norm, d_open) = totals
        odd, high = lax.rem(place, 2) == 1, place >= 2
        on_x = jnp.where(odd, jnp.ones_like(x_open), 0.0)
        on_y = jnp.where(high, jnp.where(odd, x_open, d_open), 0.0)
        on_d = jnp.where(high, jnp.where(odd, x_open * y_open, 1.0), 0.0)
        norm = on_x * x_norm + on_y * y_norm + on_d * d_norm
        carry_ref[i, 0:DH, :] = on_x * x_mem + on_y * y_mem + on_d * d_mem
        carry_ref[i, DH:ROWS, :] = tail(ROWS - DH, norm)


def local_kernel(heads, valid_ref, q_ref, k_ref, v_ref, after_ref, probs_ref, local_ref):
    length = q_ref.shape[0]
    row = lax.broadcasted_iota(jnp.int32, (length, length), 0)
    col = lax.broadcasted_iota(jnp.int32, (length, length), 1)
    allowed = (col <= row) & (col < valid_ref[...])
    for h in range(heads):
        scores = dot(head(q_ref, h), head(k_ref, h), NT) * DH ** (-0.5)
        scores = jnp.where(allowed, scores, -1e30)
        expo = jnp.exp(scores - jnp.max(scores, axis=1, keepdims=True))
        probs = (expo / jnp.sum(expo, axis=1, keepdims=True)).astype(BF16)
        probs_ref[h] = probs
        local_ref[:, h * DH : (h + 1) * DH] = dot(probs, head(v_ref, h), NN)


def columns(z_ref, way, cols):
    return pl.ds(pl.multiple_of((z_ref[0] ^ way) * cols, DH), cols)


def read_kernel(
    heads, project, pos_ref, z_ref, valid_ref, gate_ref, q_ref, mine_ref, other_ref, own_ref, far_ref, local_ref,
    *refs,
):
    if project:
        weight_ref, after_ref, mixed_ref, read_ref, memory_ref, norm_ref, first_ref = refs
    else:
        mixed_ref, read_ref, memory_ref, norm_ref = refs
    live = live_rows(valid_ref, q_ref.shape[0])
    upper = lax.rem(pos_ref[0], 2) == 1
    for h in range(heads):
        i, part = h % (heads // 2), h // (heads // 2)
        own_here = upper if part else jnp.logical_not(upper)
        carry = jnp.where(own_here, own_ref[i], far_ref[i])
        other = other_ref[h]
        before = jnp.where(upper, other[DH + 1 : DH + 2] * carry + other, carry)
        state = mine_ref[h, DH + 1 : DH + 2, :] * before
        memory, norm = state[0:DH], state[DH : DH + 1]
        parts = jnp.concatenate(split(memory), axis=1)
        memory_ref[h] = parts
        norm_ref[h] = jnp.broadcast_to(norm, (8, DH))
        sig = feature(head(q_ref, h).astype(F32)).astype(BF16)
        numer = dot(sig, parts, NN)
        numer = numer[:, 0:DH] + numer[:, DH:]
        denom = jnp.sum(sig.astype(F32) * norm, axis=1, keepdims=True) + 1.0
        read = numer / denom
        gate = gate_row(gate_ref, h)
        mixed = live * (gate * read + (1.0 - gate) * head(local_ref, h))
        read_ref[:, h * DH : (h + 1) * DH] = read
        mixed_ref[:, h * DH : (h + 1) * DH] = mixed.astype(BF16)
    if project:
        block = weight_ref[:, columns(z_ref, 2, first_ref.shape[1])]
        first_ref[...] = dot(mixed_ref[...], block, NN).astype(BF16)


def more_kernel(ways, z_ref, *refs):
    grad_refs, (weight_ref, *before, after_ref, total_ref) = refs[: len(ways)], refs[len(ways) :]
    total = before[0][...] if before else None
    for way, grad_ref in zip(ways, grad_refs):
        block = weight_ref[:, columns(z_ref, way, grad_ref.shape[1])]
        part = dot(grad_ref[...], block, NT)
        total = part if total is None else total + part
    total_ref[...] = total


def add_kernel(z_ref, mixed_ref, weight_ref, more_ref, after_ref, out_ref):
    block = weight_ref[:, columns(z_ref, 3, out_ref.shape[1])]
    part = dot(mixed_ref[...], block, NN)
    out_ref[...] = (part + more_ref[...].astype(F32)).astype(BF16)


def rest_kernel(z_ref, mixed_ref, weight_ref, after_ref, near_ref, own_ref):
    cols = own_ref.shape[1]
    near = dot(mixed_ref[...], weight_ref[:, columns(z_ref, 1, cols)], NN)
    near_ref[...] = near.astype(BF16)
    own_ref[...] = dot(mixed_ref[...], weight_ref[:, columns(z_ref, 0, cols)], NN)


def spread_kernel(
    heads, ways, z_ref, valid_ref, starts_ref, gate_ref, q_ref, norm_ref, read_ref, *refs,
):
    if ways:
        parts, (total_ref, weight_ref) = refs[: len(ways)], refs[len(ways) : len(ways) + 2]
        passed_ref, numer_ref, denom_ref, grad_ref = refs[len(ways) + 3 :]
        total = total_ref[...]
        for way, part_ref in zip(ways, parts):
            block = weight_ref[:, columns(z_ref, way, part_ref.shape[1])]
            total = total + dot(part_ref[...], block, NT)
        grad_ref[...] = total.astype(BF16)
    else:
        grad_ref, passed_ref, numer_ref, denom_ref = refs
    live = live_rows(valid_ref, q_ref.shape[0])
    for h in range(heads):
        cut = slice(h * DH, (h + 1) * DH)
        sig = feature(head(q_ref, h).astype(F32)).astype(BF16)
        sig_full = sig.astype(F32)
        denom = jnp.sum(sig_full * norm_ref[h, 0:1, :], axis=1, keepdims=True) + 1.0
        gate = gate_row(gate_ref, h)
        numer_grad = (head(grad_ref, h).astype(F32) * gate * (live / denom)).astype(BF16)
        denom_grad = -jnp.sum(
            numer_grad.astype(F32) * head(read_ref, h), axis=1, keepdims=True
        )
        passed_ref[h, 0:DH, :] = dot(sig, numer_grad, TN)
        norm_grad = jnp.sum(sig_full * denom_grad, axis=0, keepdims=True)
        passed_ref[h, DH:ROWS, :] = tail(ROWS - DH, norm_grad, opened(starts_ref))
        numer_ref[:, cut] = numer_grad
        denom_ref[h] = denom_grad


def grads_kernel(heads, valid_ref, gate_ref, q_ref, k_ref, v_ref, probs_ref, grad_ref, numer_ref,
                 denom_ref, memory_ref, norm_ref, after_ref, query_ref, key_ref, value_ref):
    length = q_ref.shape[0]
    live = live_rows(valid_ref, length)
    for h in range(heads):
        cut = slice(h * DH, (h + 1) * DH)
        q, k, v = head(q_ref, h), head(k_ref, h), head(v_ref, h)
        gate = gate_row(gate_ref, h)
        grad = (head(grad_ref, h).astype(F32) * (1.0 - gate) * live).astype(BF16)
        probs = probs_ref[h]
        probs_grad = dot(grad, v, NT)
        full = probs.astype(F32)
        mean = jnp.sum(full * probs_grad, axis=1, keepdims=True)
        scores_grad = (full * (probs_grad - mean) * DH ** (-0.5)).astype(BF16)
        key_ref[:, cut] = dot(scores_grad, q, TN)
        value_ref[:, cut] = dot(probs, grad, TN)
        parts = memory_ref[h]
        numer = head(numer_ref, h)
        sig_grad = dot(numer, parts[:, 0:DH], NT) + dot(numer, parts[:, DH:], NT)
        sig_grad = sig_grad + denom_ref[h] * norm_ref[h, 0:1, :]
        total = dot(scores_grad, k, NN) + sig_grad * slope(q.astype(F32))
        query_ref[:, cut] = total.astype(BF16)


def last_kernel(heads, pos_ref, valid_ref, k_ref, v_ref, other_ref, own_ref, far_ref, key_ref,
                value_ref, key_out, value_out):
    live = live_rows(valid_ref, k_ref.shape[0])
    upper = lax.rem(pos_ref[0], 2) == 1
    for h in range(heads):
        cut = slice(h * DH, (h + 1) * DH)
        i, part = h % (heads // 2), h // (heads // 2)
        own_here = upper if part else jnp.logical_not(upper)
        carry = jnp.where(own_here, own_ref[i], far_ref[i])
        other = other_ref[h]
        back = jnp.where(upper, carry, other[DH + 1 : DH + 2] * (other + carry))
        memory, norm = back[0:DH], back[DH : DH + 1]
        top, low = split(memory)
        k, v = head(k_ref, h).astype(F32), head(v_ref, h)
        sig = (feature(k) * live).astype(BF16)
        sig_grad = (dot(v, top, NT) + dot(v, low, NT) + norm) * live
        key_out[:, cut] = (key_ref[:, cut] + sig_grad * slope(k)).astype(BF16)
        more = dot(sig, jnp.concatenate([top, low], axis=1), NN)
        value_out[:, cut] = (value_ref[:, cut] + more[:, 0:DH] + more[:, DH:]).astype(BF16)


def weighted(state, forward):
    count, mine = lax.axis_size("seq"), lax.axis_index("seq")
    states = lax.all_gather(state, "seq")
    total = jnp.zeros_like(state)
    weight = jnp.ones((), F32)

    def turn(step, carried):
        total, weight = carried
        at = mine - 1 - step if forward else mine + 1 + step
        inside = (at >= 0) & (at < count)
        one = lax.dynamic_index_in_dim(states, jnp.clip(at, 0, count - 1), keepdims=False)
        opened = one[0, DH + 1, 0]
        here = weight if forward else weight * opened
        total = jnp.where(inside, total + here * one, total)
        return total, weight * opened

    return lax.fori_loop(0, count - 1, turn, (total, weight))[0]


def scan_states(state, pos, heads, forward, before_pair, before_join):
    count = lax.axis_size("seq")
    if count != 8:
        before_pair()
        before_join(state)
        carry = weighted(state, forward)
        place = jnp.full_like(pos, 0 if forward else 1)
        own, far = carry[: heads // 2], carry[heads // 2 :]
        return (own, far, state, place) if forward else (far, own, state, place)
    pairs = [(s, s ^ 1) for s in range(count)]
    other = lax.ppermute(state, "seq", pairs)
    after = before_pair()
    sent = call(
        functools.partial(pair_kernel, heads, forward),
        [jax.ShapeDtypeStruct((heads // 2, SENT, DH), BF16)],
        [SMEM, VMEM, VMEM] + [ANY] * len(after),
        [pos, state, other, *after],
        0.3, "pair",
    )[0]
    arrived = [
        lax.ppermute(sent, "seq", [(s, s ^ way) for s in range(count)]) for way in (6, 2, 4)
    ]
    after = before_join(sent)
    own = call(
        functools.partial(join_kernel, heads, forward),
        [jax.ShapeDtypeStruct((heads // 2, ROWS, DH), F32)],
        [SMEM, VMEM, VMEM, VMEM] + [ANY] * len(after),
        [pos, arrived[1], arrived[2], arrived[0], *after],
        0.3, "join",
    )[0]
    far = lax.ppermute(own, "seq", pairs)
    return own, far, other, pos


def shards(queries, keys, values, gate, out_weight, out_grad, valid, starts):
    length, width = queries.shape
    heads = width // DH
    cols = out_grad.shape[1]
    groups = lax.axis_size("head")
    direct = groups == 4
    pos = lax.axis_index("seq").astype(jnp.int32).reshape(1)
    z = lax.axis_index("head").astype(jnp.int32).reshape(1)
    valid, starts = valid.reshape(1, 1), starts.reshape(1, 1)
    flat = jax.ShapeDtypeStruct((length, width), F32)
    low = jax.ShapeDtypeStruct((length, width), BF16)
    part_low = jax.ShapeDtypeStruct((length, cols), BF16)
    part_full = jax.ShapeDtypeStruct((length, cols), F32)
    states = jax.ShapeDtypeStruct((heads, ROWS, DH), F32)

    def swap(array, way):
        return lax.ppermute(array, "head", [(s, s ^ way) for s in range(groups)])

    state = call(
        functools.partial(state_kernel, heads), [states], [SMEM] * 2 + [VMEM] * 4,
        [pos, z, valid, starts, keys, values], 0.4, "state",
    )[0]
    if direct:
        grad_3 = swap(out_grad, 3)
        grad_1 = swap(out_grad, 1)
        grad_2 = swap(grad_3, 1)
    kept = {}

    def beside_forward(sent):
        kept["local"] = call(
            functools.partial(local_kernel, heads),
            [jax.ShapeDtypeStruct((heads, length, length), BF16), flat],
            [VMEM] * 4 + [ANY],
            [valid, queries, keys, values, sent], 2.7, "local",
        )
        return [kept["local"][1]]

    own, far, other, place = scan_states(state, pos, heads, True, lambda: [], beside_forward)
    probs, local = kept["local"]
    if direct:
        total = call(
            functools.partial(more_kernel, (0, 1)), [flat], [SMEM] + [VMEM] * 3 + [ANY],
            [z, out_grad, grad_1, out_weight, own], 1.5, "unproject_near",
        )[0]
    outs = call(
        functools.partial(read_kernel, heads, direct),
        [low, flat, jax.ShapeDtypeStruct((heads, DH, 2 * DH), BF16),
         jax.ShapeDtypeStruct((heads, 8, DH), F32)] + [part_low] * direct,
        [SMEM, SMEM, VMEM, SMEM] + [VMEM] * 6 + [VMEM, ANY] * direct,
        [place, z, valid, gate, queries, state, other, own, far, local]
        + ([out_weight, total] if direct else []),
        0.9, "read",
    )
    mixed, read, memory, norm = outs[:4]
    if direct:
        sum_2 = swap(outs[4], 1)
        total = call(
            functools.partial(more_kernel, (3,)), [flat], [SMEM] + [VMEM] * 3 + [ANY],
            [z, grad_3, out_weight, total, mixed], 0.9, "unproject_more",
        )[0]
        grads_in = [grad_2, total, out_weight]
    else:
        part = dot(mixed, out_weight, NN)
        output = lax.psum_scatter(part, "head", scatter_dimension=1, tiled=True).astype(BF16)
        whole = lax.all_gather(out_grad, "head", axis=1, tiled=True)
        grads_in = [dot(whole, out_weight, NT).astype(BF16)]
    outs = call(
        functools.partial(spread_kernel, heads, (2,) * direct),
        [states, low, jax.ShapeDtypeStruct((heads, length, 1), F32)] + [low] * direct,
        [SMEM, VMEM, VMEM, SMEM] + [VMEM] * (3 + len(grads_in)) + [ANY] * direct,
        [z, valid, starts, gate, queries, norm, read, *grads_in] + ([sum_2] if direct else []),
        2.5, "spread",
    )
    passed, numer_grad, denom_grad = outs[:3]
    mixed_grad = outs[3] if direct else grads_in[0]

    def add_here():
        if not direct:
            return []
        sum_3 = call(
            add_kernel, [part_low], [SMEM, VMEM, VMEM, VMEM, ANY],
            [z, mixed, out_weight, sum_2, passed], 0.5, "project_add",
        )[0]
        kept["from_3"] = swap(sum_3, 3)
        return [sum_3]

    def beside_back(sent):
        after = sent
        if direct:
            near, kept["own"] = call(
                rest_kernel, [part_low, part_full], [SMEM, VMEM, VMEM, ANY],
                [z, mixed, out_weight, sent], 1.3, "project_rest",
            )
            kept["from_1"] = swap(near, 1)
            after = near
        kept["grads"] = call(
            functools.partial(grads_kernel, heads),
            [low, flat, flat],
            [VMEM, SMEM] + [VMEM] * 9 + [ANY],
            [valid, gate, queries, keys, values, probs, mixed_grad, numer_grad, denom_grad, memory,
             norm, after],
            3.1, "grads",
        )
        return [kept["grads"][1]]

    own, far, other, place = scan_states(passed, pos, heads, False, add_here, beside_back)
    query_grad, key_part, value_part = kept["grads"]
    if direct:
        output = kept["own"] + kept["from_1"].astype(F32) + kept["from_3"].astype(F32)
        output = output.astype(BF16)
    key_grad, value_grad = call(
        functools.partial(last_kernel, heads),
        [low, low],
        [SMEM] + [VMEM] * 8,
        [place, valid, keys, values, other, own, far, key_part, value_part], 1.5, "last",
    )
    return (output, query_grad, key_grad, value_grad)


def solution(mesh):
    placed = (
        P("seq", "head"),
        P("seq", "head"),
        P("seq", "head"),
        P("head"),
        P("head", None),
        P("seq", "head"),
        P("seq"),
        P("seq"),
    )
    return jax.shard_map(
        shards,
        mesh=mesh,
        in_specs=placed,
        out_specs=(P("seq", "head"), P("seq", "head"), P("seq", "head"), P("seq", "head")),
        check_vma=False,
    )
```

```python
import functools

import jax
import jax.numpy as jnp
from jax import lax
from jax.experimental import pallas as pl
from jax.experimental.pallas import tpu as pltpu
from jax.sharding import PartitionSpec as P

DH = 128
ROWS = 136
SENT = 144
BF16 = jnp.bfloat16
F32 = jnp.float32
VMEM = pl.BlockSpec(memory_space=pltpu.VMEM)
SMEM = pl.BlockSpec(memory_space=pltpu.SMEM)


ANY = pl.BlockSpec(memory_space=pl.ANY)


def call(kernel, outs, in_specs, args, micros, name):
    return pl.pallas_call(
        kernel,
        out_shape=outs,
        in_specs=in_specs,
        out_specs=[VMEM] * len(outs),
        compiler_params=pltpu.CompilerParams(vmem_limit_bytes=24 * 1024 * 1024),
        cost_estimate=pl.CostEstimate(flops=int(micros * 1.15e9), bytes_accessed=1024, transcendentals=0),
        name=name,
    )(*args)


def feature(x):
    return jnp.where(x > 0, x + 1.0, jnp.exp(jnp.minimum(x, 0.0)))


def slope(x):
    return jnp.where(x > 0, 1.0, jnp.where(x == 0, 0.5, jnp.exp(jnp.minimum(x, 0.0))))


def sigmoid(x):
    return 1.0 / (1.0 + jnp.exp(-x))


def dot(a, b, dims):
    return lax.dot_general(a, b, (dims, ((), ())), preferred_element_type=F32)


NN = ((1,), (0,))
NT = ((1,), (1,))
TN = ((0,), (0,))


def live_rows(valid_ref, length):
    where = lax.broadcasted_iota(jnp.int32, (length, 1), 0)
    return (where < valid_ref[...]).astype(F32)


def opened(starts_ref):
    return 1.0 - starts_ref[...].astype(F32)


def gate_row(gate_ref, h):
    return sigmoid(jnp.full((1, DH), gate_ref[h], F32))


def head(ref, h):
    return ref[:, h * DH : (h + 1) * DH]


def tail(rows, *values):
    where = lax.broadcasted_iota(jnp.int32, (rows, DH), 0)
    out = jnp.zeros((rows, DH), F32)
    for at, value in enumerate(values):
        out = jnp.where(where == at, value, out)
    return out


def split(x):
    top = x.astype(BF16)
    rest = x - top.astype(F32)
    return top, rest.astype(BF16)


def cut(h):
    return pl.ds(h * DH if isinstance(h, int) else pl.multiple_of(h * DH, DH), DH)


def by_half(heads, pos_ref):
    half = lax.rem(pos_ref[0], 2)
    count = heads // 2
    for kept, first in ((True, half * count), (False, (1 - half) * count)):
        for i in range(count):
            yield kept, i, first + i


def state_kernel(
    heads, pos_ref, z_ref, valid_ref, starts_ref, k_ref, v_ref, keep_ref, give_ref
):
    live = live_rows(valid_ref, k_ref.shape[0])
    for kept, i, h in by_half(heads, pos_ref):
        out_ref = keep_ref if kept else give_ref
        sig = (feature(k_ref[:, cut(h)].astype(F32)) * live).astype(BF16)
        out_ref[i, 0:DH, :] = dot(sig, v_ref[:, cut(h)], TN)
        norm = jnp.sum(sig.astype(F32), axis=0, keepdims=True)
        out_ref[i, DH:ROWS, :] = tail(ROWS - DH, norm, opened(starts_ref))


def in_three(x):
    first = x.astype(BF16).astype(F32)
    second = (x - first).astype(BF16).astype(F32)
    return first, second, x - first - second


def store_sent(ref, i, memory, norm, flag, centre):
    ref[i, 0:DH, :] = memory.astype(BF16)
    ref[i, DH:SENT, :] = tail(SENT - DH, *in_three(norm), centre, flag).astype(BF16)


def load_sent(ref, i, centred):
    memory = ref[i, 0:DH, :].astype(F32)
    rows = ref[i, DH:SENT, :].astype(F32)
    if centred:
        norms = tail(16, rows[0:1], rows[1:2], rows[2:3]).astype(BF16)
        centres = tail(16, rows[3:4], rows[3:4], rows[3:4]).astype(BF16)
        memory = memory + dot(norms, centres, TN)
    return memory, rows[0:1] + rows[1:2] + rows[2:3], rows[4:5]


def load_state(ref, i):
    return ref[i, 0:DH, :], ref[i, DH : DH + 1, :], ref[i, DH + 1 : DH + 2, :]


def load_other(ref, i, forward):
    return load_state(ref, i) if forward else load_sent(ref, i, False)


def pair_kernel(heads, forward, pos_ref, keep_ref, other_ref, *refs):
    sent_ref = refs[-1]
    lower = lax.rem(pos_ref[0], 2) == 0
    for i in range(heads // 2):
        memory, norm, flag = load_state(keep_ref, i)
        other_memory, other_norm, other_flag = load_other(other_ref, i, forward)
        one = jnp.ones_like(flag)
        if forward:
            on_mine = jnp.where(lower, other_flag, one)
            on_other = jnp.where(lower, one, flag)
        else:
            on_mine = jnp.where(lower, flag, flag * other_flag)
            on_other = jnp.where(lower, flag * other_flag, other_flag)
        memory = on_mine * memory + on_other * other_memory
        norm = on_mine * norm + on_other * other_norm
        centre = jnp.zeros_like(norm)
        if forward:
            weight = jnp.maximum(jnp.sum(norm, axis=1, keepdims=True), 1e-30)
            centre = jnp.sum(memory, axis=0, keepdims=True) / weight
            centre = centre.astype(BF16).astype(F32)
            norms = tail(16, *in_three(norm)).astype(BF16)
            centres = tail(16, centre, centre, centre).astype(BF16)
            memory = memory - dot(norms, centres, TN)
        store_sent(sent_ref, i, memory, norm, flag * other_flag, centre)


def join_kernel(
    heads, forward, pos_ref, x_ref, y_ref, d_ref, keep_ref, other_ref, *refs
):
    own_ref, sent_ref = refs[-2:]
    lower = lax.rem(pos_ref[0], 2) == 0
    chip = pos_ref[0] // 2
    place = chip if forward else 3 - chip
    odd, high = lax.rem(place, 2) == 1, place >= 2
    for i in range(heads // 2):
        x_mem, x_norm, x_open = load_sent(x_ref, i, forward)
        y_mem, y_norm, y_open = load_sent(y_ref, i, forward)
        d_mem, d_norm, d_open = load_sent(d_ref, i, forward)
        on_x = jnp.where(odd, jnp.ones_like(x_open), 0.0)
        on_y = jnp.where(high, jnp.where(odd, x_open, d_open), 0.0)
        on_d = jnp.where(high, jnp.where(odd, x_open * y_open, 1.0), 0.0)
        memory = on_x * x_mem + on_y * y_mem + on_d * d_mem
        norm = on_x * x_norm + on_y * y_norm + on_d * d_norm
        mine_mem, mine_norm, mine_open = load_state(keep_ref, i)
        other_mem, other_norm, other_open = load_other(other_ref, i, forward)
        if forward:
            own = (
                jnp.where(lower, memory, other_open * memory + other_mem),
                jnp.where(lower, norm, other_open * norm + other_norm),
            )
            sent = (
                jnp.where(lower, mine_open * memory + mine_mem, memory),
                jnp.where(lower, mine_open * norm + mine_norm, norm),
            )
        else:
            own = (
                jnp.where(lower, other_open * (memory + other_mem), memory),
                jnp.where(lower, other_open * (norm + other_norm), norm),
            )
            sent = (
                jnp.where(lower, memory, mine_open * (memory + mine_mem)),
                jnp.where(lower, norm, mine_open * (norm + mine_norm)),
            )
        for ref, (value, sums) in ((own_ref, own), (sent_ref, sent)):
            ref[i, 0:DH, :] = value
            ref[i, DH:ROWS, :] = tail(ROWS - DH, sums)


def local_kernel(heads, valid_ref, q_ref, k_ref, v_ref, after_ref, probs_ref, local_ref):
    length = q_ref.shape[0]
    row = lax.broadcasted_iota(jnp.int32, (length, length), 0)
    col = lax.broadcasted_iota(jnp.int32, (length, length), 1)
    allowed = (col <= row) & (col < valid_ref[...])
    for h in range(heads):
        scores = dot(head(q_ref, h), head(k_ref, h), NT) * DH ** (-0.5)
        scores = jnp.where(allowed, scores, -1e30)
        expo = jnp.exp(scores - jnp.max(scores, axis=1, keepdims=True))
        probs = (expo / jnp.sum(expo, axis=1, keepdims=True)).astype(BF16)
        probs_ref[h] = probs
        local_ref[:, h * DH : (h + 1) * DH] = dot(probs, head(v_ref, h), NN)


def columns(z_ref, way, cols):
    return pl.ds(pl.multiple_of((z_ref[0] ^ way) * cols, DH), cols)


def read_kernel(
    heads, project, pos_ref, z_ref, valid_ref, gate_ref, q_ref, keep_ref, own_ref, far_ref,
    local_ref, *refs,
):
    if project:
        weight_ref, _, mixed_ref, read_ref, memory_ref, norm_ref, first_ref = refs
    else:
        mixed_ref, read_ref, memory_ref, norm_ref = refs
    live = live_rows(valid_ref, q_ref.shape[0])
    for kept, i, h in by_half(heads, pos_ref):
        carry, norm, _ = load_state(own_ref if kept else far_ref, i)
        flag = keep_ref[i, DH + 1 : DH + 2, :]
        norm = flag * norm
        parts = jnp.concatenate(split(flag * carry), axis=1)
        memory_ref[h] = parts
        norm_ref[h] = jnp.broadcast_to(norm, (8, DH))
        sig = feature(q_ref[:, cut(h)].astype(F32)).astype(BF16)
        numer = dot(sig, parts, NN)
        numer = numer[:, 0:DH] + numer[:, DH:]
        denom = jnp.sum(sig.astype(F32) * norm, axis=1, keepdims=True) + 1.0
        read = numer / denom
        gate = gate_row(gate_ref, h)
        mixed = live * (gate * read + (1.0 - gate) * local_ref[:, cut(h)])
        read_ref[:, cut(h)] = read
        mixed_ref[:, cut(h)] = mixed.astype(BF16)
    if project:
        block = weight_ref[:, columns(z_ref, 2, first_ref.shape[1])]
        first_ref[...] = dot(mixed_ref[...], block, NN).astype(BF16)


def pass_kernel(block_ref, after_ref, out_ref):
    out_ref[...] = block_ref[...]


def token_kernel(*refs):
    refs[-1][...] = jnp.zeros(refs[-1].shape, F32)


def more_kernel(ways, z_ref, *refs):
    grad_refs, (weight_ref, *before, after_ref, total_ref) = refs[: len(ways)], refs[len(ways) :]
    total = before[0][...] if before else None
    for way, grad_ref in zip(ways, grad_refs):
        block = weight_ref[:, columns(z_ref, way, grad_ref.shape[1])]
        part = dot(grad_ref[...], block, NT)
        total = part if total is None else total + part
    total_ref[...] = total


def add_kernel(z_ref, mixed_ref, weight_ref, more_ref, after_ref, out_ref):
    block = weight_ref[:, columns(z_ref, 3, out_ref.shape[1])]
    part = dot(mixed_ref[...], block, NN)
    out_ref[...] = (part + more_ref[...].astype(F32)).astype(BF16)


def rest_kernel(z_ref, mixed_ref, weight_ref, after_ref, near_ref, own_ref):
    cols = own_ref.shape[1]
    near = dot(mixed_ref[...], weight_ref[:, columns(z_ref, 1, cols)], NN)
    near_ref[...] = near.astype(BF16)
    own_ref[...] = dot(mixed_ref[...], weight_ref[:, columns(z_ref, 0, cols)], NN)


def spread_kernel(
    heads, ways, packed, pos_ref, z_ref, valid_ref, starts_ref, gate_ref, q_ref, norm_ref, read_ref, *refs,
):
    if ways:
        parts, (total_ref, weight_ref) = refs[: len(ways)], refs[len(ways) : len(ways) + 2]
        keep_ref, give_ref, numer_ref, denom_ref, grad_ref = refs[-5:]
        total = total_ref[...]
        for way, part_ref in zip(ways, parts):
            block = weight_ref[:, columns(z_ref, way, part_ref.shape[1])]
            total = total + dot(part_ref[...], block, NT)
        grad_ref[...] = total.astype(BF16)
    else:
        grad_ref, keep_ref, give_ref, numer_ref, denom_ref = refs
    live = live_rows(valid_ref, q_ref.shape[0])
    for kept, i, h in by_half(heads, pos_ref):
        sig = feature(q_ref[:, cut(h)].astype(F32)).astype(BF16)
        sig_full = sig.astype(F32)
        denom = jnp.sum(sig_full * norm_ref[h, 0:1, :], axis=1, keepdims=True) + 1.0
        gate = gate_row(gate_ref, h)
        numer_grad = (grad_ref[:, cut(h)].astype(F32) * gate * (live / denom)).astype(BF16)
        denom_grad = -jnp.sum(
            numer_grad.astype(F32) * read_ref[:, cut(h)], axis=1, keepdims=True
        )
        memory = dot(sig, numer_grad, TN)
        norm = jnp.sum(sig_full * denom_grad, axis=0, keepdims=True)
        numer_ref[:, cut(h)] = numer_grad
        denom_ref[h] = denom_grad
        flag = opened(starts_ref)
        if packed and not kept:
            store_sent(give_ref, i, memory, norm, flag, jnp.zeros_like(norm))
        else:
            out_ref = keep_ref if kept else give_ref
            out_ref[i, 0:DH, :] = memory
            out_ref[i, DH:ROWS, :] = tail(ROWS - DH, norm, flag)


def grads_kernel(heads, valid_ref, gate_ref, q_ref, k_ref, v_ref, probs_ref, grad_ref, numer_ref,
                 denom_ref, memory_ref, norm_ref, after_ref, query_ref, key_ref, value_ref):
    length = q_ref.shape[0]
    live = live_rows(valid_ref, length)
    for h in range(heads):
        here = slice(h * DH, (h + 1) * DH)
        q, k, v = head(q_ref, h), head(k_ref, h), head(v_ref, h)
        gate = gate_row(gate_ref, h)
        grad = (head(grad_ref, h).astype(F32) * (1.0 - gate) * live).astype(BF16)
        probs = probs_ref[h]
        probs_grad = dot(grad, v, NT)
        full = probs.astype(F32)
        mean = jnp.sum(full * probs_grad, axis=1, keepdims=True)
        scores_grad = (full * (probs_grad - mean) * DH ** (-0.5)).astype(BF16)
        key_ref[:, here] = dot(scores_grad, q, TN)
        value_ref[:, here] = dot(probs, grad, TN)
        parts = memory_ref[h]
        numer = head(numer_ref, h)
        sig_grad = dot(numer, parts[:, 0:DH], NT) + dot(numer, parts[:, DH:], NT)
        sig_grad = sig_grad + denom_ref[h] * norm_ref[h, 0:1, :]
        total = dot(scores_grad, k, NN) + sig_grad * slope(q.astype(F32))
        query_ref[:, here] = total.astype(BF16)


def last_kernel(heads, pos_ref, valid_ref, k_ref, v_ref, own_ref, far_ref, key_ref, value_ref,
                key_out, value_out):
    live = live_rows(valid_ref, k_ref.shape[0])
    for kept, i, h in by_half(heads, pos_ref):
        memory, norm, _ = load_state(own_ref if kept else far_ref, i)
        top, low = split(memory)
        k, v = k_ref[:, cut(h)].astype(F32), v_ref[:, cut(h)]
        sig = (feature(k) * live).astype(BF16)
        sig_grad = (dot(v, top, NT) + dot(v, low, NT) + norm) * live
        key_out[:, cut(h)] = (key_ref[:, cut(h)] + sig_grad * slope(k)).astype(BF16)
        more = dot(sig, jnp.concatenate([top, low], axis=1), NN)
        value_out[:, cut(h)] = (value_ref[:, cut(h)] + more[:, 0:DH] + more[:, DH:]).astype(BF16)


def weighted(state, forward):
    count, mine = lax.axis_size("seq"), lax.axis_index("seq")
    states = lax.all_gather(state, "seq")
    total = jnp.zeros_like(state)
    weight = jnp.ones((), F32)

    def turn(step, carried):
        total, weight = carried
        at = mine - 1 - step if forward else mine + 1 + step
        inside = (at >= 0) & (at < count)
        one = lax.dynamic_index_in_dim(states, jnp.clip(at, 0, count - 1), keepdims=False)
        opened = one[0, DH + 1, 0]
        here = weight if forward else weight * opened
        total = jnp.where(inside, total + here * one, total)
        return total, weight * opened

    return lax.fori_loop(0, count - 1, turn, (total, weight))[0]


def scan_states(keep, give, pos, heads, forward, before_pair, before_join):
    count = lax.axis_size("seq")
    half = heads // 2
    if count != 8:
        before_pair()
        before_join(keep)
        carry = weighted(jnp.concatenate([keep, give]), forward)
        return carry[:half], carry[half:]
    pairs = [(s, s ^ 1) for s in range(count)]
    other = lax.ppermute(give, "seq", pairs)
    after = before_pair()
    sent = call(
        functools.partial(pair_kernel, heads, forward),
        [jax.ShapeDtypeStruct((half, SENT, DH), BF16)],
        [SMEM, VMEM, VMEM] + [ANY] * len(after),
        [pos, keep, other, *after],
        0.3, "pair",
    )[0]
    arrived = [
        lax.ppermute(sent, "seq", [(s, s ^ way) for s in range(count)]) for way in (6, 2, 4)
    ]
    after = before_join(sent)
    own, passed = call(
        functools.partial(join_kernel, heads, forward),
        [jax.ShapeDtypeStruct((half, ROWS, DH), F32)] * 2,
        [SMEM] + [VMEM] * 5 + [ANY] * len(after),
        [pos, arrived[1], arrived[2], arrived[0], keep, other, *after],
        0.3, "join",
    )
    return own, lax.ppermute(passed, "seq", pairs)


def shards(queries, keys, values, gate, out_weight, out_grad, valid, starts):
    length, width = queries.shape
    heads = width // DH
    cols = out_grad.shape[1]
    groups = lax.axis_size("head")
    direct = groups == 4
    pos = lax.axis_index("seq").astype(jnp.int32).reshape(1)
    paired = lax.axis_size("seq") == 8
    if not paired:
        pos = jnp.zeros_like(pos)
    z = lax.axis_index("head").astype(jnp.int32).reshape(1)
    valid, starts = valid.reshape(1, 1), starts.reshape(1, 1)
    flat = jax.ShapeDtypeStruct((length, width), F32)
    low = jax.ShapeDtypeStruct((length, width), BF16)
    part_low = jax.ShapeDtypeStruct((length, cols), BF16)
    part_full = jax.ShapeDtypeStruct((length, cols), F32)
    states = jax.ShapeDtypeStruct((heads // 2, ROWS, DH), F32)
    packed = jax.ShapeDtypeStruct((heads // 2, SENT, DH), BF16)

    def swap(array, way):
        return lax.ppermute(array, "head", [(s, s ^ way) for s in range(groups)])

    keep, give = call(
        functools.partial(state_kernel, heads), [states] * 2, [SMEM] * 2 + [VMEM] * 4,
        [pos, z, valid, starts, keys, values], 0.4, "state",
    )
    if direct:
        grad_3 = swap(out_grad, 3)
        grad_1 = swap(out_grad, 1)
    kept = {}

    def beside_forward(sent):
        kept["local"] = call(
            functools.partial(local_kernel, heads),
            [jax.ShapeDtypeStruct((heads, length, length), BF16), flat],
            [VMEM] * 4 + [ANY],
            [valid, queries, keys, values, sent], 3, "local",
        )
        return [kept["local"][1]]

    own, far = scan_states(keep, give, pos, heads, True, lambda: [], beside_forward)
    probs, local = kept["local"]
    orders = []
    if direct:
        grad_2 = swap(
            call(pass_kernel, [part_low], [VMEM, ANY], [grad_3, own], 0.1, "pass_on")[0], 1
        )
        orders = call(
            token_kernel, [jax.ShapeDtypeStruct((8, DH), F32)], [ANY] * 2, [grad_1, own],
            3, "arrived",
        )
    outs = call(
        functools.partial(read_kernel, heads, direct),
        [low, flat, jax.ShapeDtypeStruct((heads, DH, 2 * DH), BF16),
         jax.ShapeDtypeStruct((heads, 8, DH), F32)] + [part_low] * direct,
        [SMEM, SMEM, VMEM, SMEM] + [VMEM] * 5 + [VMEM, ANY] * direct,
        [pos, z, valid, gate, queries, keep, own, far, local] + [out_weight, *orders] * direct,
        0.1, "read",
    )
    mixed, read, memory, norm = outs[:4]
    if direct:
        sum_2 = swap(outs[4], 1)
        total = call(
            functools.partial(more_kernel, (0, 1, 3)), [flat], [SMEM] + [VMEM] * 4 + [ANY],
            [z, out_grad, grad_1, grad_3, out_weight, mixed], 0.1, "unproject_more",
        )[0]
        near, mine = call(
            rest_kernel, [part_low, part_full], [SMEM, VMEM, VMEM, ANY],
            [z, mixed, out_weight, total], 0.1, "project_rest",
        )
        kept["from_1"] = swap(near, 1)
        grads_in = [grad_2, total, out_weight]
        orders = [near]
    else:
        part = dot(mixed, out_weight, NN)
        output = lax.psum_scatter(part, "head", scatter_dimension=1, tiled=True).astype(BF16)
        whole = lax.all_gather(out_grad, "head", axis=1, tiled=True)
        grads_in = [dot(whole, out_weight, NT).astype(BF16)]
        orders = []
    outs = call(
        functools.partial(spread_kernel, heads, (2,) * direct, paired),
        [states, packed if paired else states, low,
         jax.ShapeDtypeStruct((heads, length, 1), F32)] + [low] * direct,
        [SMEM, SMEM, VMEM, VMEM, SMEM] + [VMEM] * (3 + len(grads_in)) + [ANY] * len(orders),
        [pos, z, valid, starts, gate, queries, norm, read, *grads_in, *orders],
        0.5, "spread",
    )
    keep, give, numer_grad, denom_grad = outs[:4]
    mixed_grad = outs[4] if direct else grads_in[0]

    def add_here():
        if not direct:
            return []
        sum_3 = call(
            add_kernel, [part_low], [SMEM, VMEM, VMEM, VMEM, ANY],
            [z, mixed, out_weight, sum_2, numer_grad], 0.5, "project_add",
        )[0]
        kept["from_3"] = swap(sum_3, 3)
        return [sum_3]

    def beside_back(sent):
        kept["grads"] = call(
            functools.partial(grads_kernel, heads),
            [low, flat, flat],
            [VMEM, SMEM] + [VMEM] * 9 + [ANY],
            [valid, gate, queries, keys, values, probs, mixed_grad, numer_grad, denom_grad, memory,
             norm, sent],
            0.3, "grads",
        )
        return [kept["grads"][1]] + ([kept["from_1"]] if direct else [])

    own, far = scan_states(keep, give, pos, heads, False, add_here, beside_back)
    query_grad, key_part, value_part = kept["grads"]
    if direct:
        output = mine + kept["from_1"].astype(F32) + kept["from_3"].astype(F32)
        output = output.astype(BF16)
    key_grad, value_grad = call(
        functools.partial(last_kernel, heads),
        [low, low],
        [SMEM] + [VMEM] * 7,
        [pos, valid, keys, values, own, far, key_part, value_part], 1.5, "last",
    )
    return (output, query_grad, key_grad, value_grad)


def solution(mesh):
    placed = (
        P("seq", "head"),
        P("seq", "head"),
        P("seq", "head"),
        P("head"),
        P("head", None),
        P("seq", "head"),
        P("seq"),
        P("seq"),
    )
    return jax.shard_map(
        shards,
        mesh=mesh,
        in_specs=placed,
        out_specs=(P("seq", "head"), P("seq", "head"), P("seq", "head"), P("seq", "head")),
        check_vma=False,
    )
```

```python
import functools

import jax
import jax.numpy as jnp
from jax import lax
from jax.experimental import pallas as pl
from jax.experimental.pallas import tpu as pltpu
from jax.sharding import NamedSharding
from jax.sharding import PartitionSpec as P

DH = 128
ROWS = 136
SENT = 144
BF16 = jnp.bfloat16
F32 = jnp.float32
VMEM = pl.BlockSpec(memory_space=pltpu.VMEM)
SMEM = pl.BlockSpec(memory_space=pltpu.SMEM)


ANY = pl.BlockSpec(memory_space=pl.ANY)


def call(kernel, outs, in_specs, args, micros, name):
    return pl.pallas_call(
        kernel,
        out_shape=outs,
        in_specs=in_specs,
        out_specs=[VMEM] * len(outs),
        compiler_params=pltpu.CompilerParams(vmem_limit_bytes=24 * 1024 * 1024),
        cost_estimate=pl.CostEstimate(flops=int(micros * 1.15e9), bytes_accessed=1024, transcendentals=0),
        name=name,
    )(*args)


def feature(x):
    return jnp.where(x > 0, x + 1.0, jnp.exp(jnp.minimum(x, 0.0)))


def slope(x):
    return jnp.where(x > 0, 1.0, jnp.where(x == 0, 0.5, jnp.exp(jnp.minimum(x, 0.0))))


def sigmoid(x):
    return 1.0 / (1.0 + jnp.exp(-x))


def dot(a, b, dims):
    return lax.dot_general(a, b, (dims, ((), ())), preferred_element_type=F32)


NN = ((1,), (0,))
NT = ((1,), (1,))
TN = ((0,), (0,))


def live_rows(facts_ref, length):
    where = lax.broadcasted_iota(jnp.int32, (length, 1), 0)
    return (where.astype(F32) < facts_ref[0:1, 0:1]).astype(F32)


def opened(facts_ref):
    return 1.0 - facts_ref[4:5, 0:1]


def gate_row(gate_ref, h):
    return sigmoid(jnp.full((1, DH), gate_ref[h], F32))


def head(ref, h):
    return ref[:, h * DH : (h + 1) * DH]


def tail(rows, *values):
    where = lax.broadcasted_iota(jnp.int32, (rows, DH), 0)
    out = jnp.zeros((rows, DH), F32)
    for at, value in enumerate(values):
        out = jnp.where(where == at, value, out)
    return out


def split(x):
    top = x.astype(BF16)
    rest = x - top.astype(F32)
    return top, rest.astype(BF16)


def cut(h):
    return pl.ds(h * DH if isinstance(h, int) else pl.multiple_of(h * DH, DH), DH)


def by_half(heads, pos_ref):
    half = lax.rem(pos_ref[0], 2)
    count = heads // 2
    for kept, first in ((True, half * count), (False, (1 - half) * count)):
        for i in range(count):
            yield kept, i, first + i


def state_kernel(
    heads, pos_ref, z_ref, facts_ref, k_ref, v_ref, after_ref, keep_ref, give_ref
):
    live = live_rows(facts_ref, k_ref.shape[0])
    for kept, i, h in by_half(heads, pos_ref):
        out_ref = keep_ref if kept else give_ref
        sig = (feature(k_ref[:, cut(h)].astype(F32)) * live).astype(BF16)
        out_ref[i, 0:DH, :] = dot(sig, v_ref[:, cut(h)], TN)
        norm = jnp.sum(sig.astype(F32), axis=0, keepdims=True)
        out_ref[i, DH:ROWS, :] = tail(ROWS - DH, norm, opened(facts_ref))


def in_three(x):
    first = x.astype(BF16).astype(F32)
    second = (x - first).astype(BF16).astype(F32)
    return first, second, x - first - second


def store_sent(ref, i, memory, norm, flag, centred):
    centre = jnp.zeros_like(norm)
    if centred:
        weight = jnp.maximum(jnp.sum(norm, axis=1, keepdims=True), 1e-30)
        centre = jnp.sum(memory, axis=0, keepdims=True) / weight
        centre = centre.astype(BF16).astype(F32)
        norms = tail(16, *in_three(norm)).astype(BF16)
        centres = tail(16, centre, centre, centre).astype(BF16)
        memory = memory - dot(norms, centres, TN)
    ref[i, 0:DH, :] = memory.astype(BF16)
    ref[i, DH:SENT, :] = tail(SENT - DH, *in_three(norm), centre, flag).astype(BF16)


def load_sent(ref, i, centred):
    memory = ref[i, 0:DH, :].astype(F32)
    rows = ref[i, DH:SENT, :].astype(F32)
    if centred:
        norms = tail(16, rows[0:1], rows[1:2], rows[2:3]).astype(BF16)
        centres = tail(16, rows[3:4], rows[3:4], rows[3:4]).astype(BF16)
        memory = memory + dot(norms, centres, TN)
    return memory, rows[0:1] + rows[1:2] + rows[2:3], rows[4:5]


def load_state(ref, i):
    return ref[i, 0:DH, :], ref[i, DH : DH + 1, :], ref[i, DH + 1 : DH + 2, :]


def load_other(ref, i, forward):
    return load_state(ref, i) if forward else load_sent(ref, i, False)


def pair_kernel(heads, forward, pos_ref, keep_ref, other_ref, *refs):
    sent_ref = refs[-1]
    lower = lax.rem(pos_ref[0], 2) == 0
    for i in range(heads // 2):
        memory, norm, flag = load_state(keep_ref, i)
        other_memory, other_norm, other_flag = load_other(other_ref, i, forward)
        one = jnp.ones_like(flag)
        if forward:
            on_mine = jnp.where(lower, other_flag, one)
            on_other = jnp.where(lower, one, flag)
        else:
            on_mine = jnp.where(lower, flag, flag * other_flag)
            on_other = jnp.where(lower, flag * other_flag, other_flag)
        memory = on_mine * memory + on_other * other_memory
        norm = on_mine * norm + on_other * other_norm
        store_sent(sent_ref, i, memory, norm, flag * other_flag, forward)


def join_kernel(
    heads, forward, pos_ref, x_ref, y_ref, d_ref, keep_ref, other_ref, *refs
):
    own_ref, sent_ref = refs[-2:]
    lower = lax.rem(pos_ref[0], 2) == 0
    chip = pos_ref[0] // 2
    place = chip if forward else 3 - chip
    odd, high = lax.rem(place, 2) == 1, place >= 2
    for i in range(heads // 2):
        x_mem, x_norm, x_open = load_sent(x_ref, i, forward)
        y_mem, y_norm, y_open = load_sent(y_ref, i, forward)
        d_mem, d_norm, d_open = load_sent(d_ref, i, forward)
        on_x = jnp.where(odd, jnp.ones_like(x_open), 0.0)
        on_y = jnp.where(high, jnp.where(odd, x_open, d_open), 0.0)
        on_d = jnp.where(high, jnp.where(odd, x_open * y_open, 1.0), 0.0)
        memory = on_x * x_mem + on_y * y_mem + on_d * d_mem
        norm = on_x * x_norm + on_y * y_norm + on_d * d_norm
        mine_mem, mine_norm, mine_open = load_state(keep_ref, i)
        other_mem, other_norm, other_open = load_other(other_ref, i, forward)
        if forward:
            own = (
                jnp.where(lower, memory, other_open * memory + other_mem),
                jnp.where(lower, norm, other_open * norm + other_norm),
            )
            sent = (
                jnp.where(lower, mine_open * memory + mine_mem, memory),
                jnp.where(lower, mine_open * norm + mine_norm, norm),
            )
        else:
            own = (
                jnp.where(lower, other_open * (memory + other_mem), memory),
                jnp.where(lower, other_open * (norm + other_norm), norm),
            )
            sent = (
                jnp.where(lower, memory, mine_open * (memory + mine_mem)),
                jnp.where(lower, norm, mine_open * (norm + mine_norm)),
            )
        own_ref[i, 0:DH, :] = own[0]
        own_ref[i, DH:ROWS, :] = tail(ROWS - DH, own[1])
        if forward:
            sent_ref[i, 0:DH, :] = sent[0]
            sent_ref[i, DH:ROWS, :] = tail(ROWS - DH, sent[1])
        else:
            store_sent(sent_ref, i, *sent, mine_open, False)


def local_kernel(heads, facts_ref, q_ref, k_ref, v_ref, after_ref, probs_ref, local_ref):
    length = q_ref.shape[0]
    row = lax.broadcasted_iota(jnp.int32, (length, length), 0)
    col = lax.broadcasted_iota(jnp.int32, (length, length), 1)
    allowed = (col <= row) & (col.astype(F32) < facts_ref[0:1, 0:1])
    for h in range(heads):
        scores = dot(head(q_ref, h), head(k_ref, h), NT) * DH ** (-0.5)
        scores = jnp.where(allowed, scores, -1e30)
        expo = jnp.exp(scores - jnp.max(scores, axis=1, keepdims=True))
        probs = (expo / jnp.sum(expo, axis=1, keepdims=True)).astype(BF16)
        probs_ref[h] = probs
        local_ref[:, h * DH : (h + 1) * DH] = dot(probs, head(v_ref, h), NN)


def columns(z_ref, way, cols):
    return pl.ds(pl.multiple_of((z_ref[0] ^ way) * cols, DH), cols)


def read_kernel(
    heads, project, pos_ref, z_ref, facts_ref, gate_ref, q_ref, keep_ref, own_ref, far_ref,
    local_ref, *refs,
):
    if project:
        weight_ref, _, mixed_ref, read_ref, memory_ref, norm_ref, sig_ref, scale_ref, first_ref = refs
    else:
        mixed_ref, read_ref, memory_ref, norm_ref, sig_ref, scale_ref = refs
    live = live_rows(facts_ref, q_ref.shape[0])
    for kept, i, h in by_half(heads, pos_ref):
        carry, norm, _ = load_state(own_ref if kept else far_ref, i)
        flag = keep_ref[i, DH + 1 : DH + 2, :]
        norm = flag * norm
        parts = jnp.concatenate(split(flag * carry), axis=1)
        memory_ref[h] = parts
        norm_ref[h] = jnp.broadcast_to(norm, (8, DH))
        sig = feature(q_ref[:, cut(h)].astype(F32)).astype(BF16)
        numer = dot(sig, parts, NN)
        numer = numer[:, 0:DH] + numer[:, DH:]
        denom = jnp.sum(sig.astype(F32) * norm, axis=1, keepdims=True) + 1.0
        read = numer / denom
        gate = gate_row(gate_ref, h)
        mixed = live * (gate * read + (1.0 - gate) * local_ref[:, cut(h)])
        sig_ref[:, cut(h)] = sig
        scale_ref[h] = live * gate[:, 0:1] / denom
        read_ref[:, cut(h)] = read
        mixed_ref[:, cut(h)] = mixed.astype(BF16)
    if project:
        block = weight_ref[:, columns(z_ref, 2, first_ref.shape[1])]
        first_ref[...] = dot(mixed_ref[...], block, NN).astype(BF16)


def pass_kernel(block_ref, after_ref, out_ref):
    out_ref[...] = block_ref[...]


def token_kernel(*refs):
    refs[-1][...] = jnp.zeros(refs[-1].shape, F32)


def more_kernel(ways, z_ref, *refs):
    grad_refs, (weight_ref, *before, after_ref, total_ref) = refs[: len(ways)], refs[len(ways) :]
    total = before[0][...] if before else None
    for way, grad_ref in zip(ways, grad_refs):
        block = weight_ref[:, columns(z_ref, way, grad_ref.shape[1])]
        part = dot(grad_ref[...], block, NT)
        total = part if total is None else total + part
    total_ref[...] = total


def add_kernel(z_ref, mixed_ref, weight_ref, more_ref, after_ref, out_ref):
    block = weight_ref[:, columns(z_ref, 3, out_ref.shape[1])]
    part = dot(mixed_ref[...], block, NN)
    out_ref[...] = (part + more_ref[...].astype(F32)).astype(BF16)


def rest_kernel(z_ref, mixed_ref, weight_ref, after_ref, near_ref, own_ref):
    cols = own_ref.shape[1]
    near = dot(mixed_ref[...], weight_ref[:, columns(z_ref, 1, cols)], NN)
    near_ref[...] = near.astype(BF16)
    own_ref[...] = dot(mixed_ref[...], weight_ref[:, columns(z_ref, 0, cols)], NN)


def spread_kernel(
    heads, ways, packed, pos_ref, z_ref, facts_ref, sig_ref, scale_ref, read_ref, *refs,
):
    if ways:
        parts, (total_ref, weight_ref) = refs[: len(ways)], refs[len(ways) : len(ways) + 2]
        keep_ref, give_ref, numer_ref, denom_ref, grad_ref = refs[-5:]
        total = total_ref[...]
        for way, part_ref in zip(ways, parts):
            block = weight_ref[:, columns(z_ref, way, part_ref.shape[1])]
            total = total + dot(part_ref[...], block, NT)
        grad_ref[...] = total.astype(BF16)
    else:
        grad_ref, keep_ref, give_ref, numer_ref, denom_ref = refs
    for kept, i, h in by_half(heads, pos_ref):
        sig = sig_ref[:, cut(h)]
        numer_grad = (grad_ref[:, cut(h)].astype(F32) * scale_ref[h]).astype(BF16)
        denom_grad = -jnp.sum(
            numer_grad.astype(F32) * read_ref[:, cut(h)], axis=1, keepdims=True
        )
        memory = dot(sig, numer_grad, TN)
        norm = jnp.sum(sig.astype(F32) * denom_grad, axis=0, keepdims=True)
        numer_ref[:, cut(h)] = numer_grad
        denom_ref[h] = denom_grad
        flag = opened(facts_ref)
        if packed and not kept:
            store_sent(give_ref, i, memory, norm, flag, False)
        else:
            out_ref = keep_ref if kept else give_ref
            out_ref[i, 0:DH, :] = memory
            out_ref[i, DH:ROWS, :] = tail(ROWS - DH, norm, flag)


def grads_kernel(heads, facts_ref, gate_ref, q_ref, k_ref, v_ref, probs_ref, grad_ref, numer_ref,
                 denom_ref, memory_ref, norm_ref, *refs):
    query_ref, key_ref, value_ref = refs[-3:]
    length = q_ref.shape[0]
    live = live_rows(facts_ref, length)
    for h in range(heads):
        here = slice(h * DH, (h + 1) * DH)
        q, k, v = head(q_ref, h), head(k_ref, h), head(v_ref, h)
        gate = gate_row(gate_ref, h)
        grad = (head(grad_ref, h).astype(F32) * (1.0 - gate) * live).astype(BF16)
        probs = probs_ref[h]
        probs_grad = dot(grad, v, NT)
        full = probs.astype(F32)
        mean = jnp.sum(full * probs_grad, axis=1, keepdims=True)
        scores_grad = (full * (probs_grad - mean) * DH ** (-0.5)).astype(BF16)
        key_ref[:, here] = dot(scores_grad, q, TN)
        value_ref[:, here] = dot(probs, grad, TN)
        parts = memory_ref[h]
        numer = head(numer_ref, h)
        sig_grad = dot(numer, parts[:, 0:DH], NT) + dot(numer, parts[:, DH:], NT)
        sig_grad = sig_grad + denom_ref[h] * norm_ref[h, 0:1, :]
        total = dot(scores_grad, k, NN) + sig_grad * slope(q.astype(F32))
        query_ref[:, here] = total.astype(BF16)


def last_kernel(heads, packed, pos_ref, facts_ref, k_ref, v_ref, own_ref, far_ref, key_ref, value_ref,
                *refs):
    key_out, value_out = refs[-2:]
    live = live_rows(facts_ref, k_ref.shape[0])
    for kept, i, h in by_half(heads, pos_ref):
        if kept or not packed:
            memory, norm, _ = load_state(own_ref if kept else far_ref, i)
        else:
            memory, norm, _ = load_sent(far_ref, i, False)
        top, low = split(memory)
        k, v = k_ref[:, cut(h)].astype(F32), v_ref[:, cut(h)]
        sig = (feature(k) * live).astype(BF16)
        sig_grad = (dot(v, top, NT) + dot(v, low, NT) + norm) * live
        key_out[:, cut(h)] = (key_ref[:, cut(h)] + sig_grad * slope(k)).astype(BF16)
        more = dot(sig, jnp.concatenate([top, low], axis=1), NN)
        value_out[:, cut(h)] = (value_ref[:, cut(h)] + more[:, 0:DH] + more[:, DH:]).astype(BF16)


def weighted(state, forward):
    count, mine = lax.axis_size("seq"), lax.axis_index("seq")
    states = lax.all_gather(state, "seq")
    total = jnp.zeros_like(state)
    weight = jnp.ones((), F32)

    def turn(step, carried):
        total, weight = carried
        at = mine - 1 - step if forward else mine + 1 + step
        inside = (at >= 0) & (at < count)
        one = lax.dynamic_index_in_dim(states, jnp.clip(at, 0, count - 1), keepdims=False)
        opened = one[0, DH + 1, 0]
        here = weight if forward else weight * opened
        total = jnp.where(inside, total + here * one, total)
        return total, weight * opened

    return lax.fori_loop(0, count - 1, turn, (total, weight))[0]


def scan_states(keep, give, pos, heads, forward, before_pair, before_join):
    count = lax.axis_size("seq")
    half = heads // 2
    if count != 8:
        before_pair()
        before_join(keep)
        carry = weighted(jnp.concatenate([keep, give]), forward)
        return carry[:half], carry[half:]
    pairs = [(s, s ^ 1) for s in range(count)]
    other = lax.ppermute(give, "seq", pairs)
    after = before_pair()
    sent = call(
        functools.partial(pair_kernel, heads, forward),
        [jax.ShapeDtypeStruct((half, SENT, DH), BF16)],
        [SMEM, VMEM, VMEM] + [ANY] * len(after),
        [pos, keep, other, *after],
        0.01, "pair",
    )[0]
    arrived = [
        lax.ppermute(sent, "seq", [(s, s ^ way) for s in range(count)]) for way in (6, 2, 4)
    ]
    after = before_join(sent)
    own, passed = call(
        functools.partial(join_kernel, heads, forward),
        [jax.ShapeDtypeStruct((half, ROWS, DH), F32),
         jax.ShapeDtypeStruct((half, ROWS, DH), F32) if forward
         else jax.ShapeDtypeStruct((half, SENT, DH), BF16)],
        [SMEM] + [VMEM] * 5 + [ANY] * len(after),
        [pos, arrived[1], arrived[2], arrived[0], keep, other, *after],
        0.3, "join",
    )
    return own, lax.ppermute(passed, "seq", pairs)


def shards(queries, keys, values, gate, out_weight, out_grad, facts):
    length, width = queries.shape
    heads = width // DH
    cols = out_grad.shape[1]
    groups = lax.axis_size("head")
    direct = groups == 4
    pos = lax.axis_index("seq").astype(jnp.int32).reshape(1)
    paired = lax.axis_size("seq") == 8
    if not paired:
        pos = jnp.zeros_like(pos)
    z = lax.axis_index("head").astype(jnp.int32).reshape(1)
    facts = facts[0]
    flat = jax.ShapeDtypeStruct((length, width), F32)
    low = jax.ShapeDtypeStruct((length, width), BF16)
    part_low = jax.ShapeDtypeStruct((length, cols), BF16)
    part_full = jax.ShapeDtypeStruct((length, cols), F32)
    states = jax.ShapeDtypeStruct((heads // 2, ROWS, DH), F32)
    packed = jax.ShapeDtypeStruct((heads // 2, SENT, DH), BF16)
    column = jax.ShapeDtypeStruct((heads, length, 1), F32)

    def swap(array, way):
        return lax.ppermute(array, "head", [(s, s ^ way) for s in range(groups)])

    first = call(token_kernel, [jax.ShapeDtypeStruct((8, DH), F32)], [VMEM], [facts], 10, "warm")
    keep, give = call(
        functools.partial(state_kernel, heads), [states] * 2, [SMEM] * 2 + [VMEM] * 3 + [ANY],
        [pos, z, facts, keys, values, *first], 0.4, "state",
    )
    if direct:
        grad_3 = swap(out_grad, 3)
        grad_1 = swap(out_grad, 1)
    kept = {}

    def beside_forward(sent):
        kept["local"] = call(
            functools.partial(local_kernel, heads),
            [jax.ShapeDtypeStruct((heads, length, length), BF16), flat],
            [VMEM] * 4 + [ANY],
            [facts, queries, keys, values, sent], 0.1, "local",
        )
        if not direct:
            return [kept["local"][1]]
        kept["total"] = call(
            functools.partial(more_kernel, (0,)), [flat], [SMEM] + [VMEM] * 2 + [ANY],
            [z, out_grad, out_weight, kept["local"][1]], 0.8, "unproject_own",
        )[0]
        return [kept["total"]]

    own, far = scan_states(keep, give, pos, heads, True, lambda: [], beside_forward)
    probs, local = kept["local"]
    orders = []
    if direct:
        orders = call(
            token_kernel, [jax.ShapeDtypeStruct((8, DH), F32)], [ANY] * 2, [grad_1, own],
            3, "arrived",
        )
        grad_2 = swap(
            call(pass_kernel, [part_low], [VMEM, ANY], [grad_3, own], 0.1, "pass_on")[0], 1
        )
    outs = call(
        functools.partial(read_kernel, heads, direct),
        [low, flat, jax.ShapeDtypeStruct((heads, DH, 2 * DH), BF16),
         jax.ShapeDtypeStruct((heads, 8, DH), F32), low, column] + [part_low] * direct,
        [SMEM, SMEM, VMEM, SMEM] + [VMEM] * 5 + [VMEM, ANY] * direct,
        [pos, z, facts, gate, queries, keep, own, far, local] + [out_weight, *orders] * direct,
        0.01, "read",
    )
    mixed, read, memory, norm, sig, scale = outs[:6]
    if direct:
        sum_2 = swap(outs[6], 1)
        total = call(
            functools.partial(more_kernel, (1, 3)), [flat], [SMEM] + [VMEM] * 4 + [ANY],
            [z, grad_1, grad_3, out_weight, kept["total"], mixed], 0.01, "unproject_more",
        )[0]
        near, mine = call(
            rest_kernel, [part_low, part_full], [SMEM, VMEM, VMEM, ANY],
            [z, mixed, out_weight, total], 0.01, "project_rest",
        )
        kept["from_1"] = swap(near, 1)
        grads_in = [grad_2, total, out_weight]
        orders = [near]
    else:
        part = dot(mixed, out_weight, NN)
        output = lax.psum_scatter(part, "head", scatter_dimension=1, tiled=True).astype(BF16)
        whole = lax.all_gather(out_grad, "head", axis=1, tiled=True)
        grads_in = [dot(whole, out_weight, NT).astype(BF16)]
        orders = []
    outs = call(
        functools.partial(spread_kernel, heads, (2,) * direct, paired),
        [states, packed if paired else states, low,
         column] + [low] * direct,
        [SMEM, SMEM] + [VMEM] * (4 + len(grads_in)) + [ANY] * len(orders),
        [pos, z, facts, sig, scale, read, *grads_in, *orders],
        0.01, "spread",
    )
    keep, give, numer_grad, denom_grad = outs[:4]
    mixed_grad = outs[4] if direct else grads_in[0]

    def beside_back(sent):
        after = [sent]
        if direct:
            after = call(
                add_kernel, [part_low], [SMEM, VMEM, VMEM, VMEM, ANY],
                [z, mixed, out_weight, sum_2, sent], 0.01, "project_add",
            )
            kept["from_3"] = swap(after[0], 3)
        kept["grads"] = call(
            functools.partial(grads_kernel, heads),
            [low, flat, flat],
            [VMEM, SMEM] + [VMEM] * 9 + [ANY] * len(after),
            [facts, gate, queries, keys, values, probs, mixed_grad, numer_grad, denom_grad, memory,
             norm, *after],
            0.01, "grads",
        )
        if not direct:
            return [kept["grads"][1]]
        return call(
            token_kernel, [jax.ShapeDtypeStruct((8, DH), F32)], [ANY] * 2,
            [kept["from_1"], kept["grads"][1]], 1.5, "settled",
        )

    own, far = scan_states(keep, give, pos, heads, False, lambda: [], beside_back)
    query_grad, key_part, value_part = kept["grads"]
    if direct:
        output = mine + kept["from_1"].astype(F32) + kept["from_3"].astype(F32)
        output = output.astype(BF16)
    key_grad, value_grad = call(
        functools.partial(last_kernel, heads, paired),
        [low, low],
        [SMEM] + [VMEM] * 7,
        [pos, facts, keys, values, own, far, key_part, value_part],
        0.01, "last",
    )
    return (output, query_grad, key_grad, value_grad)


def solution(mesh):
    tokens = P("seq", "head")
    placed = (tokens, tokens, tokens, P("head"), P("head", None), tokens, P("seq", None, None))
    parts = jax.shard_map(
        shards, mesh=mesh, in_specs=placed, out_specs=(tokens,) * 4, check_vma=False
    )

    def whole(queries, keys, values, gate, out_weight, out_grad, valid, starts):
        row = lax.broadcasted_iota(jnp.int32, (valid.shape[0], 8, DH), 1)
        facts = jnp.where(row < 4, valid[:, None, None], starts[:, None, None]).astype(F32)
        facts = lax.with_sharding_constraint(facts, NamedSharding(mesh, placed[-1]))
        return parts(queries, keys, values, gate, out_weight, out_grad, facts)

    return whole
```

```python
import functools

import jax
import jax.numpy as jnp
from jax import lax
from jax.experimental import pallas as pl
from jax.experimental.pallas import tpu as pltpu
from jax.sharding import NamedSharding
from jax.sharding import PartitionSpec as P

DH = 128
ROWS = 136
TAIL = 16
BF16 = jnp.bfloat16
F32 = jnp.float32
VMEM = pl.BlockSpec(memory_space=pltpu.VMEM)
SMEM = pl.BlockSpec(memory_space=pltpu.SMEM)


ANY = pl.BlockSpec(memory_space=pl.ANY)


def call(kernel, outs, in_specs, args, micros, name):
    return pl.pallas_call(
        kernel,
        out_shape=outs,
        in_specs=in_specs,
        out_specs=[VMEM] * len(outs),
        compiler_params=pltpu.CompilerParams(vmem_limit_bytes=24 * 1024 * 1024),
        cost_estimate=pl.CostEstimate(flops=int(micros * 1.15e9), bytes_accessed=1024, transcendentals=0),
        name=name,
    )(*args)


def feature(x):
    return jnp.where(x > 0, x + 1.0, jnp.exp(jnp.minimum(x, 0.0)))


def slope(x):
    return jnp.where(x > 0, 1.0, jnp.where(x == 0, 0.5, jnp.exp(jnp.minimum(x, 0.0))))


def sigmoid(x):
    return 1.0 / (1.0 + jnp.exp(-x))


def dot(a, b, dims):
    return lax.dot_general(a, b, (dims, ((), ())), preferred_element_type=F32)


NN = ((1,), (0,))
NT = ((1,), (1,))
TN = ((0,), (0,))


def live_rows(facts_ref, length):
    where = lax.broadcasted_iota(jnp.int32, (length, 1), 0)
    return (where.astype(F32) < facts_ref[0:1, 0:1]).astype(F32)


def opened(facts_ref):
    return 1.0 - facts_ref[4:5, 0:1]


def gate_row(gate_ref, h):
    return sigmoid(jnp.full((1, DH), gate_ref[h], F32))


def head(ref, h):
    return ref[:, h * DH : (h + 1) * DH]


def tail(rows, *values):
    where = lax.broadcasted_iota(jnp.int32, (rows, DH), 0)
    out = jnp.zeros((rows, DH), F32)
    for at, value in enumerate(values):
        out = jnp.where(where == at, value, out)
    return out


def split(x):
    top = x.astype(BF16)
    rest = x - top.astype(F32)
    return top, rest.astype(BF16)


def cut(h):
    return pl.ds(h * DH if isinstance(h, int) else pl.multiple_of(h * DH, DH), DH)


def by_half(heads, pos_ref):
    half = lax.rem(pos_ref[0], 2)
    count = heads // 2
    for kept, first in ((True, half * count), (False, (1 - half) * count)):
        for i in range(count):
            yield kept, i, first + i


def pack(ref, states, flag, centred):
    count = len(states)
    norms = [split(norm) for _, norm in states]
    centres = [jnp.zeros_like(norm) for _, norm in states]
    memories = [memory for memory, _ in states]
    if centred:
        sums = [jnp.sum(memory, axis=0, keepdims=True) for memory in memories]
        weights = [jnp.sum(norm, axis=1, keepdims=True) for _, norm in states]
        centres = [a / jnp.maximum(b, 1e-30) for a, b in zip(sums, weights)]
        centres = [centre.astype(BF16).astype(F32) for centre in centres]
        outers = [outer(*norm, centre) for norm, centre in zip(norms, centres)]
        memories = [memory - less for memory, less in zip(memories, outers)]
    for i, memory in enumerate(memories):
        ref[i * DH : (i + 1) * DH, :] = memory.astype(BF16)
    tops, lows = zip(*norms)
    rows = tail(TAIL, *[x.astype(F32) for x in tops + lows], *centres, flag)
    ref[count * DH : count * DH + TAIL, :] = rows.astype(BF16)


def pack_parts(refs, states, flag, centred):
    share = len(states) // len(refs)
    for at, ref in enumerate(refs):
        pack(ref, states[at * share : (at + 1) * share], flag, centred)


def outer(top, low, centre):
    norms = tail(TAIL, top.astype(F32), low.astype(F32)).astype(BF16)
    return dot(norms, tail(TAIL, centre, centre).astype(BF16), TN)


def unpack(ref, centred):
    count = ref.shape[0] // DH
    rows = ref[count * DH : count * DH + TAIL, :].astype(F32)
    row = [rows[i : i + 1] for i in range(3 * count + 1)]
    states = []
    for i in range(count):
        memory = ref[i * DH : (i + 1) * DH, :].astype(F32)
        if centred:
            memory = memory + outer(row[i], row[count + i], row[2 * count + i])
        states.append((memory, row[i] + row[count + i]))
    return states, row[3 * count]


def load_states(ref):
    states = [(ref[i, 0:DH, :], ref[i, DH : DH + 1, :]) for i in range(ref.shape[0])]
    return states, ref[0, DH + 1 : DH + 2, :]


def store_states(ref, states, flag):
    for i, (memory, norm) in enumerate(states):
        ref[i, 0:DH, :] = memory
        ref[i, DH:ROWS, :] = tail(ROWS - DH, norm, flag)


def scaled(scale, state):
    return scale * state[0], scale * state[1]


def added(*states):
    return sum(memory for memory, _ in states), sum(norm for _, norm in states)


def chosen(which, yes, no):
    return jnp.where(which, yes[0], no[0]), jnp.where(which, yes[1], no[1])


def state_kernel(heads, packed, pos_ref, z_ref, facts_ref, k_ref, v_ref, after_ref, *refs):
    live = live_rows(facts_ref, k_ref.shape[0])
    kept, given = [], []
    for mine, i, h in by_half(heads, pos_ref):
        sig = (feature(k_ref[:, cut(h)].astype(F32)) * live).astype(BF16)
        memory = dot(sig, v_ref[:, cut(h)], TN)
        norm = jnp.sum(sig.astype(F32), axis=0, keepdims=True)
        (kept if mine else given).append((memory, norm))
    flag = jnp.broadcast_to(opened(facts_ref), (1, DH))
    store_states(refs[0], kept, flag)
    if packed:
        pack_parts(refs[1:], given, flag, True)
    else:
        store_states(refs[1], given, flag)


def load_others(refs, forward):
    states = []
    for ref in refs:
        part, flag = unpack(ref, forward)
        states += part
    return states, flag


def pair_kernel(heads, forward, count, pos_ref, keep_ref, *refs):
    sent_ref = refs[-1]
    lower = lax.rem(pos_ref[0], 2) == 0
    mine, flag = load_states(keep_ref)
    others, other_flag = load_others(refs[:count], forward)
    one = jnp.ones_like(flag)
    if forward:
        on_mine = jnp.where(lower, other_flag, one)
        on_other = jnp.where(lower, one, flag)
    else:
        on_mine = jnp.where(lower, flag, flag * other_flag)
        on_other = jnp.where(lower, flag * other_flag, other_flag)
    totals = [added(scaled(on_mine, a), scaled(on_other, b)) for a, b in zip(mine, others)]
    pack(sent_ref, totals, flag * other_flag, forward)


def join_kernel(heads, forward, count, parts, pos_ref, x_ref, y_ref, d_ref, keep_ref, *refs):
    own_ref, *sent_refs = refs[-1 - parts :]
    lower = lax.rem(pos_ref[0], 2) == 0
    chip = pos_ref[0] // 2
    place = chip if forward else 3 - chip
    odd, high = lax.rem(place, 2) == 1, place >= 2
    xs, x_open = unpack(x_ref, forward)
    ys, y_open = unpack(y_ref, forward)
    ds, d_open = unpack(d_ref, forward)
    on_x = jnp.where(odd, jnp.ones_like(x_open), 0.0)
    on_y = jnp.where(high, jnp.where(odd, x_open, d_open), 0.0)
    on_d = jnp.where(high, jnp.where(odd, x_open * y_open, 1.0), 0.0)
    mines, mine_open = load_states(keep_ref)
    others, other_open = load_others(refs[:count], forward)
    own, sent = [], []
    for x, y, d, mine, other in zip(xs, ys, ds, mines, others):
        carry = added(scaled(on_x, x), scaled(on_y, y), scaled(on_d, d))
        if forward:
            own.append(chosen(lower, carry, added(scaled(other_open, carry), other)))
            sent.append(chosen(lower, added(scaled(mine_open, carry), mine), carry))
        else:
            own.append(chosen(lower, scaled(other_open, added(carry, other)), carry))
            sent.append(chosen(lower, carry, scaled(mine_open, added(carry, mine))))
    store_states(own_ref, own, mine_open)
    pack_parts(sent_refs, sent, mine_open, forward)


def local_kernel(heads, facts_ref, q_ref, k_ref, v_ref, after_ref, probs_ref, local_ref):
    length = q_ref.shape[0]
    row = lax.broadcasted_iota(jnp.int32, (length, length), 0)
    col = lax.broadcasted_iota(jnp.int32, (length, length), 1)
    allowed = (col <= row) & (col.astype(F32) < facts_ref[0:1, 0:1])
    for h in range(heads):
        scores = dot(head(q_ref, h), head(k_ref, h), NT) * DH ** (-0.5)
        scores = jnp.where(allowed, scores, -1e30)
        expo = jnp.exp(scores - jnp.max(scores, axis=1, keepdims=True))
        probs = (expo / jnp.sum(expo, axis=1, keepdims=True)).astype(BF16)
        probs_ref[h] = probs
        local_ref[:, h * DH : (h + 1) * DH] = dot(probs, head(v_ref, h), NN)


def columns(z_ref, way, cols):
    return pl.ds(pl.multiple_of((z_ref[0] ^ way) * cols, DH), cols)


def load_carries(own_ref, far_refs, packed, forward):
    own, flag = load_states(own_ref)
    far = load_others(far_refs, forward)[0] if packed else load_states(far_refs[0])[0]
    return {True: own, False: far}, flag


def read_kernel(
    heads, project, packed, pos_ref, z_ref, facts_ref, gate_ref, q_ref, own_ref, local_ref, far_ref,
    *refs,
):
    if project:
        weight_ref = refs[0]
        mixed_ref, read_ref, memory_ref, norm_ref, sig_ref, scale_ref, first_ref = refs[-7:]
    else:
        mixed_ref, read_ref, memory_ref, norm_ref, sig_ref, scale_ref = refs
    live = live_rows(facts_ref, q_ref.shape[0])
    carries, flag = load_carries(own_ref, [far_ref], packed, True)
    for kept, i, h in by_half(heads, pos_ref):
        carry, norm = carries[kept][i]
        norm = flag * norm
        parts = jnp.concatenate(split(flag * carry), axis=1)
        memory_ref[h] = parts
        norm_ref[h] = jnp.broadcast_to(norm, (8, DH))
        sig = feature(q_ref[:, cut(h)].astype(F32)).astype(BF16)
        numer = dot(sig, parts, NN)
        numer = numer[:, 0:DH] + numer[:, DH:]
        denom = jnp.sum(sig.astype(F32) * norm, axis=1, keepdims=True) + 1.0
        read = numer / denom
        gate = gate_row(gate_ref, h)
        mixed = live * (gate * read + (1.0 - gate) * local_ref[:, cut(h)])
        sig_ref[:, cut(h)] = sig
        scale_ref[h] = live * gate[:, 0:1] / denom
        read_ref[:, cut(h)] = read
        mixed_ref[:, cut(h)] = mixed.astype(BF16)
    if project:
        block = weight_ref[:, columns(z_ref, 2, first_ref.shape[1])]
        first_ref[...] = dot(mixed_ref[...], block, NN).astype(BF16)


def pass_kernel(block_ref, after_ref, out_ref):
    out_ref[...] = block_ref[...]


def token_kernel(*refs):
    refs[-1][...] = jnp.zeros(refs[-1].shape, F32)


def more_kernel(ways, z_ref, *refs):
    grad_refs, (weight_ref, *before, after_ref, total_ref) = refs[: len(ways)], refs[len(ways) :]
    total = before[0][...] if before else None
    for way, grad_ref in zip(ways, grad_refs):
        block = weight_ref[:, columns(z_ref, way, grad_ref.shape[1])]
        part = dot(grad_ref[...], block, NT)
        total = part if total is None else total + part
    total_ref[...] = total


def add_kernel(z_ref, mixed_ref, weight_ref, more_ref, after_ref, out_ref):
    block = weight_ref[:, columns(z_ref, 3, out_ref.shape[1])]
    part = dot(mixed_ref[...], block, NN)
    out_ref[...] = (part + more_ref[...].astype(F32)).astype(BF16)


def rest_kernel(z_ref, mixed_ref, weight_ref, after_ref, near_ref, own_ref):
    cols = own_ref.shape[1]
    near = dot(mixed_ref[...], weight_ref[:, columns(z_ref, 1, cols)], NN)
    near_ref[...] = near.astype(BF16)
    own_ref[...] = dot(mixed_ref[...], weight_ref[:, columns(z_ref, 0, cols)], NN)


def spread_kernel(
    heads, ways, packed, pos_ref, z_ref, facts_ref, sig_ref, scale_ref, read_ref, *refs,
):
    if ways:
        parts, (total_ref, weight_ref) = refs[: len(ways)], refs[len(ways) : len(ways) + 2]
        keep_ref, give_ref, numer_ref, denom_ref, grad_ref = refs[-5:]
        total = total_ref[...]
        for way, part_ref in zip(ways, parts):
            block = weight_ref[:, columns(z_ref, way, part_ref.shape[1])]
            total = total + dot(part_ref[...], block, NT)
        grad_ref[...] = total.astype(BF16)
    else:
        grad_ref, keep_ref, give_ref, numer_ref, denom_ref = refs
    mine, given = [], []
    for kept, i, h in by_half(heads, pos_ref):
        sig = sig_ref[:, cut(h)]
        numer_grad = (grad_ref[:, cut(h)].astype(F32) * scale_ref[h]).astype(BF16)
        denom_grad = -jnp.sum(
            numer_grad.astype(F32) * read_ref[:, cut(h)], axis=1, keepdims=True
        )
        memory = dot(sig, numer_grad, TN)
        norm = jnp.sum(sig.astype(F32) * denom_grad, axis=0, keepdims=True)
        numer_ref[:, cut(h)] = numer_grad
        denom_ref[h] = denom_grad
        (mine if kept else given).append((memory, norm))
    flag = jnp.broadcast_to(opened(facts_ref), (1, DH))
    store_states(keep_ref, mine, flag)
    if packed:
        pack(give_ref, given, flag, False)
    else:
        store_states(give_ref, given, flag)


def grads_kernel(heads, facts_ref, gate_ref, q_ref, k_ref, v_ref, probs_ref, grad_ref, numer_ref,
                 denom_ref, memory_ref, norm_ref, *refs):
    query_ref, key_ref, value_ref = refs[-3:]
    length = q_ref.shape[0]
    live = live_rows(facts_ref, length)
    for h in range(heads):
        here = slice(h * DH, (h + 1) * DH)
        q, k, v = head(q_ref, h), head(k_ref, h), head(v_ref, h)
        gate = gate_row(gate_ref, h)
        grad = (head(grad_ref, h).astype(F32) * (1.0 - gate) * live).astype(BF16)
        probs = probs_ref[h]
        probs_grad = dot(grad, v, NT)
        full = probs.astype(F32)
        mean = jnp.sum(full * probs_grad, axis=1, keepdims=True)
        scores_grad = (full * (probs_grad - mean) * DH ** (-0.5)).astype(BF16)
        key_ref[:, here] = dot(scores_grad, q, TN)
        value_ref[:, here] = dot(probs, grad, TN)
        parts = memory_ref[h]
        numer = head(numer_ref, h)
        sig_grad = dot(numer, parts[:, 0:DH], NT) + dot(numer, parts[:, DH:], NT)
        sig_grad = sig_grad + denom_ref[h] * norm_ref[h, 0:1, :]
        total = dot(scores_grad, k, NN) + sig_grad * slope(q.astype(F32))
        query_ref[:, here] = total.astype(BF16)


def last_kernel(
    heads, packed, pos_ref, facts_ref, k_ref, v_ref, own_ref, key_ref, value_ref, *refs
):
    far_refs, (key_out, value_out) = refs[:-2], refs[-2:]
    live = live_rows(facts_ref, k_ref.shape[0])
    carries, _ = load_carries(own_ref, far_refs, packed, False)
    for kept, i, h in by_half(heads, pos_ref):
        memory, norm = carries[kept][i]
        top, low = split(memory)
        k, v = k_ref[:, cut(h)].astype(F32), v_ref[:, cut(h)]
        sig = (feature(k) * live).astype(BF16)
        sig_grad = (dot(v, top, NT) + dot(v, low, NT) + norm) * live
        key_out[:, cut(h)] = (key_ref[:, cut(h)] + sig_grad * slope(k)).astype(BF16)
        more = dot(sig, jnp.concatenate([top, low], axis=1), NN)
        value_out[:, cut(h)] = (value_ref[:, cut(h)] + more[:, 0:DH] + more[:, DH:]).astype(BF16)


def weighted(state, forward):
    count, mine = lax.axis_size("seq"), lax.axis_index("seq")
    states = lax.all_gather(state, "seq")
    total = jnp.zeros_like(state)
    weight = jnp.ones((), F32)

    def turn(step, carried):
        total, weight = carried
        at = mine - 1 - step if forward else mine + 1 + step
        inside = (at >= 0) & (at < count)
        one = lax.dynamic_index_in_dim(states, jnp.clip(at, 0, count - 1), keepdims=False)
        opened = one[0, DH + 1, 0]
        here = weight if forward else weight * opened
        total = jnp.where(inside, total + here * one, total)
        return total, weight * opened

    return lax.fori_loop(0, count - 1, turn, (total, weight))[0]


def scan_states(keep, give, pos, heads, forward, before_pair, before_join):
    count = lax.axis_size("seq")
    half = heads // 2
    if count != 8:
        before_pair()
        before_join(keep)
        carry = weighted(jnp.concatenate([keep, *give]), forward)
        return carry[:half], [carry[half:]]
    pairs = [(s, s ^ 1) for s in range(count)]
    others = [lax.ppermute(part, "seq", pairs) for part in give]
    sent_shape = jax.ShapeDtypeStruct((half * DH + TAIL, DH), BF16)
    after = before_pair()
    sent = call(
        functools.partial(pair_kernel, heads, forward, len(give)),
        [sent_shape],
        [SMEM, VMEM] + [VMEM] * len(give) + [ANY] * len(after),
        [pos, keep, *others, *after],
        0.01, "pair",
    )[0]
    arrived = [
        lax.ppermute(sent, "seq", [(s, s ^ way) for s in range(count)]) for way in (6, 2, 4)
    ]
    after = before_join(sent)
    parts = 1 if forward else 2
    part = jax.ShapeDtypeStruct((half // parts * DH + TAIL, DH), BF16)
    own, *passed = call(
        functools.partial(join_kernel, heads, forward, len(give), parts),
        [jax.ShapeDtypeStruct((half, ROWS, DH), F32)] + [part] * parts,
        [SMEM] + [VMEM] * 4 + [VMEM] * len(give) + [ANY] * len(after),
        [pos, arrived[1], arrived[2], arrived[0], keep, *others, *after],
        0.01, "join",
    )
    return own, [lax.ppermute(part, "seq", pairs) for part in passed]


def shards(queries, keys, values, gate, out_weight, out_grad, facts):
    length, width = queries.shape
    heads = width // DH
    cols = out_grad.shape[1]
    groups = lax.axis_size("head")
    direct = groups == 4
    pos = lax.axis_index("seq").astype(jnp.int32).reshape(1)
    paired = lax.axis_size("seq") == 8
    if not paired:
        pos = jnp.zeros_like(pos)
    z = lax.axis_index("head").astype(jnp.int32).reshape(1)
    facts = facts[0]
    flat = jax.ShapeDtypeStruct((length, width), F32)
    low = jax.ShapeDtypeStruct((length, width), BF16)
    part_low = jax.ShapeDtypeStruct((length, cols), BF16)
    part_full = jax.ShapeDtypeStruct((length, cols), F32)
    states = jax.ShapeDtypeStruct((heads // 2, ROWS, DH), F32)

    def packed(count):
        return jax.ShapeDtypeStruct((count * DH + TAIL, DH), BF16)

    column = jax.ShapeDtypeStruct((heads, length, 1), F32)

    def swap(array, way):
        return lax.ppermute(array, "head", [(s, s ^ way) for s in range(groups)])

    first = call(token_kernel, [jax.ShapeDtypeStruct((8, DH), F32)], [VMEM], [facts], 10, "warm")
    shares = 2 if paired else 1
    keep, *give = call(
        functools.partial(state_kernel, heads, paired),
        [states] + ([packed(heads // 2 // shares)] * shares if paired else [states]),
        [SMEM] * 2 + [VMEM] * 3 + [ANY],
        [pos, z, facts, keys, values, *first], 3, "state",
    )
    if direct:
        grad_3 = swap(out_grad, 3)
        grad_1 = swap(out_grad, 1)
    kept = {}

    def beside_forward(sent):
        kept["local"] = call(
            functools.partial(local_kernel, heads),
            [jax.ShapeDtypeStruct((heads, length, length), BF16), flat],
            [VMEM] * 4 + [ANY],
            [facts, queries, keys, values, sent], 0.01, "local",
        )
        if not direct:
            return [kept["local"][1]]
        kept["total"] = call(
            functools.partial(more_kernel, (0,)), [flat], [SMEM] + [VMEM] * 2 + [ANY],
            [z, out_grad, out_weight, kept["local"][1]], 0.01, "unproject_own",
        )[0]
        passed = call(
            pass_kernel, [part_low], [VMEM, ANY], [grad_3, kept["total"]], 0.01, "pass_on"
        )
        kept["grad_2"] = swap(passed[0], 1)
        return [*passed, grad_1]

    own, far = scan_states(keep, give, pos, heads, True, lambda: [], beside_forward)
    probs, local = kept["local"]
    orders = []
    outs = call(
        functools.partial(read_kernel, heads, direct, paired),
        [low, flat, jax.ShapeDtypeStruct((heads, DH, 2 * DH), BF16),
         jax.ShapeDtypeStruct((heads, 8, DH), F32), low, column] + [part_low] * direct,
        [SMEM, SMEM, VMEM, SMEM] + [VMEM] * (4 + direct) + [ANY] * len(orders),
        [pos, z, facts, gate, queries, own, local, *far] + [out_weight] * direct + orders,
        0.01, "read",
    )
    mixed, read, memory, norm, sig, scale = outs[:6]
    if direct:
        sum_2 = swap(outs[6], 1)
        total = call(
            functools.partial(more_kernel, (1, 3)), [flat], [SMEM] + [VMEM] * 4 + [ANY],
            [z, grad_1, grad_3, out_weight, kept["total"], mixed], 0.01, "unproject_more",
        )[0]
        grads_in = [kept["grad_2"], total, out_weight]
    else:
        part = dot(mixed, out_weight, NN)
        output = lax.psum_scatter(part, "head", scatter_dimension=1, tiled=True).astype(BF16)
        whole = lax.all_gather(out_grad, "head", axis=1, tiled=True)
        grads_in = [dot(whole, out_weight, NT).astype(BF16)]
    outs = call(
        functools.partial(spread_kernel, heads, (2,) * direct, paired),
        [states, packed(heads // 2) if paired else states, low,
         column] + [low] * direct,
        [SMEM, SMEM] + [VMEM] * (4 + len(grads_in)),
        [pos, z, facts, sig, scale, read, *grads_in],
        0.01, "spread",
    )
    keep, give, numer_grad, denom_grad = outs[:4]
    mixed_grad = outs[4] if direct else grads_in[0]

    def project_rest():
        if not direct:
            return []
        near, kept["mine"] = call(
            rest_kernel, [part_low, part_full], [SMEM, VMEM, VMEM, ANY],
            [z, mixed, out_weight, numer_grad], 0.01, "project_rest",
        )
        kept["from_1"] = swap(near, 1)
        return [near]

    def beside_back(sent):
        after = [sent]
        if direct:
            after = call(
                add_kernel, [part_low], [SMEM, VMEM, VMEM, VMEM, ANY],
                [z, mixed, out_weight, sum_2, sent], 0.01, "project_add",
            )
            kept["from_3"] = swap(after[0], 3)
        kept["grads"] = call(
            functools.partial(grads_kernel, heads),
            [low, flat, flat],
            [VMEM, SMEM] + [VMEM] * 9 + [ANY] * len(after),
            [facts, gate, queries, keys, values, probs, mixed_grad, numer_grad, denom_grad, memory,
             norm, *after],
            0.01, "grads",
        )
        return [kept["grads"][1]]

    own, far = scan_states(keep, [give], pos, heads, False, project_rest, beside_back)
    query_grad, key_part, value_part = kept["grads"]
    key_grad, value_grad = call(
        functools.partial(last_kernel, heads, paired),
        [low, low],
        [SMEM] + [VMEM] * (6 + len(far)),
        [pos, facts, keys, values, own, key_part, value_part, *far], 0.01, "last",
    )
    if direct:
        output = kept["mine"] + kept["from_1"].astype(F32) + kept["from_3"].astype(F32)
        output = output.astype(BF16)
    return (output, query_grad, key_grad, value_grad)


def solution(mesh):
    tokens = P("seq", "head")
    placed = (tokens, tokens, tokens, P("head"), P("head", None), tokens, P("seq", None, None))
    parts = jax.shard_map(
        shards, mesh=mesh, in_specs=placed, out_specs=(tokens,) * 4, check_vma=False
    )

    def whole(queries, keys, values, gate, out_weight, out_grad, valid, starts):
        row = lax.broadcasted_iota(jnp.int32, (valid.shape[0], 8, DH), 1)
        facts = jnp.where(row < 4, valid[:, None, None], starts[:, None, None]).astype(F32)
        facts = lax.with_sharding_constraint(facts, NamedSharding(mesh, placed[-1]))
        return parts(queries, keys, values, gate, out_weight, out_grad, facts)

    return whole
```

```python
import functools

import jax
import jax.numpy as jnp
from jax import lax
from jax.experimental import pallas as pl
from jax.experimental.pallas import tpu as pltpu
from jax.sharding import NamedSharding
from jax.sharding import PartitionSpec as P

DH = 128
ROWS = 136
TAIL = 16
BF16 = jnp.bfloat16
F32 = jnp.float32
VMEM = pl.BlockSpec(memory_space=pltpu.VMEM)
SMEM = pl.BlockSpec(memory_space=pltpu.SMEM)


ANY = pl.BlockSpec(memory_space=pl.ANY)


def call(kernel, outs, in_specs, args, micros, name):
    return pl.pallas_call(
        kernel,
        out_shape=outs,
        in_specs=in_specs,
        out_specs=[VMEM] * len(outs),
        compiler_params=pltpu.CompilerParams(vmem_limit_bytes=24 * 1024 * 1024),
        cost_estimate=pl.CostEstimate(flops=int(micros * 1.15e9), bytes_accessed=1024, transcendentals=0),
        name=name,
    )(*args)


def feature(x):
    return jnp.where(x > 0, x + 1.0, jnp.exp(jnp.minimum(x, 0.0)))


def slope(x):
    return jnp.where(x > 0, 1.0, jnp.where(x == 0, 0.5, jnp.exp(jnp.minimum(x, 0.0))))


def sigmoid(x):
    return 1.0 / (1.0 + jnp.exp(-x))


def dot(a, b, dims):
    return lax.dot_general(a, b, (dims, ((), ())), preferred_element_type=F32)


NN = ((1,), (0,))
NT = ((1,), (1,))
TN = ((0,), (0,))


def live_rows(facts_ref, length):
    where = lax.broadcasted_iota(jnp.int32, (length, 1), 0)
    return (where.astype(F32) < facts_ref[0:1, 0:1]).astype(F32)


def opened(facts_ref):
    return 1.0 - facts_ref[4:5, 0:1]


def gate_row(gate_ref, h):
    return sigmoid(jnp.full((1, DH), gate_ref[h], F32))


def head(ref, h):
    return ref[:, h * DH : (h + 1) * DH]


def tail(rows, *values):
    where = lax.broadcasted_iota(jnp.int32, (rows, DH), 0)
    out = jnp.zeros((rows, DH), F32)
    for at, value in enumerate(values):
        out = jnp.where(where == at, value, out)
    return out


def split(x):
    top = x.astype(BF16)
    rest = x - top.astype(F32)
    return top, rest.astype(BF16)


def cut(h):
    return pl.ds(h * DH if isinstance(h, int) else pl.multiple_of(h * DH, DH), DH)


def by_half(heads, pos_ref):
    half = lax.rem(pos_ref[0], 2)
    count = heads // 2
    for kept, first in ((True, half * count), (False, (1 - half) * count)):
        for i in range(count):
            yield kept, i, first + i


def pack(ref, states, flag, centred):
    count = len(states)
    norms = [split(norm) for _, norm in states]
    centres = [jnp.zeros_like(norm) for _, norm in states]
    memories = [memory for memory, _ in states]
    if centred:
        sums = [jnp.sum(memory, axis=0, keepdims=True) for memory in memories]
        weights = [jnp.sum(norm, axis=1, keepdims=True) for _, norm in states]
        centres = [a / jnp.maximum(b, 1e-30) for a, b in zip(sums, weights)]
        centres = [centre.astype(BF16).astype(F32) for centre in centres]
        outers = [outer(*norm, centre) for norm, centre in zip(norms, centres)]
        memories = [memory - less for memory, less in zip(memories, outers)]
    for i, memory in enumerate(memories):
        ref[i * DH : (i + 1) * DH, :] = memory.astype(BF16)
    tops, lows = zip(*norms)
    rows = tail(TAIL, *[x.astype(F32) for x in tops + lows], *centres, flag)
    ref[count * DH : count * DH + TAIL, :] = rows.astype(BF16)


def pack_parts(refs, states, flag, centred):
    share = len(states) // len(refs)
    for at, ref in enumerate(refs):
        pack(ref, states[at * share : (at + 1) * share], flag, centred)


def outer(top, low, centre):
    norms = tail(TAIL, top.astype(F32), low.astype(F32)).astype(BF16)
    return dot(norms, tail(TAIL, centre, centre).astype(BF16), TN)


def unpack(ref, centred):
    count = ref.shape[0] // DH
    rows = ref[count * DH : count * DH + TAIL, :].astype(F32)
    row = [rows[i : i + 1] for i in range(3 * count + 1)]
    states = []
    for i in range(count):
        memory = ref[i * DH : (i + 1) * DH, :].astype(F32)
        if centred:
            memory = memory + outer(row[i], row[count + i], row[2 * count + i])
        states.append((memory, row[i] + row[count + i]))
    return states, row[3 * count]


def load_states(ref):
    states = [(ref[i, 0:DH, :], ref[i, DH : DH + 1, :]) for i in range(ref.shape[0])]
    return states, ref[0, DH + 1 : DH + 2, :]


def store_states(ref, states, flag):
    for i, (memory, norm) in enumerate(states):
        ref[i, 0:DH, :] = memory
        ref[i, DH:ROWS, :] = tail(ROWS - DH, norm, flag)


def scaled(scale, state):
    return scale * state[0], scale * state[1]


def added(*states):
    return sum(memory for memory, _ in states), sum(norm for _, norm in states)


def chosen(which, yes, no):
    return jnp.where(which, yes[0], no[0]), jnp.where(which, yes[1], no[1])


def state_kernel(heads, packed, pos_ref, z_ref, facts_ref, k_ref, v_ref, after_ref, *refs):
    live = live_rows(facts_ref, k_ref.shape[0])
    kept, given = [], []
    for mine, i, h in by_half(heads, pos_ref):
        sig = (feature(k_ref[:, cut(h)].astype(F32)) * live).astype(BF16)
        memory = dot(sig, v_ref[:, cut(h)], TN)
        norm = jnp.sum(sig.astype(F32), axis=0, keepdims=True)
        (kept if mine else given).append((memory, norm))
    flag = jnp.broadcast_to(opened(facts_ref), (1, DH))
    store_states(refs[0], kept, flag)
    if packed:
        pack_parts(refs[1:], given, flag, True)
    else:
        store_states(refs[1], given, flag)


def load_others(refs, forward):
    states = []
    for ref in refs:
        part, flag = unpack(ref, forward)
        states += part
    return states, flag


def pair_kernel(heads, forward, count, pos_ref, keep_ref, *refs):
    sent_ref = refs[-1]
    lower = lax.rem(pos_ref[0], 2) == 0
    mine, flag = load_states(keep_ref)
    others, other_flag = load_others(refs[:count], forward)
    one = jnp.ones_like(flag)
    if forward:
        on_mine = jnp.where(lower, other_flag, one)
        on_other = jnp.where(lower, one, flag)
    else:
        on_mine = jnp.where(lower, flag, flag * other_flag)
        on_other = jnp.where(lower, flag * other_flag, other_flag)
    totals = [added(scaled(on_mine, a), scaled(on_other, b)) for a, b in zip(mine, others)]
    pack(sent_ref, totals, flag * other_flag, forward)


def join_kernel(heads, forward, count, parts, pos_ref, x_ref, y_ref, d_ref, keep_ref, *refs):
    own_ref, *sent_refs = refs[-1 - parts :]
    lower = lax.rem(pos_ref[0], 2) == 0
    chip = pos_ref[0] // 2
    place = chip if forward else 3 - chip
    odd, high = lax.rem(place, 2) == 1, place >= 2
    xs, x_open = unpack(x_ref, forward)
    ys, y_open = unpack(y_ref, forward)
    ds, d_open = unpack(d_ref, forward)
    on_x = jnp.where(odd, jnp.ones_like(x_open), 0.0)
    on_y = jnp.where(high, jnp.where(odd, x_open, d_open), 0.0)
    on_d = jnp.where(high, jnp.where(odd, x_open * y_open, 1.0), 0.0)
    mines, mine_open = load_states(keep_ref)
    others, other_open = load_others(refs[:count], forward)
    own, sent = [], []
    for x, y, d, mine, other in zip(xs, ys, ds, mines, others):
        carry = added(scaled(on_x, x), scaled(on_y, y), scaled(on_d, d))
        if forward:
            own.append(chosen(lower, carry, added(scaled(other_open, carry), other)))
            sent.append(chosen(lower, added(scaled(mine_open, carry), mine), carry))
        else:
            own.append(chosen(lower, scaled(other_open, added(carry, other)), carry))
            sent.append(chosen(lower, carry, scaled(mine_open, added(carry, mine))))
    store_states(own_ref, own, mine_open)
    pack_parts(sent_refs, sent, mine_open, forward)


def local_kernel(heads, facts_ref, q_ref, k_ref, v_ref, after_ref, probs_ref, local_ref):
    length = q_ref.shape[0]
    row = lax.broadcasted_iota(jnp.int32, (length, length), 0)
    col = lax.broadcasted_iota(jnp.int32, (length, length), 1)
    allowed = (col <= row) & (col.astype(F32) < facts_ref[0:1, 0:1])
    for h in range(heads):
        scores = dot(head(q_ref, h), head(k_ref, h), NT) * DH ** (-0.5)
        scores = jnp.where(allowed, scores, -1e30)
        expo = jnp.exp(scores - jnp.max(scores, axis=1, keepdims=True))
        probs = (expo / jnp.sum(expo, axis=1, keepdims=True)).astype(BF16)
        probs_ref[h] = probs
        local_ref[:, h * DH : (h + 1) * DH] = dot(probs, head(v_ref, h), NN)


def columns(z_ref, way, cols):
    return pl.ds(pl.multiple_of((z_ref[0] ^ way) * cols, DH), cols)


def load_carries(own_ref, far_refs, packed, forward):
    own, flag = load_states(own_ref)
    far = load_others(far_refs, forward)[0] if packed else load_states(far_refs[0])[0]
    return {True: own, False: far}, flag


def read_kernel(
    heads, project, packed, pos_ref, z_ref, facts_ref, gate_ref, q_ref, own_ref, local_ref, far_ref,
    *refs,
):
    if project:
        weight_ref = refs[0]
        mixed_ref, read_ref, memory_ref, norm_ref, sig_ref, scale_ref, first_ref = refs[-7:]
    else:
        mixed_ref, read_ref, memory_ref, norm_ref, sig_ref, scale_ref = refs
    live = live_rows(facts_ref, q_ref.shape[0])
    carries, flag = load_carries(own_ref, [far_ref], packed, True)
    order = list(by_half(heads, pos_ref))
    for at in range(0, heads, 4):
        some = order[at : at + 4]
        states = [scaled(flag, carries[kept][i]) for kept, i, _ in some]
        sigs = [feature(q_ref[:, cut(h)].astype(F32)).astype(BF16) for _, _, h in some]
        parts = [jnp.concatenate(split(memory), axis=1) for memory, _ in states]
        numers = [dot(sig, part, NN) for sig, part in zip(sigs, parts)]
        denoms = [
            jnp.sum(sig.astype(F32) * norm, axis=1, keepdims=True) + 1.0
            for sig, (_, norm) in zip(sigs, states)
        ]
        inverses = [1.0 / denom for denom in denoms]
        reads = [(n[:, 0:DH] + n[:, DH:]) * d for n, d in zip(numers, inverses)]
        for (_, _, h), state, sig, part, inverse, read in zip(
            some, states, sigs, parts, inverses, reads
        ):
            gate = gate_row(gate_ref, h)
            mixed = live * (gate * read + (1.0 - gate) * local_ref[:, cut(h)])
            mixed_ref[:, cut(h)] = mixed.astype(BF16)
            read_ref[:, cut(h)] = read
            memory_ref[h] = part
            norm_ref[h] = jnp.broadcast_to(state[1], (8, DH))
            sig_ref[:, cut(h)] = sig
            scale_ref[h] = live * gate[:, 0:1] * inverse
    if project:
        block = weight_ref[:, columns(z_ref, 2, first_ref.shape[1])]
        first_ref[...] = dot(mixed_ref[...], block, NN).astype(BF16)


def pass_kernel(block_ref, after_ref, out_ref):
    out_ref[...] = block_ref[...]


def token_kernel(*refs):
    refs[-1][...] = jnp.zeros(refs[-1].shape, F32)


def more_kernel(ways, z_ref, *refs):
    grad_refs, (weight_ref, *before, after_ref, total_ref) = refs[: len(ways)], refs[len(ways) :]
    total = before[0][...] if before else None
    for way, grad_ref in zip(ways, grad_refs):
        block = weight_ref[:, columns(z_ref, way, grad_ref.shape[1])]
        part = dot(grad_ref[...], block, NT)
        total = part if total is None else total + part
    total_ref[...] = total


def add_kernel(z_ref, mixed_ref, weight_ref, more_ref, after_ref, out_ref):
    block = weight_ref[:, columns(z_ref, 3, out_ref.shape[1])]
    part = dot(mixed_ref[...], block, NN)
    out_ref[...] = (part + more_ref[...].astype(F32)).astype(BF16)


def rest_kernel(z_ref, mixed_ref, weight_ref, after_ref, near_ref, own_ref):
    cols = own_ref.shape[1]
    near = dot(mixed_ref[...], weight_ref[:, columns(z_ref, 1, cols)], NN)
    near_ref[...] = near.astype(BF16)
    own_ref[...] = dot(mixed_ref[...], weight_ref[:, columns(z_ref, 0, cols)], NN)


def spread_kernel(
    heads, ways, packed, pos_ref, z_ref, facts_ref, sig_ref, scale_ref, read_ref, *refs,
):
    if ways:
        parts, (total_ref, weight_ref) = refs[: len(ways)], refs[len(ways) : len(ways) + 2]
        keep_ref, give_ref, numer_ref, denom_ref, grad_ref = refs[-5:]
        total = total_ref[...]
        for way, part_ref in zip(ways, parts):
            block = weight_ref[:, columns(z_ref, way, part_ref.shape[1])]
            total = total + dot(part_ref[...], block, NT)
        grad_ref[...] = total.astype(BF16)
    else:
        grad_ref, keep_ref, give_ref, numer_ref, denom_ref = refs
    mine, given = [], []
    for kept, i, h in by_half(heads, pos_ref):
        sig = sig_ref[:, cut(h)]
        numer_grad = (grad_ref[:, cut(h)].astype(F32) * scale_ref[h]).astype(BF16)
        denom_grad = -jnp.sum(
            numer_grad.astype(F32) * read_ref[:, cut(h)], axis=1, keepdims=True
        )
        memory = dot(sig, numer_grad, TN)
        norm = jnp.sum(sig.astype(F32) * denom_grad, axis=0, keepdims=True)
        numer_ref[:, cut(h)] = numer_grad
        denom_ref[h] = denom_grad
        (mine if kept else given).append((memory, norm))
    flag = jnp.broadcast_to(opened(facts_ref), (1, DH))
    store_states(keep_ref, mine, flag)
    if packed:
        pack(give_ref, given, flag, False)
    else:
        store_states(give_ref, given, flag)


def grads_kernel(heads, facts_ref, gate_ref, q_ref, k_ref, v_ref, probs_ref, grad_ref, numer_ref,
                 denom_ref, memory_ref, norm_ref, *refs):
    query_ref, key_ref, value_ref = refs[-3:]
    length = q_ref.shape[0]
    live = live_rows(facts_ref, length)
    for h in range(heads):
        here = slice(h * DH, (h + 1) * DH)
        q, k, v = head(q_ref, h), head(k_ref, h), head(v_ref, h)
        gate = gate_row(gate_ref, h)
        grad = (head(grad_ref, h).astype(F32) * (1.0 - gate) * live).astype(BF16)
        probs = probs_ref[h]
        probs_grad = dot(grad, v, NT)
        full = probs.astype(F32)
        mean = jnp.sum(full * probs_grad, axis=1, keepdims=True)
        scores_grad = (full * (probs_grad - mean) * DH ** (-0.5)).astype(BF16)
        key_ref[:, here] = dot(scores_grad, q, TN)
        value_ref[:, here] = dot(probs, grad, TN)
        parts = memory_ref[h]
        numer = head(numer_ref, h)
        sig_grad = dot(numer, parts[:, 0:DH], NT) + dot(numer, parts[:, DH:], NT)
        sig_grad = sig_grad + denom_ref[h] * norm_ref[h, 0:1, :]
        total = dot(scores_grad, k, NN) + sig_grad * slope(q.astype(F32))
        query_ref[:, here] = total.astype(BF16)


def last_kernel(
    heads, packed, far, pos_ref, facts_ref, k_ref, v_ref, own_ref, key_ref, value_ref, *refs
):
    far_refs, (key_out, value_out) = refs[:far], refs[-2:]
    live = live_rows(facts_ref, k_ref.shape[0])
    carries, _ = load_carries(own_ref, far_refs, packed, False)
    for kept, i, h in by_half(heads, pos_ref):
        memory, norm = carries[kept][i]
        top, low = split(memory)
        k, v = k_ref[:, cut(h)].astype(F32), v_ref[:, cut(h)]
        sig = (feature(k) * live).astype(BF16)
        sig_grad = (dot(v, top, NT) + dot(v, low, NT) + norm) * live
        key_out[:, cut(h)] = (key_ref[:, cut(h)] + sig_grad * slope(k)).astype(BF16)
        more = dot(sig, jnp.concatenate([top, low], axis=1), NN)
        value_out[:, cut(h)] = (value_ref[:, cut(h)] + more[:, 0:DH] + more[:, DH:]).astype(BF16)


def weighted(state, forward):
    count, mine = lax.axis_size("seq"), lax.axis_index("seq")
    states = lax.all_gather(state, "seq")
    total = jnp.zeros_like(state)
    weight = jnp.ones((), F32)

    def turn(step, carried):
        total, weight = carried
        at = mine - 1 - step if forward else mine + 1 + step
        inside = (at >= 0) & (at < count)
        one = lax.dynamic_index_in_dim(states, jnp.clip(at, 0, count - 1), keepdims=False)
        opened = one[0, DH + 1, 0]
        here = weight if forward else weight * opened
        total = jnp.where(inside, total + here * one, total)
        return total, weight * opened

    return lax.fori_loop(0, count - 1, turn, (total, weight))[0]


def scan_states(keep, give, pos, heads, forward, before_pair, before_join):
    count = lax.axis_size("seq")
    half = heads // 2
    if count != 8:
        before_pair()
        before_join(keep)
        carry = weighted(jnp.concatenate([keep, *give]), forward)
        return carry[:half], [carry[half:]]
    pairs = [(s, s ^ 1) for s in range(count)]
    others = [lax.ppermute(part, "seq", pairs) for part in give]
    sent_shape = jax.ShapeDtypeStruct((half * DH + TAIL, DH), BF16)
    after = before_pair()
    sent = call(
        functools.partial(pair_kernel, heads, forward, len(give)),
        [sent_shape],
        [SMEM, VMEM] + [VMEM] * len(give) + [ANY] * len(after),
        [pos, keep, *others, *after],
        0.01, "pair",
    )[0]
    arrived = [
        lax.ppermute(sent, "seq", [(s, s ^ way) for s in range(count)]) for way in (6, 2, 4)
    ]
    after = before_join(sent)
    parts = 1 if forward else 2
    part = jax.ShapeDtypeStruct((half // parts * DH + TAIL, DH), BF16)
    own, *passed = call(
        functools.partial(join_kernel, heads, forward, len(give), parts),
        [jax.ShapeDtypeStruct((half, ROWS, DH), F32)] + [part] * parts,
        [SMEM] + [VMEM] * 4 + [VMEM] * len(give) + [ANY] * len(after),
        [pos, arrived[1], arrived[2], arrived[0], keep, *others, *after],
        0.01, "join",
    )
    return own, [lax.ppermute(part, "seq", pairs) for part in passed]


def shards(queries, keys, values, gate, out_weight, out_grad, facts):
    length, width = queries.shape
    heads = width // DH
    cols = out_grad.shape[1]
    groups = lax.axis_size("head")
    direct = groups == 4
    pos = lax.axis_index("seq").astype(jnp.int32).reshape(1)
    paired = lax.axis_size("seq") == 8
    if not paired:
        pos = jnp.zeros_like(pos)
    z = lax.axis_index("head").astype(jnp.int32).reshape(1)
    facts = facts[0]
    flat = jax.ShapeDtypeStruct((length, width), F32)
    low = jax.ShapeDtypeStruct((length, width), BF16)
    part_low = jax.ShapeDtypeStruct((length, cols), BF16)
    part_full = jax.ShapeDtypeStruct((length, cols), F32)
    states = jax.ShapeDtypeStruct((heads // 2, ROWS, DH), F32)

    def packed(count):
        return jax.ShapeDtypeStruct((count * DH + TAIL, DH), BF16)

    column = jax.ShapeDtypeStruct((heads, length, 1), F32)

    def swap(array, way):
        return lax.ppermute(array, "head", [(s, s ^ way) for s in range(groups)])

    first = call(token_kernel, [jax.ShapeDtypeStruct((8, DH), F32)], [SMEM], [pos], 10, "warm")
    shares = 1 if paired else 1
    keep, *give = call(
        functools.partial(state_kernel, heads, paired),
        [states] + ([packed(heads // 2 // shares)] * shares if paired else [states]),
        [SMEM] * 2 + [VMEM] * 3 + [ANY],
        [pos, z, facts, keys, values, *first], 3, "state",
    )
    if direct:
        grad_3 = swap(out_grad, 3)
        grad_1 = swap(out_grad, 1)
    kept = {}

    def beside_forward(sent):
        kept["local"] = call(
            functools.partial(local_kernel, heads),
            [jax.ShapeDtypeStruct((heads, length, length), BF16), flat],
            [VMEM] * 4 + [ANY],
            [facts, queries, keys, values, sent], 0.01, "local",
        )
        if not direct:
            return [kept["local"][1]]
        passed = call(
            pass_kernel, [part_low], [VMEM, ANY], [grad_3, kept["local"][1]], 0.01, "pass_on"
        )
        kept["grad_2"] = swap(passed[0], 1)
        kept["total"] = call(
            functools.partial(more_kernel, (0,)), [flat], [SMEM] + [VMEM] * 2 + [ANY],
            [z, out_grad, out_weight, passed[0]], 0.8, "unproject_own",
        )[0]
        return [kept["total"]]

    own, far = scan_states(keep, give, pos, heads, True, lambda: [], beside_forward)
    probs, local = kept["local"]
    orders = []
    if direct:
        orders = call(
            token_kernel, [jax.ShapeDtypeStruct((8, DH), F32)], [ANY] * 2, [grad_1, own],
            0.5, "arrived",
        )
    outs = call(
        functools.partial(read_kernel, heads, direct, paired),
        [low, flat, jax.ShapeDtypeStruct((heads, DH, 2 * DH), BF16),
         jax.ShapeDtypeStruct((heads, 8, DH), F32), low, column] + [part_low] * direct,
        [SMEM, SMEM, VMEM, SMEM] + [VMEM] * (4 + direct) + [ANY] * len(orders),
        [pos, z, facts, gate, queries, own, local, *far] + [out_weight] * direct + [*orders],
        0.01, "read",
    )
    mixed, read, memory, norm, sig, scale = outs[:6]
    if direct:
        sum_2 = swap(outs[6], 1)
        total = call(
            functools.partial(more_kernel, (1, 3)), [flat], [SMEM] + [VMEM] * 4 + [ANY],
            [z, grad_1, grad_3, out_weight, kept["total"], mixed], 0.01, "unproject_more",
        )[0]
        grads_in = [kept["grad_2"], total, out_weight]
    else:
        part = dot(mixed, out_weight, NN)
        output = lax.psum_scatter(part, "head", scatter_dimension=1, tiled=True).astype(BF16)
        whole = lax.all_gather(out_grad, "head", axis=1, tiled=True)
        grads_in = [dot(whole, out_weight, NT).astype(BF16)]
    outs = call(
        functools.partial(spread_kernel, heads, (2,) * direct, paired),
        [states, packed(heads // 2) if paired else states, low,
         column] + [low] * direct,
        [SMEM, SMEM] + [VMEM] * (4 + len(grads_in)),
        [pos, z, facts, sig, scale, read, *grads_in],
        0.01, "spread",
    )
    keep, give, numer_grad, denom_grad = outs[:4]
    mixed_grad = outs[4] if direct else grads_in[0]

    def project_rest():
        if not direct:
            return []
        near, kept["mine"] = call(
            rest_kernel, [part_low, part_full], [SMEM, VMEM, VMEM, ANY],
            [z, mixed, out_weight, numer_grad], 0.01, "project_rest",
        )
        kept["from_1"] = swap(near, 1)
        return [near]

    def beside_back(sent):
        after = [sent]
        if direct:
            after = call(
                add_kernel, [part_low], [SMEM, VMEM, VMEM, VMEM, ANY],
                [z, mixed, out_weight, sum_2, sent], 0.01, "project_add",
            )
            kept["from_3"] = swap(after[0], 3)
        kept["grads"] = call(
            functools.partial(grads_kernel, heads),
            [low, flat, flat],
            [VMEM, SMEM] + [VMEM] * 9 + [ANY] * len(after),
            [facts, gate, queries, keys, values, probs, mixed_grad, numer_grad, denom_grad, memory,
             norm, *after],
            0.01, "grads",
        )
        return [kept["grads"][1]]

    own, far = scan_states(keep, [give], pos, heads, False, project_rest, beside_back)
    query_grad, key_part, value_part = kept["grads"]
    orders = [kept["from_1"]] if direct else []
    key_grad, value_grad = call(
        functools.partial(last_kernel, heads, paired, len(far)),
        [low, low],
        [SMEM] + [VMEM] * (6 + len(far)) + [ANY] * len(orders),
        [pos, facts, keys, values, own, key_part, value_part, *far, *orders], 1, "last",
    )
    if direct:
        kept["mine"], key_grad = lax.optimization_barrier((kept["mine"], key_grad))
        output = kept["mine"] + kept["from_1"].astype(F32) + kept["from_3"].astype(F32)
        output = output.astype(BF16)
    return (output, query_grad, key_grad, value_grad)


def solution(mesh):
    tokens = P("seq", "head")
    placed = (tokens, tokens, tokens, P("head"), P("head", None), tokens, P("seq", None, None))
    parts = jax.shard_map(
        shards, mesh=mesh, in_specs=placed, out_specs=(tokens,) * 4, check_vma=False
    )

    def whole(queries, keys, values, gate, out_weight, out_grad, valid, starts):
        row = lax.broadcasted_iota(jnp.int32, (valid.shape[0], 8, DH), 1)
        facts = jnp.where(row < 4, valid[:, None, None], starts[:, None, None]).astype(F32)
        facts = lax.with_sharding_constraint(facts, NamedSharding(mesh, placed[-1]))
        return parts(queries, keys, values, gate, out_weight, out_grad, facts)

    return whole
```

```python
import functools

import jax
import jax.numpy as jnp
from jax import lax
from jax.experimental import pallas as pl
from jax.experimental.pallas import tpu as pltpu
from jax.sharding import NamedSharding
from jax.sharding import PartitionSpec as P

DH = 128
ROWS = 136
TAIL = 16
BF16 = jnp.bfloat16
F32 = jnp.float32
VMEM = pl.BlockSpec(memory_space=pltpu.VMEM)
SMEM = pl.BlockSpec(memory_space=pltpu.SMEM)


ANY = pl.BlockSpec(memory_space=pl.ANY)


def call(kernel, outs, in_specs, args, micros, name):
    return pl.pallas_call(
        kernel,
        out_shape=outs,
        in_specs=in_specs,
        out_specs=[VMEM] * len(outs),
        compiler_params=pltpu.CompilerParams(vmem_limit_bytes=24 * 1024 * 1024),
        cost_estimate=pl.CostEstimate(flops=int(micros * 1.15e9), bytes_accessed=1024, transcendentals=0),
        name=name,
    )(*args)


def feature(x):
    return jnp.where(x > 0, x + 1.0, jnp.exp(jnp.minimum(x, 0.0)))


def slope(x):
    return jnp.where(x > 0, 1.0, jnp.where(x == 0, 0.5, jnp.exp(jnp.minimum(x, 0.0))))


def sigmoid(x):
    return 1.0 / (1.0 + jnp.exp(-x))


def dot(a, b, dims):
    return lax.dot_general(a, b, (dims, ((), ())), preferred_element_type=F32)


NN = ((1,), (0,))
NT = ((1,), (1,))
TN = ((0,), (0,))


def live_rows(facts_ref, length):
    where = lax.broadcasted_iota(jnp.int32, (length, 1), 0)
    return (where.astype(F32) < facts_ref[0:1, 0:1]).astype(F32)


def opened(facts_ref):
    return 1.0 - facts_ref[4:5, 0:1]


def gate_row(gate_ref, h):
    return sigmoid(jnp.full((1, DH), gate_ref[h], F32))


def head(ref, h):
    return ref[:, h * DH : (h + 1) * DH]


def tail(rows, *values):
    where = lax.broadcasted_iota(jnp.int32, (rows, DH), 0)
    out = jnp.zeros((rows, DH), F32)
    for at, value in enumerate(values):
        out = jnp.where(where == at, value, out)
    return out


def split(x):
    top = x.astype(BF16)
    rest = x - top.astype(F32)
    return top, rest.astype(BF16)


def cut(h):
    return pl.ds(h * DH if isinstance(h, int) else pl.multiple_of(h * DH, DH), DH)


def by_half(heads, pos_ref):
    half = lax.rem(pos_ref[0], 2)
    count = heads // 2
    for kept, first in ((True, half * count), (False, (1 - half) * count)):
        for i in range(count):
            yield kept, i, first + i


def pack(ref, states, flag, centred):
    count = len(states)
    norms = [split(norm) for _, norm in states]
    centres = [jnp.zeros_like(norm) for _, norm in states]
    memories = [memory for memory, _ in states]
    if centred:
        sums = [jnp.sum(memory, axis=0, keepdims=True) for memory in memories]
        weights = [jnp.sum(norm, axis=1, keepdims=True) for _, norm in states]
        centres = [a / jnp.maximum(b, 1e-30) for a, b in zip(sums, weights)]
        centres = [centre.astype(BF16).astype(F32) for centre in centres]
        outers = [outer(*norm, centre) for norm, centre in zip(norms, centres)]
        memories = [memory - less for memory, less in zip(memories, outers)]
    for i, memory in enumerate(memories):
        ref[i * DH : (i + 1) * DH, :] = memory.astype(BF16)
    tops, lows = zip(*norms)
    rows = tail(TAIL, *[x.astype(F32) for x in tops + lows], *centres, flag)
    ref[count * DH : count * DH + TAIL, :] = rows.astype(BF16)


def pack_parts(refs, states, flag, centred):
    share = len(states) // len(refs)
    for at, ref in enumerate(refs):
        pack(ref, states[at * share : (at + 1) * share], flag, centred)


def outer(top, low, centre):
    norms = tail(TAIL, top.astype(F32), low.astype(F32)).astype(BF16)
    return dot(norms, tail(TAIL, centre, centre).astype(BF16), TN)


def unpack(ref, centred):
    count = ref.shape[0] // DH
    rows = ref[count * DH : count * DH + TAIL, :].astype(F32)
    row = [rows[i : i + 1] for i in range(3 * count + 1)]
    states = []
    for i in range(count):
        memory = ref[i * DH : (i + 1) * DH, :].astype(F32)
        if centred:
            memory = memory + outer(row[i], row[count + i], row[2 * count + i])
        states.append((memory, row[i] + row[count + i]))
    return states, row[3 * count]


def load_states(ref):
    states = [(ref[i, 0:DH, :], ref[i, DH : DH + 1, :]) for i in range(ref.shape[0])]
    return states, ref[0, DH + 1 : DH + 2, :]


def store_states(ref, states, flag):
    for i, (memory, norm) in enumerate(states):
        ref[i, 0:DH, :] = memory
        ref[i, DH:ROWS, :] = tail(ROWS - DH, norm, flag)


def scaled(scale, state):
    return scale * state[0], scale * state[1]


def added(*states):
    return sum(memory for memory, _ in states), sum(norm for _, norm in states)


def chosen(which, yes, no):
    return jnp.where(which, yes[0], no[0]), jnp.where(which, yes[1], no[1])


def state_kernel(heads, packed, pos_ref, z_ref, facts_ref, k_ref, v_ref, after_ref, *refs):
    live = live_rows(facts_ref, k_ref.shape[0])
    kept, given = [], []
    for mine, i, h in by_half(heads, pos_ref):
        sig = (feature(k_ref[:, cut(h)].astype(F32)) * live).astype(BF16)
        memory = dot(sig, v_ref[:, cut(h)], TN)
        norm = jnp.sum(sig.astype(F32), axis=0, keepdims=True)
        (kept if mine else given).append((memory, norm))
    flag = jnp.broadcast_to(opened(facts_ref), (1, DH))
    store_states(refs[0], kept, flag)
    if packed:
        pack_parts(refs[1:], given, flag, True)
    else:
        store_states(refs[1], given, flag)


def load_others(refs, forward):
    states = []
    for ref in refs:
        part, flag = unpack(ref, forward)
        states += part
    return states, flag


def pair_kernel(heads, forward, count, pos_ref, keep_ref, *refs):
    sent_ref = refs[-1]
    lower = lax.rem(pos_ref[0], 2) == 0
    mine, flag = load_states(keep_ref)
    others, other_flag = load_others(refs[:count], forward)
    one = jnp.ones_like(flag)
    if forward:
        on_mine = jnp.where(lower, other_flag, one)
        on_other = jnp.where(lower, one, flag)
    else:
        on_mine = jnp.where(lower, flag, flag * other_flag)
        on_other = jnp.where(lower, flag * other_flag, other_flag)
    totals = [added(scaled(on_mine, a), scaled(on_other, b)) for a, b in zip(mine, others)]
    pack(sent_ref, totals, flag * other_flag, forward)


def join_kernel(heads, forward, count, parts, pos_ref, x_ref, y_ref, d_ref, keep_ref, *refs):
    own_ref, *sent_refs = refs[-1 - parts :]
    lower = lax.rem(pos_ref[0], 2) == 0
    chip = pos_ref[0] // 2
    place = chip if forward else 3 - chip
    odd, high = lax.rem(place, 2) == 1, place >= 2
    xs, x_open = unpack(x_ref, forward)
    ys, y_open = unpack(y_ref, forward)
    ds, d_open = unpack(d_ref, forward)
    on_x = jnp.where(odd, jnp.ones_like(x_open), 0.0)
    on_y = jnp.where(high, jnp.where(odd, x_open, d_open), 0.0)
    on_d = jnp.where(high, jnp.where(odd, x_open * y_open, 1.0), 0.0)
    mines, mine_open = load_states(keep_ref)
    others, other_open = load_others(refs[:count], forward)
    own, sent = [], []
    for x, y, d, mine, other in zip(xs, ys, ds, mines, others):
        carry = added(scaled(on_x, x), scaled(on_y, y), scaled(on_d, d))
        if forward:
            own.append(chosen(lower, carry, added(scaled(other_open, carry), other)))
            sent.append(chosen(lower, added(scaled(mine_open, carry), mine), carry))
        else:
            own.append(chosen(lower, scaled(other_open, added(carry, other)), carry))
            sent.append(chosen(lower, carry, scaled(mine_open, added(carry, mine))))
    store_states(own_ref, own, mine_open)
    pack_parts(sent_refs, sent, mine_open, forward)


def local_kernel(heads, facts_ref, q_ref, k_ref, v_ref, after_ref, probs_ref, local_ref):
    length = q_ref.shape[0]
    row = lax.broadcasted_iota(jnp.int32, (length, length), 0)
    col = lax.broadcasted_iota(jnp.int32, (length, length), 1)
    allowed = (col <= row) & (col.astype(F32) < facts_ref[0:1, 0:1])
    for h in range(heads):
        scores = dot(head(q_ref, h), head(k_ref, h), NT) * DH ** (-0.5)
        scores = jnp.where(allowed, scores, -1e30)
        expo = jnp.exp(scores - jnp.max(scores, axis=1, keepdims=True))
        probs = (expo / jnp.sum(expo, axis=1, keepdims=True)).astype(BF16)
        probs_ref[h] = probs
        local_ref[:, h * DH : (h + 1) * DH] = dot(probs, head(v_ref, h), NN)


def columns(z_ref, way, cols):
    return pl.ds(pl.multiple_of((z_ref[0] ^ way) * cols, DH), cols)


def load_carries(own_ref, far_refs, packed, forward):
    own, flag = load_states(own_ref)
    far = load_others(far_refs, forward)[0] if packed else load_states(far_refs[0])[0]
    return {True: own, False: far}, flag


def read_kernel(
    heads, project, packed, pos_ref, z_ref, facts_ref, gate_ref, q_ref, own_ref, local_ref, far_ref,
    *refs,
):
    if project:
        weight_ref = refs[0]
        mixed_ref, read_ref, memory_ref, norm_ref, sig_ref, scale_ref, first_ref = refs[-7:]
    else:
        mixed_ref, read_ref, memory_ref, norm_ref, sig_ref, scale_ref = refs
    live = live_rows(facts_ref, q_ref.shape[0])
    carries, flag = load_carries(own_ref, [far_ref], packed, True)
    order = list(by_half(heads, pos_ref))
    for at in range(0, heads, 4):
        some = order[at : at + 4]
        states = [scaled(flag, carries[kept][i]) for kept, i, _ in some]
        sigs = [feature(q_ref[:, cut(h)].astype(F32)).astype(BF16) for _, _, h in some]
        parts = [jnp.concatenate(split(memory), axis=1) for memory, _ in states]
        numers = [dot(sig, part, NN) for sig, part in zip(sigs, parts)]
        denoms = [
            jnp.sum(sig.astype(F32) * norm, axis=1, keepdims=True) + 1.0
            for sig, (_, norm) in zip(sigs, states)
        ]
        inverses = [1.0 / denom for denom in denoms]
        reads = [(n[:, 0:DH] + n[:, DH:]) * d for n, d in zip(numers, inverses)]
        for (_, _, h), state, sig, part, inverse, read in zip(
            some, states, sigs, parts, inverses, reads
        ):
            gate = gate_row(gate_ref, h)
            mixed = live * (gate * read + (1.0 - gate) * local_ref[:, cut(h)])
            mixed_ref[:, cut(h)] = mixed.astype(BF16)
            read_ref[:, cut(h)] = read
            memory_ref[h] = part
            norm_ref[h] = jnp.broadcast_to(state[1], (8, DH))
            sig_ref[:, cut(h)] = sig
            scale_ref[h] = live * gate[:, 0:1] * inverse
    if project:
        block = weight_ref[:, columns(z_ref, 2, first_ref.shape[1])]
        first_ref[...] = dot(mixed_ref[...], block, NN).astype(BF16)


def pass_kernel(block_ref, after_ref, out_ref):
    out_ref[...] = block_ref[...]


def token_kernel(*refs):
    refs[-1][...] = jnp.zeros(refs[-1].shape, F32)


def more_kernel(ways, z_ref, *refs):
    grad_refs, (weight_ref, *before, after_ref, total_ref) = refs[: len(ways)], refs[len(ways) :]
    total = before[0][...] if before else None
    for way, grad_ref in zip(ways, grad_refs):
        block = weight_ref[:, columns(z_ref, way, grad_ref.shape[1])]
        part = dot(grad_ref[...], block, NT)
        total = part if total is None else total + part
    total_ref[...] = total


def add_kernel(z_ref, mixed_ref, weight_ref, more_ref, after_ref, out_ref):
    block = weight_ref[:, columns(z_ref, 3, out_ref.shape[1])]
    part = dot(mixed_ref[...], block, NN)
    out_ref[...] = (part + more_ref[...].astype(F32)).astype(BF16)


def rest_kernel(z_ref, mixed_ref, weight_ref, after_ref, near_ref, own_ref):
    cols = own_ref.shape[1]
    near = dot(mixed_ref[...], weight_ref[:, columns(z_ref, 1, cols)], NN)
    near_ref[...] = near.astype(BF16)
    own_ref[...] = dot(mixed_ref[...], weight_ref[:, columns(z_ref, 0, cols)], NN)


def spread_kernel(
    heads, ways, packed, pos_ref, z_ref, facts_ref, sig_ref, scale_ref, read_ref, *refs,
):
    if ways:
        parts, (total_ref, weight_ref) = refs[: len(ways)], refs[len(ways) : len(ways) + 2]
        keep_ref, give_ref, numer_ref, denom_ref, grad_ref = refs[-5:]
        total = total_ref[...]
        for way, part_ref in zip(ways, parts):
            block = weight_ref[:, columns(z_ref, way, part_ref.shape[1])]
            total = total + dot(part_ref[...], block, NT)
        grad_ref[...] = total.astype(BF16)
    else:
        grad_ref, keep_ref, give_ref, numer_ref, denom_ref = refs
    mine, given = [], []
    for kept, i, h in by_half(heads, pos_ref):
        sig = sig_ref[:, cut(h)]
        numer_grad = (grad_ref[:, cut(h)].astype(F32) * scale_ref[h]).astype(BF16)
        denom_grad = -jnp.sum(
            numer_grad.astype(F32) * read_ref[:, cut(h)], axis=1, keepdims=True
        )
        memory = dot(sig, numer_grad, TN)
        norm = jnp.sum(sig.astype(F32) * denom_grad, axis=0, keepdims=True)
        numer_ref[:, cut(h)] = numer_grad
        denom_ref[h] = denom_grad
        (mine if kept else given).append((memory, norm))
    flag = jnp.broadcast_to(opened(facts_ref), (1, DH))
    store_states(keep_ref, mine, flag)
    if packed:
        pack(give_ref, given, flag, False)
    else:
        store_states(give_ref, given, flag)


def grads_kernel(heads, facts_ref, gate_ref, q_ref, k_ref, v_ref, probs_ref, grad_ref, numer_ref,
                 denom_ref, memory_ref, norm_ref, *refs):
    query_ref, key_ref, value_ref = refs[-3:]
    length = q_ref.shape[0]
    live = live_rows(facts_ref, length)
    for h in range(heads):
        here = slice(h * DH, (h + 1) * DH)
        q, k, v = head(q_ref, h), head(k_ref, h), head(v_ref, h)
        gate = gate_row(gate_ref, h)
        grad = (head(grad_ref, h).astype(F32) * (1.0 - gate) * live).astype(BF16)
        probs = probs_ref[h]
        probs_grad = dot(grad, v, NT)
        full = probs.astype(F32)
        mean = jnp.sum(full * probs_grad, axis=1, keepdims=True)
        scores_grad = (full * (probs_grad - mean) * DH ** (-0.5)).astype(BF16)
        key_ref[:, here] = dot(scores_grad, q, TN)
        value_ref[:, here] = dot(probs, grad, TN)
        parts = memory_ref[h]
        numer = head(numer_ref, h)
        sig_grad = dot(numer, parts[:, 0:DH], NT) + dot(numer, parts[:, DH:], NT)
        sig_grad = sig_grad + denom_ref[h] * norm_ref[h, 0:1, :]
        total = dot(scores_grad, k, NN) + sig_grad * slope(q.astype(F32))
        query_ref[:, here] = total.astype(BF16)


def last_kernel(
    heads, packed, far, pos_ref, facts_ref, k_ref, v_ref, own_ref, key_ref, value_ref, *refs
):
    far_refs, (key_out, value_out) = refs[:far], refs[-2:]
    live = live_rows(facts_ref, k_ref.shape[0])
    carries, _ = load_carries(own_ref, far_refs, packed, False)
    for kept, i, h in by_half(heads, pos_ref):
        memory, norm = carries[kept][i]
        top, low = split(memory)
        k, v = k_ref[:, cut(h)].astype(F32), v_ref[:, cut(h)]
        sig = (feature(k) * live).astype(BF16)
        sig_grad = (dot(v, top, NT) + dot(v, low, NT) + norm) * live
        key_out[:, cut(h)] = (key_ref[:, cut(h)] + sig_grad * slope(k)).astype(BF16)
        more = dot(sig, jnp.concatenate([top, low], axis=1), NN)
        value_out[:, cut(h)] = (value_ref[:, cut(h)] + more[:, 0:DH] + more[:, DH:]).astype(BF16)


def weighted(state, forward):
    count, mine = lax.axis_size("seq"), lax.axis_index("seq")
    states = lax.all_gather(state, "seq")
    total = jnp.zeros_like(state)
    weight = jnp.ones((), F32)

    def turn(step, carried):
        total, weight = carried
        at = mine - 1 - step if forward else mine + 1 + step
        inside = (at >= 0) & (at < count)
        one = lax.dynamic_index_in_dim(states, jnp.clip(at, 0, count - 1), keepdims=False)
        opened = one[0, DH + 1, 0]
        here = weight if forward else weight * opened
        total = jnp.where(inside, total + here * one, total)
        return total, weight * opened

    return lax.fori_loop(0, count - 1, turn, (total, weight))[0]


def scan_states(keep, give, pos, heads, forward, before_pair, before_join):
    count = lax.axis_size("seq")
    half = heads // 2
    if count != 8:
        before_pair()
        before_join(keep)
        carry = weighted(jnp.concatenate([keep, *give]), forward)
        carry = carry.at[:, DH + 1].set(keep[0, DH + 1])
        return carry[:half], [carry[half:]]
    pairs = [(s, s ^ 1) for s in range(count)]
    others = [lax.ppermute(part, "seq", pairs) for part in give]
    sent_shape = jax.ShapeDtypeStruct((half * DH + TAIL, DH), BF16)
    after = before_pair()
    sent = call(
        functools.partial(pair_kernel, heads, forward, len(give)),
        [sent_shape],
        [SMEM, VMEM] + [VMEM] * len(give) + [ANY] * len(after),
        [pos, keep, *others, *after],
        0.01, "pair",
    )[0]
    arrived = [
        lax.ppermute(sent, "seq", [(s, s ^ way) for s in range(count)]) for way in (6, 2, 4)
    ]
    after = before_join(sent)
    parts = 1 if forward else 2
    part = jax.ShapeDtypeStruct((half // parts * DH + TAIL, DH), BF16)
    own, *passed = call(
        functools.partial(join_kernel, heads, forward, len(give), parts),
        [jax.ShapeDtypeStruct((half, ROWS, DH), F32)] + [part] * parts,
        [SMEM] + [VMEM] * 4 + [VMEM] * len(give) + [ANY] * len(after),
        [pos, arrived[1], arrived[2], arrived[0], keep, *others, *after],
        0.01, "join",
    )
    return own, [lax.ppermute(part, "seq", pairs) for part in passed]


def shards(queries, keys, values, gate, out_weight, out_grad, facts):
    length, width = queries.shape
    heads = width // DH
    cols = out_grad.shape[1]
    groups = lax.axis_size("head")
    direct = groups == 4
    pos = lax.axis_index("seq").astype(jnp.int32).reshape(1)
    paired = lax.axis_size("seq") == 8
    if not paired:
        pos = jnp.zeros_like(pos)
    z = lax.axis_index("head").astype(jnp.int32).reshape(1)
    facts = facts[0]
    flat = jax.ShapeDtypeStruct((length, width), F32)
    low = jax.ShapeDtypeStruct((length, width), BF16)
    part_low = jax.ShapeDtypeStruct((length, cols), BF16)
    part_full = jax.ShapeDtypeStruct((length, cols), F32)
    states = jax.ShapeDtypeStruct((heads // 2, ROWS, DH), F32)

    def packed(count):
        return jax.ShapeDtypeStruct((count * DH + TAIL, DH), BF16)

    column = jax.ShapeDtypeStruct((heads, length, 1), F32)

    def swap(array, way):
        return lax.ppermute(array, "head", [(s, s ^ way) for s in range(groups)])

    first = call(token_kernel, [jax.ShapeDtypeStruct((8, DH), F32)], [SMEM], [pos], 10, "warm")
    shares = 1 if paired else 1
    keep, *give = call(
        functools.partial(state_kernel, heads, paired),
        [states] + ([packed(heads // 2 // shares)] * shares if paired else [states]),
        [SMEM] * 2 + [VMEM] * 3 + [ANY],
        [pos, z, facts, keys, values, *first], 3, "state",
    )
    if direct:
        grad_3 = swap(out_grad, 3)
        grad_1 = swap(out_grad, 1)
    kept = {}

    def beside_forward(sent):
        kept["local"] = call(
            functools.partial(local_kernel, heads),
            [jax.ShapeDtypeStruct((heads, length, length), BF16), flat],
            [VMEM] * 4 + [ANY],
            [facts, queries, keys, values, sent], 0.01, "local",
        )
        if not direct:
            return [kept["local"][1]]
        passed = call(
            pass_kernel, [part_low], [VMEM, ANY], [grad_3, kept["local"][1]], 0.01, "pass_on"
        )
        kept["grad_2"] = swap(passed[0], 1)
        kept["total"] = call(
            functools.partial(more_kernel, (0,)), [flat], [SMEM] + [VMEM] * 2 + [ANY],
            [z, out_grad, out_weight, passed[0]], 0.8, "unproject_own",
        )[0]
        return [kept["total"]]

    own, far = scan_states(keep, give, pos, heads, True, lambda: [], beside_forward)
    probs, local = kept["local"]
    orders = []
    if direct:
        orders = call(
            token_kernel, [jax.ShapeDtypeStruct((8, DH), F32)], [ANY] * 2, [grad_1, own],
            0.5, "arrived",
        )
    outs = call(
        functools.partial(read_kernel, heads, direct, paired),
        [low, flat, jax.ShapeDtypeStruct((heads, DH, 2 * DH), BF16),
         jax.ShapeDtypeStruct((heads, 8, DH), F32), low, column] + [part_low] * direct,
        [SMEM, SMEM, VMEM, SMEM] + [VMEM] * (4 + direct) + [ANY] * len(orders),
        [pos, z, facts, gate, queries, own, local, *far] + [out_weight] * direct + [*orders],
        0.01, "read",
    )
    mixed, read, memory, norm, sig, scale = outs[:6]
    if direct:
        sum_2 = swap(outs[6], 1)
        total = call(
            functools.partial(more_kernel, (1, 3)), [flat], [SMEM] + [VMEM] * 4 + [ANY],
            [z, grad_1, grad_3, out_weight, kept["total"], mixed], 0.01, "unproject_more",
        )[0]
        grads_in = [kept["grad_2"], total, out_weight]
    else:
        part = dot(mixed, out_weight, NN)
        output = lax.psum_scatter(part, "head", scatter_dimension=1, tiled=True).astype(BF16)
        whole = lax.all_gather(out_grad, "head", axis=1, tiled=True)
        grads_in = [dot(whole, out_weight, NT).astype(BF16)]
    outs = call(
        functools.partial(spread_kernel, heads, (2,) * direct, paired),
        [states, packed(heads // 2) if paired else states, low,
         column] + [low] * direct,
        [SMEM, SMEM] + [VMEM] * (4 + len(grads_in)),
        [pos, z, facts, sig, scale, read, *grads_in],
        0.01, "spread",
    )
    keep, give, numer_grad, denom_grad = outs[:4]
    mixed_grad = outs[4] if direct else grads_in[0]

    def project_rest():
        if not direct:
            return []
        near, kept["mine"] = call(
            rest_kernel, [part_low, part_full], [SMEM, VMEM, VMEM, ANY],
            [z, mixed, out_weight, numer_grad], 0.01, "project_rest",
        )
        kept["from_1"] = swap(near, 1)
        return [near]

    def beside_back(sent):
        after = [sent]
        if direct:
            after = call(
                add_kernel, [part_low], [SMEM, VMEM, VMEM, VMEM, ANY],
                [z, mixed, out_weight, sum_2, sent], 0.01, "project_add",
            )
            kept["from_3"] = swap(after[0], 3)
        kept["grads"] = call(
            functools.partial(grads_kernel, heads),
            [low, flat, flat],
            [VMEM, SMEM] + [VMEM] * 9 + [ANY] * len(after),
            [facts, gate, queries, keys, values, probs, mixed_grad, numer_grad, denom_grad, memory,
             norm, *after],
            0.01, "grads",
        )
        return [kept["grads"][1]]

    own, far = scan_states(keep, [give], pos, heads, False, project_rest, beside_back)
    query_grad, key_part, value_part = kept["grads"]
    orders = [kept["from_1"]] if direct else []
    key_grad, value_grad = call(
        functools.partial(last_kernel, heads, paired, len(far)),
        [low, low],
        [SMEM] + [VMEM] * (6 + len(far)) + [ANY] * len(orders),
        [pos, facts, keys, values, own, key_part, value_part, *far, *orders], 1, "last",
    )
    if direct:
        kept["mine"], key_grad = lax.optimization_barrier((kept["mine"], key_grad))
        output = kept["mine"] + kept["from_1"].astype(F32) + kept["from_3"].astype(F32)
        output = output.astype(BF16)
    return (output, query_grad, key_grad, value_grad)


def solution(mesh):
    tokens = P("seq", "head")
    placed = (tokens, tokens, tokens, P("head"), P("head", None), tokens, P("seq", None, None))
    parts = jax.shard_map(
        shards, mesh=mesh, in_specs=placed, out_specs=(tokens,) * 4, check_vma=False
    )

    def whole(queries, keys, values, gate, out_weight, out_grad, valid, starts):
        row = lax.broadcasted_iota(jnp.int32, (valid.shape[0], 8, DH), 1)
        facts = jnp.where(row < 4, valid[:, None, None], starts[:, None, None]).astype(F32)
        facts = lax.with_sharding_constraint(facts, NamedSharding(mesh, placed[-1]))
        return parts(queries, keys, values, gate, out_weight, out_grad, facts)

    return whole
```

```python
import functools

import jax
import jax.numpy as jnp
from jax import lax
from jax.experimental import pallas as pl
from jax.experimental.pallas import tpu as pltpu
from jax.sharding import NamedSharding
from jax.sharding import PartitionSpec as P

DH = 128
ROWS = 136
TAIL = 16
BF16 = jnp.bfloat16
F32 = jnp.float32
VMEM = pl.BlockSpec(memory_space=pltpu.VMEM)
SMEM = pl.BlockSpec(memory_space=pltpu.SMEM)


ANY = pl.BlockSpec(memory_space=pl.ANY)


def call(kernel, outs, in_specs, args, micros, name):
    return pl.pallas_call(
        kernel,
        out_shape=outs,
        in_specs=in_specs,
        out_specs=[VMEM] * len(outs),
        compiler_params=pltpu.CompilerParams(vmem_limit_bytes=24 * 1024 * 1024),
        cost_estimate=pl.CostEstimate(flops=int(micros * 1.15e9), bytes_accessed=1024, transcendentals=0),
        name=name,
    )(*args)


def feature(x):
    return jnp.where(x > 0, x + 1.0, jnp.exp(jnp.minimum(x, 0.0)))


def slope(x):
    return jnp.where(x > 0, 1.0, jnp.where(x == 0, 0.5, jnp.exp(jnp.minimum(x, 0.0))))


def sigmoid(x):
    return 1.0 / (1.0 + jnp.exp(-x))


def dot(a, b, dims):
    return lax.dot_general(a, b, (dims, ((), ())), preferred_element_type=F32)


NN = ((1,), (0,))
NT = ((1,), (1,))
TN = ((0,), (0,))


def live_rows(facts_ref, length):
    where = lax.broadcasted_iota(jnp.int32, (length, 1), 0)
    return (where.astype(F32) < facts_ref[0:1, 0:1]).astype(F32)


def opened(facts_ref):
    return 1.0 - facts_ref[4:5, 0:1]


def gate_row(gate_ref, h):
    return sigmoid(jnp.full((1, DH), gate_ref[h], F32))


def head(ref, h):
    return ref[:, h * DH : (h + 1) * DH]


def tail(rows, *values):
    where = lax.broadcasted_iota(jnp.int32, (rows, DH), 0)
    out = jnp.zeros((rows, DH), F32)
    for at, value in enumerate(values):
        out = jnp.where(where == at, value, out)
    return out


def split(x):
    top = x.astype(BF16)
    rest = x - top.astype(F32)
    return top, rest.astype(BF16)


def cut(h):
    return pl.ds(h * DH if isinstance(h, int) else pl.multiple_of(h * DH, DH), DH)


def by_half(heads, pos_ref):
    half = lax.rem(pos_ref[0], 2)
    count = heads // 2
    for kept, first in ((True, half * count), (False, (1 - half) * count)):
        for i in range(count):
            yield kept, i, first + i


def pack(ref, states, flag, centred):
    count = len(states)
    norms = [split(norm) for _, norm in states]
    centres = [jnp.zeros_like(norm) for _, norm in states]
    memories = [memory for memory, _ in states]
    if centred:
        sums = [jnp.sum(memory, axis=0, keepdims=True) for memory in memories]
        weights = [jnp.sum(norm, axis=1, keepdims=True) for _, norm in states]
        centres = [a / jnp.maximum(b, 1e-30) for a, b in zip(sums, weights)]
        centres = [centre.astype(BF16).astype(F32) for centre in centres]
        outers = [outer(*norm, centre) for norm, centre in zip(norms, centres)]
        memories = [memory - less for memory, less in zip(memories, outers)]
    for i, memory in enumerate(memories):
        ref[i * DH : (i + 1) * DH, :] = memory.astype(BF16)
    tops, lows = zip(*norms)
    rows = tail(TAIL, *[x.astype(F32) for x in tops + lows], *centres, flag)
    ref[count * DH : count * DH + TAIL, :] = rows.astype(BF16)


def pack_parts(refs, states, flag, centred):
    share = len(states) // len(refs)
    for at, ref in enumerate(refs):
        pack(ref, states[at * share : (at + 1) * share], flag, centred)


def outer(top, low, centre):
    norms = tail(TAIL, top.astype(F32), low.astype(F32)).astype(BF16)
    return dot(norms, tail(TAIL, centre, centre).astype(BF16), TN)


def unpack(ref, centred):
    count = ref.shape[0] // DH
    rows = ref[count * DH : count * DH + TAIL, :].astype(F32)
    row = [rows[i : i + 1] for i in range(3 * count + 1)]
    states = []
    for i in range(count):
        memory = ref[i * DH : (i + 1) * DH, :].astype(F32)
        if centred:
            memory = memory + outer(row[i], row[count + i], row[2 * count + i])
        states.append((memory, row[i] + row[count + i]))
    return states, row[3 * count]


def load_states(ref):
    states = [(ref[i, 0:DH, :], ref[i, DH : DH + 1, :]) for i in range(ref.shape[0])]
    return states, ref[0, DH + 1 : DH + 2, :]


def store_states(ref, states, flag):
    for i, (memory, norm) in enumerate(states):
        ref[i, 0:DH, :] = memory
        ref[i, DH:ROWS, :] = tail(ROWS - DH, norm, flag)


def scaled(scale, state):
    return scale * state[0], scale * state[1]


def added(*states):
    return sum(memory for memory, _ in states), sum(norm for _, norm in states)


def chosen(which, yes, no):
    return jnp.where(which, yes[0], no[0]), jnp.where(which, yes[1], no[1])


def state_kernel(heads, packed, pos_ref, z_ref, facts_ref, k_ref, v_ref, after_ref, *refs):
    live = live_rows(facts_ref, k_ref.shape[0])
    kept, given = [], []
    for mine, i, h in by_half(heads, pos_ref):
        sig = (feature(k_ref[:, cut(h)].astype(F32)) * live).astype(BF16)
        memory = dot(sig, v_ref[:, cut(h)], TN)
        norm = jnp.sum(sig.astype(F32), axis=0, keepdims=True)
        (kept if mine else given).append((memory, norm))
    flag = jnp.broadcast_to(opened(facts_ref), (1, DH))
    store_states(refs[0], kept, flag)
    if packed:
        pack_parts(refs[1:], given, flag, True)
    else:
        store_states(refs[1], given, flag)


def load_others(refs, forward):
    states = []
    for ref in refs:
        part, flag = unpack(ref, forward)
        states += part
    return states, flag


def pair_kernel(heads, forward, count, pos_ref, keep_ref, *refs):
    sent_ref = refs[-1]
    lower = lax.rem(pos_ref[0], 2) == 0
    mine, flag = load_states(keep_ref)
    others, other_flag = load_others(refs[:count], forward)
    one = jnp.ones_like(flag)
    if forward:
        on_mine = jnp.where(lower, other_flag, one)
        on_other = jnp.where(lower, one, flag)
    else:
        on_mine = jnp.where(lower, flag, flag * other_flag)
        on_other = jnp.where(lower, flag * other_flag, other_flag)
    totals = [added(scaled(on_mine, a), scaled(on_other, b)) for a, b in zip(mine, others)]
    pack(sent_ref, totals, flag * other_flag, forward)


def join_kernel(heads, forward, count, parts, pos_ref, x_ref, y_ref, d_ref, keep_ref, *refs):
    own_ref, *sent_refs = refs[-1 - parts :]
    lower = lax.rem(pos_ref[0], 2) == 0
    chip = pos_ref[0] // 2
    place = chip if forward else 3 - chip
    odd, high = lax.rem(place, 2) == 1, place >= 2
    xs, x_open = unpack(x_ref, forward)
    ys, y_open = unpack(y_ref, forward)
    ds, d_open = unpack(d_ref, forward)
    on_x = jnp.where(odd, jnp.ones_like(x_open), 0.0)
    on_y = jnp.where(high, jnp.where(odd, x_open, d_open), 0.0)
    on_d = jnp.where(high, jnp.where(odd, x_open * y_open, 1.0), 0.0)
    mines, mine_open = load_states(keep_ref)
    others, other_open = load_others(refs[:count], forward)
    own, sent = [], []
    for x, y, d, mine, other in zip(xs, ys, ds, mines, others):
        carry = added(scaled(on_x, x), scaled(on_y, y), scaled(on_d, d))
        if forward:
            own.append(chosen(lower, carry, added(scaled(other_open, carry), other)))
            sent.append(chosen(lower, added(scaled(mine_open, carry), mine), carry))
        else:
            own.append(chosen(lower, scaled(other_open, added(carry, other)), carry))
            sent.append(chosen(lower, carry, scaled(mine_open, added(carry, mine))))
    store_states(own_ref, own, mine_open)
    pack_parts(sent_refs, sent, mine_open, forward)


def local_kernel(heads, facts_ref, q_ref, k_ref, v_ref, after_ref, probs_ref, local_ref):
    length = q_ref.shape[0]
    row = lax.broadcasted_iota(jnp.int32, (length, length), 0)
    col = lax.broadcasted_iota(jnp.int32, (length, length), 1)
    allowed = (col <= row) & (col.astype(F32) < facts_ref[0:1, 0:1])
    for h in range(heads):
        scores = dot(head(q_ref, h), head(k_ref, h), NT) * DH ** (-0.5)
        scores = jnp.where(allowed, scores, -1e30)
        expo = jnp.exp(scores - jnp.max(scores, axis=1, keepdims=True))
        probs = (expo / jnp.sum(expo, axis=1, keepdims=True)).astype(BF16)
        probs_ref[h] = probs
        local_ref[:, h * DH : (h + 1) * DH] = dot(probs, head(v_ref, h), NN)


def columns(z_ref, way, cols):
    return pl.ds(pl.multiple_of((z_ref[0] ^ way) * cols, DH), cols)


def load_carries(own_ref, far_refs, packed, forward):
    own, flag = load_states(own_ref)
    far = load_others(far_refs, forward)[0] if packed else load_states(far_refs[0])[0]
    return {True: own, False: far}, flag


def read_kernel(
    heads, project, packed, pos_ref, z_ref, facts_ref, gate_ref, q_ref, own_ref, local_ref, far_ref,
    *refs,
):
    if project:
        weight_ref = refs[0]
        mixed_ref, read_ref, memory_ref, norm_ref, sig_ref, scale_ref, first_ref = refs[-7:]
    else:
        mixed_ref, read_ref, memory_ref, norm_ref, sig_ref, scale_ref = refs
    live = live_rows(facts_ref, q_ref.shape[0])
    carries, flag = load_carries(own_ref, [far_ref], packed, True)
    order = list(by_half(heads, pos_ref))
    for at in range(0, heads, 4):
        some = order[at : at + 4]
        states = [scaled(flag, carries[kept][i]) for kept, i, _ in some]
        sigs = [feature(q_ref[:, cut(h)].astype(F32)).astype(BF16) for _, _, h in some]
        parts = [jnp.concatenate(split(memory), axis=1) for memory, _ in states]
        numers = [dot(sig, part, NN) for sig, part in zip(sigs, parts)]
        denoms = [
            jnp.sum(sig.astype(F32) * norm, axis=1, keepdims=True) + 1.0
            for sig, (_, norm) in zip(sigs, states)
        ]
        inverses = [1.0 / denom for denom in denoms]
        reads = [(n[:, 0:DH] + n[:, DH:]) * d for n, d in zip(numers, inverses)]
        for (_, _, h), state, sig, part, inverse, read in zip(
            some, states, sigs, parts, inverses, reads
        ):
            gate = gate_row(gate_ref, h)
            mixed = live * (gate * read + (1.0 - gate) * local_ref[:, cut(h)])
            mixed_ref[:, cut(h)] = mixed.astype(BF16)
            read_ref[:, cut(h)] = read
            memory_ref[h] = part
            norm_ref[h] = jnp.broadcast_to(state[1], (8, DH))
            sig_ref[:, cut(h)] = sig
            scale_ref[h] = live * gate[:, 0:1] * inverse
    if project:
        block = weight_ref[:, columns(z_ref, 2, first_ref.shape[1])]
        first_ref[...] = dot(mixed_ref[...], block, NN).astype(BF16)


def pass_kernel(block_ref, after_ref, out_ref):
    out_ref[...] = block_ref[...]


def token_kernel(*refs):
    refs[-1][...] = jnp.zeros(refs[-1].shape, F32)


def more_kernel(ways, z_ref, *refs):
    grad_refs, (weight_ref, *before, after_ref, total_ref) = refs[: len(ways)], refs[len(ways) :]
    total = before[0][...] if before else None
    for way, grad_ref in zip(ways, grad_refs):
        block = weight_ref[:, columns(z_ref, way, grad_ref.shape[1])]
        part = dot(grad_ref[...], block, NT)
        total = part if total is None else total + part
    total_ref[...] = total


def add_kernel(z_ref, mixed_ref, weight_ref, more_ref, after_ref, out_ref):
    block = weight_ref[:, columns(z_ref, 3, out_ref.shape[1])]
    part = dot(mixed_ref[...], block, NN)
    out_ref[...] = (part + more_ref[...].astype(F32)).astype(BF16)


def rest_kernel(z_ref, mixed_ref, weight_ref, after_ref, near_ref, own_ref):
    cols = own_ref.shape[1]
    near = dot(mixed_ref[...], weight_ref[:, columns(z_ref, 1, cols)], NN)
    near_ref[...] = near.astype(BF16)
    own_ref[...] = dot(mixed_ref[...], weight_ref[:, columns(z_ref, 0, cols)], NN)


def spread_kernel(
    heads, ways, packed, pos_ref, z_ref, facts_ref, sig_ref, scale_ref, read_ref, *refs,
):
    if ways:
        parts, (total_ref, weight_ref) = refs[: len(ways)], refs[len(ways) : len(ways) + 2]
        keep_ref, give_ref, numer_ref, denom_ref, grad_ref = refs[-5:]
        total = total_ref[...]
        for way, part_ref in zip(ways, parts):
            block = weight_ref[:, columns(z_ref, way, part_ref.shape[1])]
            total = total + dot(part_ref[...], block, NT)
        grad_ref[...] = total.astype(BF16)
    else:
        grad_ref, keep_ref, give_ref, numer_ref, denom_ref = refs
    mine, given = [], []
    for kept, i, h in by_half(heads, pos_ref):
        sig = sig_ref[:, cut(h)]
        numer_grad = (grad_ref[:, cut(h)].astype(F32) * scale_ref[h]).astype(BF16)
        denom_grad = -jnp.sum(
            numer_grad.astype(F32) * read_ref[:, cut(h)], axis=1, keepdims=True
        )
        memory = dot(sig, numer_grad, TN)
        norm = jnp.sum(sig.astype(F32) * denom_grad, axis=0, keepdims=True)
        numer_ref[:, cut(h)] = numer_grad
        denom_ref[h] = denom_grad
        (mine if kept else given).append((memory, norm))
    flag = jnp.broadcast_to(opened(facts_ref), (1, DH))
    store_states(keep_ref, mine, flag)
    if packed:
        pack(give_ref, given, flag, False)
    else:
        store_states(give_ref, given, flag)


def grads_kernel(heads, facts_ref, gate_ref, q_ref, k_ref, v_ref, probs_ref, grad_ref, numer_ref,
                 denom_ref, memory_ref, norm_ref, *refs):
    query_ref, key_ref, value_ref = refs[-3:]
    length = q_ref.shape[0]
    live = live_rows(facts_ref, length)
    for h in range(heads):
        here = slice(h * DH, (h + 1) * DH)
        q, k, v = head(q_ref, h), head(k_ref, h), head(v_ref, h)
        gate = gate_row(gate_ref, h)
        grad = (head(grad_ref, h).astype(F32) * (1.0 - gate) * live).astype(BF16)
        probs = probs_ref[h]
        probs_grad = dot(grad, v, NT)
        full = probs.astype(F32)
        mean = jnp.sum(full * probs_grad, axis=1, keepdims=True)
        scores_grad = (full * (probs_grad - mean) * DH ** (-0.5)).astype(BF16)
        key_ref[:, here] = dot(scores_grad, q, TN)
        value_ref[:, here] = dot(probs, grad, TN)
        parts = memory_ref[h]
        numer = head(numer_ref, h)
        sig_grad = dot(numer, parts[:, 0:DH], NT) + dot(numer, parts[:, DH:], NT)
        sig_grad = sig_grad + denom_ref[h] * norm_ref[h, 0:1, :]
        total = dot(scores_grad, k, NN) + sig_grad * slope(q.astype(F32))
        query_ref[:, here] = total.astype(BF16)


def last_kernel(
    heads, packed, far, pos_ref, facts_ref, k_ref, v_ref, own_ref, key_ref, value_ref, *refs
):
    far_refs, sum_refs = refs[:far], refs[far:-2]
    key_out, value_out = refs[-2:]
    if sum_refs:
        own_sum, near_sum, key_out = sum_refs
        value_out, partial_ref = refs[-2:]
        partial_ref[...] = own_sum[...] + near_sum[...].astype(F32)
    live = live_rows(facts_ref, k_ref.shape[0])
    carries, _ = load_carries(own_ref, far_refs, packed, False)
    for kept, i, h in by_half(heads, pos_ref):
        memory, norm = carries[kept][i]
        top, low = split(memory)
        k, v = k_ref[:, cut(h)].astype(F32), v_ref[:, cut(h)]
        sig = (feature(k) * live).astype(BF16)
        sig_grad = (dot(v, top, NT) + dot(v, low, NT) + norm) * live
        key_out[:, cut(h)] = (key_ref[:, cut(h)] + sig_grad * slope(k)).astype(BF16)
        more = dot(sig, jnp.concatenate([top, low], axis=1), NN)
        value_out[:, cut(h)] = (value_ref[:, cut(h)] + more[:, 0:DH] + more[:, DH:]).astype(BF16)


def weighted(state, forward):
    count, mine = lax.axis_size("seq"), lax.axis_index("seq")
    states = lax.all_gather(state, "seq")
    total = jnp.zeros_like(state)
    weight = jnp.ones((), F32)

    def turn(step, carried):
        total, weight = carried
        at = mine - 1 - step if forward else mine + 1 + step
        inside = (at >= 0) & (at < count)
        one = lax.dynamic_index_in_dim(states, jnp.clip(at, 0, count - 1), keepdims=False)
        opened = one[0, DH + 1, 0]
        here = weight if forward else weight * opened
        total = jnp.where(inside, total + here * one, total)
        return total, weight * opened

    return lax.fori_loop(0, count - 1, turn, (total, weight))[0]


def scan_states(keep, give, pos, heads, forward, before_pair, before_join):
    count = lax.axis_size("seq")
    half = heads // 2
    if count != 8:
        before_pair()
        before_join(keep)
        carry = weighted(jnp.concatenate([keep, *give]), forward)
        carry = carry.at[:, DH + 1].set(keep[0, DH + 1])
        return carry[:half], [carry[half:]]
    pairs = [(s, s ^ 1) for s in range(count)]
    others = [lax.ppermute(part, "seq", pairs) for part in give]
    sent_shape = jax.ShapeDtypeStruct((half * DH + TAIL, DH), BF16)
    after = before_pair()
    sent = call(
        functools.partial(pair_kernel, heads, forward, len(give)),
        [sent_shape],
        [SMEM, VMEM] + [VMEM] * len(give) + [ANY] * len(after),
        [pos, keep, *others, *after],
        0.01, "pair",
    )[0]
    arrived = [
        lax.ppermute(sent, "seq", [(s, s ^ way) for s in range(count)]) for way in (6, 2, 4)
    ]
    after = before_join(sent)
    parts = 1 if forward else 2
    part = jax.ShapeDtypeStruct((half // parts * DH + TAIL, DH), BF16)
    own, *passed = call(
        functools.partial(join_kernel, heads, forward, len(give), parts),
        [jax.ShapeDtypeStruct((half, ROWS, DH), F32)] + [part] * parts,
        [SMEM] + [VMEM] * 4 + [VMEM] * len(give) + [ANY] * len(after),
        [pos, arrived[1], arrived[2], arrived[0], keep, *others, *after],
        0.01, "join",
    )
    return own, [lax.ppermute(part, "seq", pairs) for part in passed]


def shards(queries, keys, values, gate, out_weight, out_grad, facts):
    length, width = queries.shape
    heads = width // DH
    cols = out_grad.shape[1]
    groups = lax.axis_size("head")
    direct = groups == 4
    pos = lax.axis_index("seq").astype(jnp.int32).reshape(1)
    paired = lax.axis_size("seq") == 8
    if not paired:
        pos = jnp.zeros_like(pos)
    z = lax.axis_index("head").astype(jnp.int32).reshape(1)
    facts = facts[0]
    flat = jax.ShapeDtypeStruct((length, width), F32)
    low = jax.ShapeDtypeStruct((length, width), BF16)
    part_low = jax.ShapeDtypeStruct((length, cols), BF16)
    part_full = jax.ShapeDtypeStruct((length, cols), F32)
    states = jax.ShapeDtypeStruct((heads // 2, ROWS, DH), F32)

    def packed(count):
        return jax.ShapeDtypeStruct((count * DH + TAIL, DH), BF16)

    column = jax.ShapeDtypeStruct((heads, length, 1), F32)

    def swap(array, way):
        return lax.ppermute(array, "head", [(s, s ^ way) for s in range(groups)])

    first = call(token_kernel, [jax.ShapeDtypeStruct((8, DH), F32)], [SMEM], [pos], 10, "warm")
    shares = 1 if paired else 1
    keep, *give = call(
        functools.partial(state_kernel, heads, paired),
        [states] + ([packed(heads // 2 // shares)] * shares if paired else [states]),
        [SMEM] * 2 + [VMEM] * 3 + [ANY],
        [pos, z, facts, keys, values, *first], 3, "state",
    )
    if direct:
        grad_3 = swap(out_grad, 3)
        grad_1 = swap(out_grad, 1)
    kept = {}

    def beside_forward(sent):
        kept["local"] = call(
            functools.partial(local_kernel, heads),
            [jax.ShapeDtypeStruct((heads, length, length), BF16), flat],
            [VMEM] * 4 + [ANY],
            [facts, queries, keys, values, sent], 0.01, "local",
        )
        if not direct:
            return [kept["local"][1]]
        passed = call(
            pass_kernel, [part_low], [VMEM, ANY], [grad_3, kept["local"][1]], 0.01, "pass_on"
        )
        kept["grad_2"] = swap(passed[0], 1)
        kept["total"] = call(
            functools.partial(more_kernel, (0,)), [flat], [SMEM] + [VMEM] * 2 + [ANY],
            [z, out_grad, out_weight, passed[0]], 0.8, "unproject_own",
        )[0]
        return [kept["total"]]

    own, far = scan_states(keep, give, pos, heads, True, lambda: [], beside_forward)
    probs, local = kept["local"]
    orders = []
    if direct:
        orders = call(
            token_kernel, [jax.ShapeDtypeStruct((8, DH), F32)], [ANY] * 2, [grad_1, own],
            0.5, "arrived",
        )
        kept["total"] = call(
            functools.partial(more_kernel, (3,)), [flat], [SMEM] + [VMEM] * 3 + [ANY],
            [z, grad_3, out_weight, kept["total"], own], 0.01, "unproject_end",
        )[0]
        orders = [*orders, kept["total"]]
    outs = call(
        functools.partial(read_kernel, heads, direct, paired),
        [low, flat, jax.ShapeDtypeStruct((heads, DH, 2 * DH), BF16),
         jax.ShapeDtypeStruct((heads, 8, DH), F32), low, column] + [part_low] * direct,
        [SMEM, SMEM, VMEM, SMEM] + [VMEM] * (4 + direct) + [ANY] * len(orders),
        [pos, z, facts, gate, queries, own, local, *far] + [out_weight] * direct + [*orders],
        0.01, "read",
    )
    mixed, read, memory, norm, sig, scale = outs[:6]
    if direct:
        sum_2 = swap(outs[6], 1)
        total = call(
            functools.partial(more_kernel, (1,)), [flat], [SMEM] + [VMEM] * 3 + [ANY],
            [z, grad_1, out_weight, kept["total"], mixed], 0.01, "unproject_near",
        )[0]
        grads_in = [kept["grad_2"], total, out_weight]
    else:
        part = dot(mixed, out_weight, NN)
        output = lax.psum_scatter(part, "head", scatter_dimension=1, tiled=True).astype(BF16)
        whole = lax.all_gather(out_grad, "head", axis=1, tiled=True)
        grads_in = [dot(whole, out_weight, NT).astype(BF16)]
    outs = call(
        functools.partial(spread_kernel, heads, (2,) * direct, paired),
        [states, packed(heads // 2) if paired else states, low,
         column] + [low] * direct,
        [SMEM, SMEM] + [VMEM] * (4 + len(grads_in)),
        [pos, z, facts, sig, scale, read, *grads_in],
        0.01, "spread",
    )
    keep, give, numer_grad, denom_grad = outs[:4]
    mixed_grad = outs[4] if direct else grads_in[0]

    def project_rest():
        if not direct:
            return []
        near, kept["mine"] = call(
            rest_kernel, [part_low, part_full], [SMEM, VMEM, VMEM, ANY],
            [z, mixed, out_weight, numer_grad], 0.01, "project_rest",
        )
        kept["from_1"] = swap(near, 1)
        return [near]

    def beside_back(sent):
        after = [sent]
        if direct:
            after = call(
                add_kernel, [part_low], [SMEM, VMEM, VMEM, VMEM, ANY],
                [z, mixed, out_weight, sum_2, sent], 0.01, "project_add",
            )
            kept["from_3"] = swap(after[0], 3)
        kept["grads"] = call(
            functools.partial(grads_kernel, heads),
            [low, flat, flat],
            [VMEM, SMEM] + [VMEM] * 9 + [ANY] * len(after),
            [facts, gate, queries, keys, values, probs, mixed_grad, numer_grad, denom_grad, memory,
             norm, *after],
            0.01, "grads",
        )
        return [kept["grads"][1]]

    own, far = scan_states(keep, [give], pos, heads, False, project_rest, beside_back)
    query_grad, key_part, value_part = kept["grads"]
    sums = [kept["mine"], kept["from_1"]] if direct else []
    key_grad, value_grad, *partial = call(
        functools.partial(last_kernel, heads, paired, len(far)),
        [low, low] + [part_full] * direct,
        [SMEM] + [VMEM] * (6 + len(far) + len(sums)),
        [pos, facts, keys, values, own, key_part, value_part, *far, *sums], 1, "last",
    )
    if direct:
        output = (partial[0] + kept["from_3"].astype(F32)).astype(BF16)
    return (output, query_grad, key_grad, value_grad)


def solution(mesh):
    tokens = P("seq", "head")
    placed = (tokens, tokens, tokens, P("head"), P("head", None), tokens, P("seq", None, None))
    parts = jax.shard_map(
        shards, mesh=mesh, in_specs=placed, out_specs=(tokens,) * 4, check_vma=False
    )

    def whole(queries, keys, values, gate, out_weight, out_grad, valid, starts):
        row = lax.broadcasted_iota(jnp.int32, (valid.shape[0], 8, DH), 1)
        facts = jnp.where(row < 4, valid[:, None, None], starts[:, None, None]).astype(F32)
        facts = lax.with_sharding_constraint(facts, NamedSharding(mesh, placed[-1]))
        return parts(queries, keys, values, gate, out_weight, out_grad, facts)

    return whole
```
